32 devices in a mesh: rows: 8 (over z, x), cols: 4 (over y, core).
Axes of the slice: x: 2, y: 2, z: 4, core: 2. Of those that a mesh axis runs over, the one named last changes fastest.
Arguments:
- panel_u: bfloat16 [8, 16, 1024, 256], P('rows', 'cols'), may hold values from -2.5 to 2.5
- panel_v: bfloat16 [8, 16, 1024, 256], P('rows', 'cols'), may hold values from -0.1875 to 0.1875
- panel_rank: int32 [8, 16], P('rows', 'cols'), may hold values from 128 to 256
- pivot_u: bfloat16 [2, 16, 1024, 256], P(None, 'cols', 'rows'), may hold values from -2.5 to 2.5
- pivot_v: bfloat16 [2, 16, 1024, 256], P(None, 'cols', 'rows'), may hold values from -0.1875 to 0.1875
- pivot_rank: int32 [2, 16], P(None, 'cols'), may hold values from 128 to 256
- orig_u: bfloat16 [2, 8, 1024, 256], P(None, 'rows'), may hold values from -6 to 6
- orig_v: bfloat16 [2, 8, 1024, 256], P(None, 'rows'), may hold values from -0.375 to 0.375
- sampler: bfloat16 [1024, 256], replicated, may hold values from -6 to 6
Outputs:
- basis: float32 [2, 8, 1024, 256], P(None, 'rows', 'cols')
- coeff: float32 [2, 8, 1024, 256], P(None, 'rows', 'cols')
The draws below stay inside these ranges and needn't reach their ends.
Inputs may be any that keep to these rules, and one draw needn't show every extreme that they name: `panel_rank`: rank of each panel tile; factor columns at and beyond it carry no weight. `pivot_rank`: rank of each pivot row tile; factor columns at and beyond it carry no weight.
All inputs are finite; a program needn't handle non-finite values.
Results may differ from the reference program's by a relative error of at most 0.012.
Values may be sent and summed in bfloat16 or wider, within the bound.
No kernel may reach another device: no remote copies, remote signals or barrier semaphores. Data moves between devices by JAX's collectives and lax.ppermute only.
A program may use at most 64 MiB of HBM per device.

```python
import jax
import jax.numpy as jnp
from jax import lax

TILE = 1024
RANK_MAX = 256
SAMPLES = 256
ROWS_T = 8
PRIOR = 16


def touch_ends(drawn, stream_key, least, high):
    longest = drawn.shape.index(max(drawn.shape))
    spots = []
    for shift in (0, 1):
        where = [jax.random.randint(jax.random.fold_in(stream_key, axis), (), 0, length) for axis, length in enumerate(drawn.shape)]
        where[longest] = (where[longest] + shift) % drawn.shape[longest]
        spots.append(tuple(where))
    return drawn.at[spots[0]].set(least).at[spots[1]].set(high)


def shard_levels(stream_key, shape, split, low, largest):
    loudness = 1.0
    for axis_at, parts in split:
        draws = jax.random.uniform(jax.random.fold_in(jax.random.fold_in(stream_key, 6), axis_at), (parts,), jnp.float32, low / len(split), largest / len(split))
        loudness = loudness * jnp.repeat(jnp.exp(draws), shape[axis_at] // parts).reshape((-1,) + (1,) * (len(shape) - 1 - axis_at))
    return loudness


def bell_draw(own_key, dims, width, reach, split=(), held_as=jnp.bfloat16):
    factor_of = shard_levels(own_key, dims, split, -0.22, 0.18) if split else 1.0
    result = jax.random.normal(own_key, dims, jnp.float32) * width * factor_of
    return jnp.minimum(jnp.maximum(result, -reach), reach).astype(held_as)


def setup_inputs(seed: int = 0) -> dict:
    seeds = jax.random.split(jax.random.key(seed), 10)
    panel_u = bell_draw(seeds[0], (ROWS_T, PRIOR, TILE, RANK_MAX), 0.18, 2.5, ((0, 8), (1, 4)))
    panel_v = bell_draw(seeds[1], (ROWS_T, PRIOR, TILE, RANK_MAX), TILE ** -0.5, 0.1875, ((0, 8), (1, 4)))
    panel_rank = touch_ends(jax.random.randint(seeds[2], (ROWS_T, PRIOR), RANK_MAX // 2, RANK_MAX + 1), jax.random.fold_in(seeds[2], 1), RANK_MAX // 2, RANK_MAX).astype(jnp.int32)
    pivot_u = bell_draw(seeds[3], (2, PRIOR, TILE, RANK_MAX), 0.18, 2.5, ((1, 4), (2, 8)))
    pivot_v = bell_draw(seeds[4], (2, PRIOR, TILE, RANK_MAX), TILE ** -0.5, 0.1875, ((1, 4), (2, 8)))
    pivot_rank = touch_ends(jax.random.randint(seeds[5], (2, PRIOR), RANK_MAX // 2, RANK_MAX + 1), jax.random.fold_in(seeds[5], 1), RANK_MAX // 2, RANK_MAX).astype(jnp.int32)
    orig_u = bell_draw(seeds[6], (2, ROWS_T, TILE, RANK_MAX), 1.0, 6.0, ((1, 8),))
    orig_v = bell_draw(seeds[7], (2, ROWS_T, TILE, RANK_MAX), RANK_MAX ** -0.5, 0.375, ((1, 8),))
    sampler = bell_draw(seeds[8], (TILE, SAMPLES), 1.0, 6.0)
    return dict(panel_u=panel_u, panel_v=panel_v, panel_rank=panel_rank, pivot_u=pivot_u, pivot_v=pivot_v, pivot_rank=pivot_rank, orig_u=orig_u, orig_v=orig_v, sampler=sampler)


def rounded(value):
    return lax.optimization_barrier(value.astype(jnp.bfloat16))

def masked(factor, ranks):
    keep = (jnp.arange(factor.shape[-1]) < ranks[..., None]).astype(factor.dtype)
    return factor * keep[..., None, :]

def reference(panel_u, panel_v, panel_rank, pivot_u, pivot_v, pivot_rank, orig_u, orig_v, sampler):
    wide = jnp.float32
    pivot_um = masked(pivot_u, pivot_rank).astype(wide)
    sample_wide = sampler.astype(wide)
    sampled = rounded(jnp.einsum('cjnr,ns->cjrs', pivot_um, sample_wide)).astype(wide)
    pivot_wide = pivot_v.astype(wide)

    def one_row(tile_item):
        row_u, row_v, row_rank, first_u, first_v = tile_item
        panel_um = masked(row_u, row_rank).astype(wide)
        cross = rounded(jnp.einsum('jnr,cjnq->cjrq', row_v.astype(wide), pivot_wide)).astype(wide)
        sample_term = rounded(jnp.einsum('cjrq,cjqs->cjrs', cross, sampled)).astype(wide)
        first_u = first_u.astype(wide)
        first_v = first_v.astype(wide)
        start_proj = rounded(jnp.einsum('cnr,ns->crs', first_v, sample_wide)).astype(wide)
        ysum = jnp.einsum('cnr,crs->cns', first_u, start_proj) - jnp.einsum('jnr,cjrs->cns', panel_um, sample_term)
        gram = jnp.einsum('cns,cnt->cst', ysum, ysum, precision=lax.Precision.HIGHEST)
        factor_low = jnp.linalg.cholesky(gram)
        qmat = lax.linalg.triangular_solve(factor_low, ysum, left_side=False, lower=True, transpose_a=True)
        basis = qmat * jnp.sqrt(jnp.asarray(TILE, wide))
        qround = rounded(qmat).astype(wide)
        proj_in = rounded(jnp.einsum('jnr,cns->cjrs', panel_um, qround)).astype(wide)
        proj_mid = rounded(jnp.einsum('cjrq,cjrs->cjqs', cross, proj_in)).astype(wide)
        left_proj = rounded(jnp.einsum('cnr,cns->crs', first_u, qround)).astype(wide)
        coeff = jnp.einsum('cnr,crs->cns', first_v, left_proj) - jnp.einsum('cjnq,cjqs->cns', pivot_um, proj_mid)
        return (basis, coeff)
    basis, coeff = lax.map(one_row, (panel_u, panel_v, panel_rank, jnp.swapaxes(orig_u, 0, 1), jnp.swapaxes(orig_v, 0, 1)))
    return (jnp.swapaxes(basis, 0, 1), jnp.swapaxes(coeff, 0, 1))
```

```python
import math

import jax
import jax.numpy as jnp
import numpy as np
from jax import lax
from jax.experimental import pallas as pl
from jax.experimental.pallas import tpu as pltpu
from jax.sharding import PartitionSpec as P

F32 = jnp.float32
BF16 = jnp.bfloat16
BLOCK = 32
RING_MOST = 16


def rank_mask(ranks, width):
    return (jnp.arange(width, dtype=jnp.int32) < ranks[..., None]).astype(BF16)


def split3(x):
    high = x.astype(BF16)
    rest = x - high.astype(F32)
    mid = rest.astype(BF16)
    low = (rest - mid.astype(F32)).astype(BF16)
    return high, mid, low


def dot00(a, b):
    return lax.dot_general(a, b, (((0,), (0,)), ((), ())), preferred_element_type=F32)


def dot11(a, b):
    return lax.dot_general(a, b, (((1,), (1,)), ((), ())), preferred_element_type=F32)


def eliminate(panel, first):
    rows, width = panel.shape
    lane = lax.broadcasted_iota(jnp.int32, (1, width), 1)
    sub = lax.broadcasted_iota(jnp.int32, (rows, 1), 0)
    scale = jnp.zeros((rows, 1), F32)
    for k in range(rows):
        here = lane == first + k
        column = panel[:, first + k : first + k + 1]
        pivot = column[k : k + 1, :]
        inverse = 1.0 / pivot
        row = jnp.where(here, 1.0, panel[k : k + 1, :])
        factor = jnp.where(sub > k, column * inverse, 0.0)
        cleared = jnp.where(here & (sub >= k), jnp.where(sub == k, 1.0, 0.0), panel)
        panel = cleared - factor * row
        scale = jnp.where(sub == k, lax.rsqrt(pivot), scale)
    above = (lane > first + sub) & (lane < first + rows)
    return jnp.where(above, 0.0, panel * scale)


def orthonormal(y_ref, q_ref, work):
    width = y_ref.shape[1]
    y = y_ref[...]
    work[...] = lax.dot_general(
        y, y, (((0,), (0,)), ((), ())), precision=lax.Precision.HIGHEST, preferred_element_type=F32
    )
    lane = lax.broadcasted_iota(jnp.int32, (1, width), 1)
    for first in range(0, width, BLOCK):
        last = first + BLOCK
        panel = eliminate(work[first:last, :], first)
        work[first:last, :] = panel
        if last < width:
            high, mid, low = split3(panel)
            left = jnp.concatenate([high, high, mid, mid, high, low], 0)
            right = jnp.concatenate([high, mid, high, mid, low, high], 0)
            update = dot00(left, right)
            inside = (lane >= first) & (lane < last)
            work[last:, :] = jnp.where(inside, 0.0, work[last:, :]) - update[last:, :]
    row = lax.broadcasted_iota(jnp.int32, (width, width), 0)
    col = lax.broadcasted_iota(jnp.int32, (width, width), 1)
    inverse = jnp.where(col <= row, work[...], 0.0)
    m_high, m_low, _ = split3(inverse)
    y_high, y_low, _ = split3(y)
    q_ref[...] = dot11(y_high, m_high) + (dot11(y_high, m_low) + dot11(y_low, m_high))


def cholesky_qr(y):
    rows, width = y.shape
    return pl.pallas_call(
        orthonormal,
        out_shape=jax.ShapeDtypeStruct((rows, width), F32),
        in_specs=[pl.BlockSpec(memory_space=pltpu.VMEM)],
        out_specs=pl.BlockSpec(memory_space=pltpu.VMEM),
        scratch_shapes=[pltpu.VMEM((width, width), F32)],
        compiler_params=pltpu.CompilerParams(vmem_limit_bytes=32 << 20),
        cost_estimate=pl.CostEstimate(flops=20 * rows * width * width, bytes_accessed=8 * rows * width, transcendentals=width),
        name="cholesky_qr",
    )(y)


def ring_order(count):
    if count % 2:
        return list(range(count))
    return list(range(0, count, 2)) + list(range(count - 1, 0, -2))


def ring_gather(block, order, axis):
    count = len(order)
    if count > RING_MOST:
        return [lax.all_gather(block, axis, axis=2, tiled=True)]
    ahead = [(order[(p + 1) % count], order[p]) for p in range(count)]
    behind = [(order[p], order[(p + 1) % count]) for p in range(count)]
    found = {0: block}
    up = down = block
    for step in range(1, (count - 1) // 2 + 1):
        up = lax.ppermute(up, axis, ahead)
        down = lax.ppermute(down, axis, behind)
        found[step] = up
        found[count - step] = down
    if count % 2 == 0:
        half = block.shape[0] // 2
        found[count // 2] = jnp.concatenate(
            [lax.ppermute(up[:half], axis, ahead), lax.ppermute(down[half:], axis, behind)], 0
        )
    return [found[d] for d in range(count)]


def body(panel_u, panel_v, panel_rank, pivot_u, pivot_v, pivot_rank, orig_u, orig_v, sampler):
    order, width = panel_u.shape[2:]
    count = lax.axis_size("rows")
    cols = lax.axis_size("cols")
    pairs = cols // 2
    slab = order // count
    me = lax.axis_index("cols")
    core = me % 2
    pair = me // 2
    swap = [(i, i ^ 1) for i in range(cols)]

    ring = ring_order(count)
    place = np.argsort(np.array(ring))
    table = np.array([[ring[(place[r] + d) % count] for d in range(count)] for r in range(count)], np.int32)
    back = np.argsort(table, axis=1).astype(np.int32)
    row = lax.axis_index("rows")
    sources = jnp.asarray(table)[row]
    natural = jnp.asarray(back)[row]

    panel_mask = rank_mask(panel_rank[0], width)
    pivot_mask = rank_mask(pivot_rank, width)

    blocks_u = ring_gather(pivot_u, ring, "rows")
    blocks_v = ring_gather(pivot_v, ring, "rows")
    whole_u = jnp.concatenate(blocks_u, 2)
    whole_v = jnp.concatenate(blocks_v, 2)

    sampler_ring, panel_v_ring = sampler, panel_v[0]
    if count <= RING_MOST:
        sampler_ring = sampler.reshape(count, slab, -1)[sources].reshape(order, -1)
        panel_v_ring = panel_v[0].reshape(-1, count, slab, width)[:, sources].reshape(-1, order, width)

    sampled = jnp.einsum("cjnr,ns->cjrs", whole_u, sampler_ring, preferred_element_type=F32)
    sampled = (sampled * pivot_mask[..., None]).astype(BF16)
    cross = jnp.einsum("jnr,cjnq->cjrq", panel_v_ring, whole_v, preferred_element_type=F32).astype(BF16)
    sample_term = jnp.einsum("cjrq,cjqs->cjrs", cross, sampled, preferred_element_type=F32).astype(BF16)
    sample_term = sample_term * panel_mask[None, :, :, None]
    update = jnp.einsum("jnr,cjrs->cns", panel_u[0], sample_term, preferred_element_type=F32)

    mine_v = lax.dynamic_index_in_dim(orig_v[:, 0], core, 0, False)
    mine_u = lax.dynamic_index_in_dim(orig_u[:, 0], core, 0, False)
    start_proj = jnp.einsum("nr,ns->rs", mine_v, sampler, preferred_element_type=F32).astype(BF16)
    start = jnp.einsum("nr,rs->ns", mine_u, start_proj, preferred_element_type=F32)

    give = lax.dynamic_index_in_dim(update, 1 - core, 0, False).astype(BF16)
    keep = lax.dynamic_index_in_dim(update, core, 0, False)
    chip = keep + lax.ppermute(give, "cols", swap).astype(F32)
    total = chip
    chip_sent = chip.astype(BF16)
    for shift in range(1, pairs):
        total = total + lax.ppermute(
            chip_sent, "cols", [(i, (i + 2 * shift) % cols) for i in range(cols)]
        ).astype(F32)
    ysum = start - total

    qmine = cholesky_qr(ysum)
    qsent = qmine.astype(BF16)
    qother = lax.ppermute(qsent, "cols", swap)
    qround = jnp.where(core == 0, jnp.stack([qsent, qother]), jnp.stack([qother, qsent]))
    share = order // cols
    rows_mine = lax.dynamic_slice_in_dim(qmine, me * share, share, 0)
    rows_given = lax.dynamic_slice_in_dim(qmine, (me + 1 - 2 * core) * share, share, 0)
    rows_other = lax.ppermute(rows_given, "cols", swap)
    basis = jnp.where(core == 0, jnp.stack([rows_mine, rows_other]), jnp.stack([rows_other, rows_mine]))
    basis = basis * math.sqrt(order)

    proj_in = jnp.einsum("jnr,cns->cjrs", panel_u[0], qround, preferred_element_type=F32).astype(BF16)
    proj_in = proj_in * panel_mask[None, :, :, None]
    proj_mid = jnp.einsum("cjrq,cjrs->cjqs", cross, proj_in, preferred_element_type=F32).astype(BF16)
    proj_mid = proj_mid * pivot_mask[..., None]
    terms = jnp.einsum("cjnq,cjqs->cns", whole_u, proj_mid, preferred_element_type=F32)
    if count <= RING_MOST:
        terms = terms.reshape(-1, count, slab, width)[:, natural]
    terms = terms.reshape(-1, pairs, 2, share, width)
    give = lax.dynamic_index_in_dim(terms, 1 - core, 2, False).astype(BF16)
    keep = lax.dynamic_index_in_dim(terms, core, 2, False)
    chip = keep + lax.ppermute(give, "cols", swap).astype(F32)
    total = lax.dynamic_index_in_dim(chip, pair, 1, False)
    for shift in range(1, pairs):
        sent = lax.dynamic_index_in_dim(chip, (pair + shift) % pairs, 1, False).astype(BF16)
        total = total + lax.ppermute(
            sent, "cols", [(i, (i + 2 * shift) % cols) for i in range(cols)]
        ).astype(F32)

    left_proj = jnp.einsum("cnr,cns->crs", orig_u[:, 0], qround, preferred_element_type=F32).astype(BF16)
    right_rows = lax.dynamic_slice_in_dim(orig_v[:, 0], me * share, share, 1)
    coeff = jnp.einsum("cnr,crs->cns", right_rows, left_proj, preferred_element_type=F32) - total
    return (basis[:, None], coeff[:, None])


def solution(mesh):
    placed = (
        P("rows", "cols", None, None),
        P("rows", "cols", None, None),
        P("rows", "cols"),
        P(None, "cols", "rows", None),
        P(None, "cols", "rows", None),
        P(None, "cols"),
        P(None, "rows", None, None),
        P(None, "rows", None, None),
        P(),
    )
    return jax.shard_map(
        body,
        mesh=mesh,
        in_specs=placed,
        out_specs=(P(None, "rows", "cols", None), P(None, "rows", "cols", None)),
        check_vma=False,
    )
```

```python
import functools
import math

import jax
import jax.numpy as jnp
import numpy as np
from jax import lax
from jax.experimental import pallas as pl
from jax.experimental.pallas import tpu as pltpu
from jax.sharding import PartitionSpec as P

F32 = jnp.float32
BF16 = jnp.bfloat16
BLOCK = 32
GROUP = 4
SUB = 8
RING_MOST = 16
MIB = 1 << 20


def dot(a, b):
    return lax.dot_general(a, b, (((1,), (0,)), ((), ())), preferred_element_type=F32)


def dot00(a, b):
    return lax.dot_general(a, b, (((0,), (0,)), ((), ())), preferred_element_type=F32)


def dot11(a, b):
    return lax.dot_general(a, b, (((1,), (1,)), ((), ())), preferred_element_type=F32)


def split3(x):
    high = x.astype(BF16)
    rest = x - high.astype(F32)
    mid = rest.astype(BF16)
    low = (rest - mid.astype(F32)).astype(BF16)
    return high, mid, low


def reciprocal(x):
    guess = pl.reciprocal(x, approx=True)
    guess = guess * (2.0 - x * guess)
    return guess * (2.0 - x * guess)


def eliminate(panel, first):
    rows, width = panel.shape
    lanes = 128
    tile = (SUB, lanes)
    lane = lax.broadcasted_iota(jnp.int32, tile, 1)
    sub = lax.broadcasted_iota(jnp.int32, tile, 0)
    high = rows // SUB
    halves = width // lanes
    part = [
        [panel[v * SUB : (v + 1) * SUB, h * lanes : (h + 1) * lanes] for h in range(halves)]
        for v in range(high)
    ]
    mine = first // lanes
    pivots = [jnp.ones(tile, F32) for _ in range(high)]
    for k in range(0, rows, GROUP):
        at = first % lanes + k
        top, low = k // SUB, k % SUB
        inside = (lane >= at) & (lane < at + GROUP)
        column = [
            [jnp.broadcast_to(part[v][mine][:, at + m : at + m + 1], tile) for v in range(top, high)]
            for m in range(GROUP)
        ]
        small = [
            [jnp.broadcast_to(column[b][0][low + a : low + a + 1, :], tile) for b in range(a + 1)]
            for a in range(GROUP)
        ]
        row = []
        for a in range(GROUP):
            row.append([jnp.broadcast_to(part[top][h][low + a : low + a + 1, :], tile) for h in range(halves)])
            row[a][mine] = jnp.where(inside, jnp.where(lane == at + a, 1.0, 0.0), row[a][mine])
        factor = []
        for m in range(GROUP):
            inverse = reciprocal(small[m][m])
            pivots[top] = jnp.where(sub == low + m, small[m][m], pivots[top])
            for a in range(m + 1, GROUP):
                ratio = small[a][m] * inverse
                for b in range(m + 1, a + 1):
                    small[a][b] = small[a][b] - ratio * small[b][m]
                row[a] = [x - ratio * y for x, y in zip(row[a], row[m])]
            factor.append([c * inverse for c in column[m]])
            for b in range(m + 1, GROUP):
                column[b] = [c - f * small[b][m] for c, f in zip(column[b], factor[m])]
        for v in range(top, high):
            for h in range(halves):
                old = part[v][h]
                value = jnp.where(inside, 0.0, old) if h == mine else old
                for m in range(GROUP):
                    value = value - factor[m][v - top] * row[m][h]
                if v == top:
                    if low > 0:
                        value = jnp.where(sub < low, old, value)
                    for m in range(GROUP):
                        value = jnp.where(sub == low + m, row[m][h], value)
                part[v][h] = value
    done = []
    for v in range(high):
        scale = lax.rsqrt(pivots[v])
        cells = []
        for h in range(halves):
            value = part[v][h] * scale
            if h == mine:
                start = first % lanes
                value = jnp.where((lane > start + v * SUB + sub) & (lane < start + rows), 0.0, value)
            cells.append(value)
        done.append(jnp.concatenate(cells, 1))
    return jnp.concatenate(done, 0)


def invert_factor(work):
    width = work.shape[0]
    lane = lax.broadcasted_iota(jnp.int32, (1, width), 1)
    for first in range(0, width, BLOCK):
        last = first + BLOCK
        panel = eliminate(work[first:last, :], first)
        work[first:last, :] = panel
        if last < width:
            base = last // 128 * 128
            high, mid, low = split3(panel)
            left = jnp.concatenate([high, high, mid, mid, high, low], 0)[:, base:]
            right = jnp.concatenate([high, mid, high, mid, low, high], 0)
            update = dot00(left, right)[last - base :, :]
            inside = (lane >= first) & (lane < last)
            work[last:, :] = jnp.where(inside, 0.0, work[last:, :]) - update
    row = lax.broadcasted_iota(jnp.int32, (width, width), 0)
    col = lax.broadcasted_iota(jnp.int32, (width, width), 1)
    return jnp.where(col <= row, work[...], 0.0)


def orthonormal_kernel(info, mine, other, qt, basis, yt, work):
    half = mine.shape[1]
    core = info[0]
    yt[:, pl.ds(pl.multiple_of(core * half, 128), half)] = mine[...]
    yt[:, pl.ds(pl.multiple_of((1 - core) * half, 128), half)] = other[...]
    high, mid, low = split3(yt[...])
    cross = dot11(high, mid) + dot11(high, low)
    work[...] = dot11(high, high) + (cross + cross.T + dot11(mid, mid))
    inverse = invert_factor(work)
    m_high, m_low, _ = split3(inverse)
    q = dot(m_high, high) + (dot(m_high, mid) + dot(m_low, high))
    qt[...] = q.astype(BF16)
    yt[...] = q
    share = basis.shape[0]
    order = yt.shape[1]
    rows = yt[:, pl.ds(pl.multiple_of(info[1] * share, 128), share)]
    basis[...] = rows.T * math.sqrt(order)


def update_kernel(blocks, priors, info, ranks, panel_vt, sampler_t, panel_u, *refs):
    u, v = refs[:blocks], refs[blocks : 2 * blocks]
    cross, give, keep = refs[2 * blocks :]
    slab = u[0].shape[1]
    width = u[0].shape[2]
    half = keep.shape[1]
    core = info[0]

    def columns(index):
        return pl.ds(pl.multiple_of(info[2 + index] * slab, 128), slab)

    row = lax.broadcasted_iota(jnp.int32, (width, width), 0)
    col = lax.broadcasted_iota(jnp.int32, (width, width), 1)
    groups = [range(g, min(g + 2, blocks)) for g in range(0, blocks, 2)]
    drawn = [jnp.concatenate([sampler_t[:, columns(b)] for b in g], 1) for g in groups]
    terms = []
    for j in range(priors):
        sampled = jnp.zeros((width, width), F32)
        met = jnp.zeros((width, width), F32)
        for g, draw in zip(groups, drawn):
            sampled += dot(draw, jnp.concatenate([u[b][j] for b in g], 0))
            left = jnp.concatenate([panel_vt[j, :, columns(b)] for b in g], 1)
            met += dot(left, jnp.concatenate([v[b][j] for b in g], 0))
        met = jnp.where((row < ranks[0, j]) & (col < ranks[1, j]), met, 0.0).astype(BF16)
        cross[j] = met
        terms.append(dot11(sampled.astype(BF16), met).astype(BF16))
    for out, which in ((give, 1 - core), (keep, core)):
        rows = pl.ds(pl.multiple_of(which * half, 128), half)
        total = jnp.zeros((width, half), F32)
        for j in range(priors):
            total += dot11(terms[j], panel_u[j, rows, :])
        out[...] = total.astype(out.dtype)


def project_kernel(blocks, priors, info, qt, panel_u, cross, *refs):
    u = refs[:blocks]
    give, keep, work = refs[blocks:]
    slab = u[0].shape[1]
    pairs, share, _ = keep.shape
    core = info[0]
    mids = []
    for j in range(priors):
        inner = dot(qt[...], panel_u[j]).astype(BF16)
        mids.append(dot(inner, cross[j]).astype(BF16))
    step = max(1, blocks // 2)
    for begin in range(0, blocks, step):
        some = range(begin, min(begin + step, blocks))
        total = jnp.zeros((len(some) * slab, qt.shape[0]), F32)
        for j in range(priors):
            total += dot11(jnp.concatenate([u[b][j] for b in some], 0), mids[j])
        for n, b in enumerate(some):
            rows = pl.ds(pl.multiple_of(info[2 + b] * slab, SUB), slab)
            work[rows, :] = total[n * slab : (n + 1) * slab, :]
    for a in range(pairs):
        for out, which in ((give, 1 - core), (keep, core)):
            rows = pl.ds(pl.multiple_of((2 * a + which) * share, SUB), share)
            out[a] = work[rows, :].astype(out.dtype)


def left_kernel(info, qt, orig_u, orig_v, out):
    share = out.shape[0]
    left = dot(qt[...], orig_u[...]).astype(BF16)
    rows = orig_v[pl.ds(pl.multiple_of(info[1] * share, SUB), share), :]
    out[...] = dot11(rows, left)


def start_kernel(info, sampler_t, orig_u, orig_v, out):
    half = out.shape[2]
    for c in range(out.shape[0]):
        proj = dot(sampler_t[...], orig_v[c]).astype(BF16)
        rows = pl.ds(pl.multiple_of(info[0] * half, SUB), half)
        out[c] = dot11(proj, orig_u[c, rows, :])


def run(kernel, scalars, arrays, outs, scratch, limit, flops, name):
    smem = pl.BlockSpec(memory_space=pltpu.SMEM)
    vmem = pl.BlockSpec(memory_space=pltpu.VMEM)
    shapes = [jax.ShapeDtypeStruct(*o) for o in outs]
    moved = sum(a.size * a.dtype.itemsize for a in list(arrays) + shapes)
    return pl.pallas_call(
        kernel,
        out_shape=shapes,
        in_specs=[smem] * len(scalars) + [vmem] * len(arrays),
        out_specs=[vmem] * len(shapes),
        scratch_shapes=scratch,
        compiler_params=pltpu.CompilerParams(vmem_limit_bytes=limit * MIB),
        cost_estimate=pl.CostEstimate(flops=flops, bytes_accessed=moved, transcendentals=0),
        name=name,
    )(*scalars, *arrays)


def ring_order(count):
    if count % 2:
        return list(range(count))
    return list(range(0, count, 2)) + list(range(count - 1, 0, -2))


def ring_gather(u, v, order, axis):
    count = len(order)
    ahead = [(order[(p + 1) % count], order[p]) for p in range(count)]
    behind = [(order[p], order[(p + 1) % count]) for p in range(count)]
    found = [{0: u}, {0: v}]
    up, down = [u, v], [u, v]
    near = (count - 1) // 2
    for step in range(1, count // 2 + 1):
        for t in range(2):
            if step <= near or t == 0:
                up[t] = lax.ppermute(up[t], axis, ahead)
                found[t][step] = up[t]
            if step <= near or t == 1:
                down[t] = lax.ppermute(down[t], axis, behind)
                found[t][count - step] = down[t]
    return [[f[d] for d in range(count)] for f in found]


def body(panel_u, panel_v, panel_rank, pivot_u, pivot_v, pivot_rank, orig_u, orig_v, sampler):
    order, width = panel_u.shape[2:]
    priors = panel_u.shape[1]
    pivots = pivot_u.shape[0]
    count = lax.axis_size("rows")
    cols = lax.axis_size("cols")
    pairs = cols // 2
    half, share = order // 2, order // cols
    me = lax.axis_index("cols")
    core, pair = me % 2, me // 2
    swap = [(i, i ^ 1) for i in range(cols)]

    ring = ring_order(count)
    place = np.argsort(np.array(ring))
    table = np.array([[ring[(place[r] + d) % count] for d in range(count)] for r in range(count)], np.int32)
    if count > RING_MOST:
        table = np.zeros((count, 1), np.int32)
    sources = jnp.asarray(table)[lax.axis_index("rows")]
    info = jnp.concatenate([jnp.stack([core, me]).astype(jnp.int32), sources])

    panel_u, panel_v, orig_u, orig_v = panel_u[0], panel_v[0], orig_u[:, 0], orig_v[:, 0]
    panel_vt = panel_v.transpose(0, 2, 1)
    sampler_t = sampler.T
    square = 2 * width * width
    (start,) = run(
        start_kernel, [info], [sampler_t, orig_u, orig_v], [((pivots, width, half), F32)], [], 24,
        pivots * square * (order + half), "start"
    )

    def shifted(x, shift):
        return lax.ppermute(x, "cols", [(i, (i + 2 * shift) % cols) for i in range(cols)])

    basis, coeff = [], []
    after = None
    for c in range(pivots):
        u, v = pivot_u[c], pivot_v[c]
        if count > RING_MOST:
            blocks_u, blocks_v = ([lax.all_gather(x, "rows", axis=1, tiled=True)] for x in (u, v))
        else:
            if after is not None:
                u, v, _ = lax.optimization_barrier((u, v, after))
            blocks_u, blocks_v = ring_gather(u, v, ring, "rows")
            after = blocks_u[count // 2 - 1]
        blocks = len(blocks_u)
        ranks = jnp.stack([panel_rank[0], pivot_rank[c]])
        cross, give, keep = run(
            functools.partial(update_kernel, blocks, priors), [info, ranks],
            [panel_vt, sampler_t, panel_u, *blocks_u, *blocks_v],
            [((priors, width, width), BF16), ((width, half), BF16), ((width, half), F32)],
            [], 24, priors * square * (3 * order + width), "update"
        )
        chip = keep + lax.ppermute(give, "cols", swap).astype(F32)
        sent = chip.astype(BF16)
        for shift in range(1, pairs):
            chip = chip + shifted(sent, shift).astype(F32)
        ymine = start[c] - chip
        yother = lax.ppermute(ymine, "cols", swap)
        qt, rows = run(
            orthonormal_kernel, [info], [ymine, yother], [((width, order), BF16), ((share, width), F32)],
            [pltpu.VMEM((width, order), F32), pltpu.VMEM((width, width), F32)], 24, 40 * square * order, "orthonormal"
        )
        basis.append(rows)
        give, keep = run(
            functools.partial(project_kernel, blocks, priors), [info], [qt, panel_u, cross, *blocks_u],
            [((pairs, share, width), BF16), ((pairs, share, width), F32)], [pltpu.VMEM((order, width), F32)], 24,
            priors * square * (2 * order + width), "project"
        )
        (own,) = run(
            left_kernel, [info], [qt, orig_u[c], orig_v[c]], [((share, width), F32)], [], 16,
            square * (order + share), "left"
        )
        chip = keep + lax.ppermute(give, "cols", swap).astype(F32)
        total = lax.dynamic_index_in_dim(chip, pair, 0, False)
        for shift in range(1, pairs):
            sent = lax.dynamic_index_in_dim(chip, (pair + shift) % pairs, 0, False).astype(BF16)
            total = total + shifted(sent, shift).astype(F32)
        coeff.append(own - total)
    return (jnp.stack(basis)[:, None], jnp.stack(coeff)[:, None])


def solution(mesh):
    placed = (
        P("rows", "cols", None, None),
        P("rows", "cols", None, None),
        P("rows", "cols"),
        P(None, "cols", "rows", None),
        P(None, "cols", "rows", None),
        P(None, "cols"),
        P(None, "rows", None, None),
        P(None, "rows", None, None),
        P(),
    )
    return jax.shard_map(
        body,
        mesh=mesh,
        in_specs=placed,
        out_specs=(P(None, "rows", "cols", None), P(None, "rows", "cols", None)),
        check_vma=False,
    )
```

```python
import functools
import math

import jax
import jax.numpy as jnp
import numpy as np
from jax import lax
from jax.experimental import pallas as pl
from jax.experimental.pallas import tpu as pltpu
from jax.sharding import PartitionSpec as P

F32 = jnp.float32
BF16 = jnp.bfloat16
BLOCK = 32
GROUP = 4
SUB = 8
RING_MOST = 16
MIB = 1 << 20


def dot(a, b):
    return lax.dot_general(a, b, (((1,), (0,)), ((), ())), preferred_element_type=F32)


def dot00(a, b):
    return lax.dot_general(a, b, (((0,), (0,)), ((), ())), preferred_element_type=F32)


def dot11(a, b):
    return lax.dot_general(a, b, (((1,), (1,)), ((), ())), preferred_element_type=F32)


def split3(x):
    high = x.astype(BF16)
    rest = x - high.astype(F32)
    mid = rest.astype(BF16)
    low = (rest - mid.astype(F32)).astype(BF16)
    return high, mid, low


def reciprocal(x):
    guess = pl.reciprocal(x, approx=True)
    guess = guess * (2.0 - x * guess)
    return guess * (2.0 - x * guess)


def eliminate(panel, first):
    rows, width = panel.shape
    lanes = 128
    tile = (SUB, lanes)
    lane = lax.broadcasted_iota(jnp.int32, tile, 1)
    sub = lax.broadcasted_iota(jnp.int32, tile, 0)
    high = rows // SUB
    halves = width // lanes
    part = [
        [panel[v * SUB : (v + 1) * SUB, h * lanes : (h + 1) * lanes] for h in range(halves)]
        for v in range(high)
    ]
    mine = first // lanes
    pivots = [jnp.ones(tile, F32) for _ in range(high)]
    for k in range(0, rows, GROUP):
        at = first % lanes + k
        top, low = k // SUB, k % SUB
        inside = (lane >= at) & (lane < at + GROUP)
        column = [
            [jnp.broadcast_to(part[v][mine][:, at + m : at + m + 1], tile) for v in range(top, high)]
            for m in range(GROUP)
        ]
        small = [
            [jnp.broadcast_to(column[b][0][low + a : low + a + 1, :], tile) for b in range(a + 1)]
            for a in range(GROUP)
        ]
        row = []
        for a in range(GROUP):
            row.append([jnp.broadcast_to(part[top][h][low + a : low + a + 1, :], tile) for h in range(halves)])
            row[a][mine] = jnp.where(inside, jnp.where(lane == at + a, 1.0, 0.0), row[a][mine])
        factor = []
        for m in range(GROUP):
            inverse = reciprocal(small[m][m])
            pivots[top] = jnp.where(sub == low + m, small[m][m], pivots[top])
            for a in range(m + 1, GROUP):
                ratio = small[a][m] * inverse
                for b in range(m + 1, a + 1):
                    small[a][b] = small[a][b] - ratio * small[b][m]
                row[a] = [x - ratio * y for x, y in zip(row[a], row[m])]
            factor.append([c * inverse for c in column[m]])
            for b in range(m + 1, GROUP):
                column[b] = [c - f * small[b][m] for c, f in zip(column[b], factor[m])]
        for v in range(top, high):
            for h in range(halves):
                old = part[v][h]
                value = jnp.where(inside, 0.0, old) if h == mine else old
                for m in range(GROUP):
                    value = value - factor[m][v - top] * row[m][h]
                if v == top:
                    if low > 0:
                        value = jnp.where(sub < low, old, value)
                    for m in range(GROUP):
                        value = jnp.where(sub == low + m, row[m][h], value)
                part[v][h] = value
    done = []
    for v in range(high):
        scale = lax.rsqrt(pivots[v])
        cells = []
        for h in range(halves):
            value = part[v][h] * scale
            if h == mine:
                start = first % lanes
                value = jnp.where((lane > start + v * SUB + sub) & (lane < start + rows), 0.0, value)
            cells.append(value)
        done.append(jnp.concatenate(cells, 1))
    return jnp.concatenate(done, 0)


def invert_blocks(work, begin, end):
    width = work.shape[0]
    lane = lax.broadcasted_iota(jnp.int32, (1, width), 1)
    for first in range(begin, end, BLOCK):
        last = first + BLOCK
        panel = eliminate(work[first:last, :], first)
        work[first:last, :] = panel
        if last < width:
            base = last // 128 * 128
            high, mid, low = split3(panel)
            left = jnp.concatenate([high, high, mid, mid, high, low], 0)[:, base:]
            right = jnp.concatenate([high, mid, high, mid, low, high], 0)
            update = dot00(left, right)[last - base :, :]
            inside = (lane >= first) & (lane < last)
            work[last:, :] = jnp.where(inside, 0.0, work[last:, :]) - update


def gram_of(info, mine, other, yt, work):
    half = mine.shape[1]
    core = info[0]
    yt[:, pl.ds(pl.multiple_of(core * half, 128), half)] = mine[...]
    yt[:, pl.ds(pl.multiple_of((1 - core) * half, 128), half)] = other[...]
    high, mid, low = split3(yt[...])
    cross = dot11(high, mid) + dot11(high, low)
    work[...] = dot11(high, high) + (cross + cross.T + dot11(mid, mid))


def apply_factor(info, y, work, qt, basis, q):
    width, order = y.shape
    row = lax.broadcasted_iota(jnp.int32, (width, width), 0)
    col = lax.broadcasted_iota(jnp.int32, (width, width), 1)
    m_high, m_low, _ = split3(jnp.where(col <= row, work[...], 0.0))
    high, mid, _ = split3(y[...])
    product = dot(m_high, high) + (dot(m_high, mid) + dot(m_low, high))
    qt[...] = product.astype(BF16)
    q[...] = product
    share = basis.shape[0]
    rows = q[:, pl.ds(pl.multiple_of(info[1] * share, 128), share)]
    basis[...] = rows.T * math.sqrt(order)


def orthonormal_kernel(info, mine, other, qt, basis, yt, work):
    gram_of(info, mine, other, yt, work)
    invert_blocks(work, 0, work.shape[0])
    apply_factor(info, yt, work, qt, basis, yt)


def first_kernel(info, mine, other, yt, out, work):
    gram_of(info, mine, other, yt, work)
    invert_blocks(work, 0, work.shape[0] // 2)
    out[...] = work[...]


def last_kernel(info, y, begun, qt, basis, q, work):
    work[...] = begun[...]
    invert_blocks(work, work.shape[0] // 2, work.shape[0])
    apply_factor(info, y, work, qt, basis, q)


def fetch(blocks, buffer, sems, which):
    slab = blocks[0].shape[1]
    return [
        [
            pltpu.make_async_copy(b.at[j], buffer.at[j, pl.ds(n * slab, slab)], sems.at[which, j, n])
            for n, b in enumerate(blocks)
        ]
        for j in range(buffer.shape[0])
    ]


def update_kernel(blocks, info, ranks, panel_vt, sampler_t, panel_u, *refs):
    u, v = refs[:blocks], refs[blocks : 2 * blocks]
    cross, give, keep, u_buf, v_buf, sems = refs[2 * blocks :]
    priors, order, width = u_buf.shape
    slab = order // blocks
    half = keep.shape[1]
    core = info[0]
    copies = [fetch(u, u_buf, sems, 0), fetch(v, v_buf, sems, 1)]
    for j in range(priors):
        for t in range(2):
            for copy in copies[t][j]:
                copy.start()
    spans = [pl.ds(pl.multiple_of(info[2 + b] * slab, 128), slab) for b in range(blocks)]
    row = lax.broadcasted_iota(jnp.int32, (width, width), 0)
    col = lax.broadcasted_iota(jnp.int32, (width, width), 1)
    drawn = jnp.concatenate([sampler_t[:, span] for span in spans], 1)
    terms = []
    for j in range(priors):
        for t in range(2):
            for copy in copies[t][j]:
                copy.wait()
        sampled = dot(drawn, u_buf[j])
        met = dot(jnp.concatenate([panel_vt[j, :, span] for span in spans], 1), v_buf[j])
        met = jnp.where((row < ranks[0, j]) & (col < ranks[1, j]), met, 0.0).astype(BF16)
        cross[j] = met
        terms.append(dot11(sampled.astype(BF16), met).astype(BF16))
    for out, which in ((give, 1 - core), (keep, core)):
        rows = pl.ds(pl.multiple_of(which * half, 128), half)
        total = jnp.zeros((width, half), F32)
        for j in range(priors):
            total += dot11(terms[j], panel_u[j, rows, :])
        out[...] = total.astype(out.dtype)


def project_kernel(blocks, info, qt, panel_u, cross, *refs):
    u = refs[:blocks]
    give, keep, work, u_buf, sems = refs[blocks:]
    priors, order, width = u_buf.shape
    slab = order // blocks
    pairs, share, _ = keep.shape
    core = info[0]
    copies = fetch(u, u_buf, sems, 0)
    for each in copies:
        for copy in each:
            copy.start()
    mids = []
    for j in range(priors):
        inner = dot(qt[...], panel_u[j]).astype(BF16)
        mids.append(dot(inner, cross[j]).astype(BF16))
    for each in copies:
        for copy in each:
            copy.wait()
    some = max(1, blocks // 2)
    for begin in range(0, blocks, some):
        total = jnp.zeros((some * slab, width), F32)
        for j in range(priors):
            total += dot11(u_buf[j, begin * slab : (begin + some) * slab, :], mids[j])
        for n in range(some):
            rows = pl.ds(pl.multiple_of(info[2 + begin + n] * slab, SUB), slab)
            work[rows, :] = total[n * slab : (n + 1) * slab, :]
    for a in range(pairs):
        for out, which in ((give, 1 - core), (keep, core)):
            rows = pl.ds(pl.multiple_of((2 * a + which) * share, SUB), share)
            out[a] = work[rows, :].astype(out.dtype)


def left_kernel(info, qt, orig_u, orig_v, out):
    share = out.shape[0]
    left = dot(qt[...], orig_u[...]).astype(BF16)
    rows = orig_v[pl.ds(pl.multiple_of(info[1] * share, SUB), share), :]
    out[...] = dot11(rows, left)


def turn_kernel(panel_v, sampler, panel_vt, sampler_t):
    sampler_t[...] = sampler[...].T
    for j in range(panel_v.shape[0]):
        panel_vt[j] = panel_v[j].T


def start_kernel(info, sampler_t, orig_u, orig_v, out):
    half = out.shape[2]
    for c in range(out.shape[0]):
        proj = dot(sampler_t[...], orig_v[c]).astype(BF16)
        rows = pl.ds(pl.multiple_of(info[0] * half, SUB), half)
        out[c] = dot11(proj, orig_u[c, rows, :])


def run(kernel, scalars, arrays, outs, scratch, limit, flops, name, apart=()):
    smem = pl.BlockSpec(memory_space=pltpu.SMEM)
    vmem = pl.BlockSpec(memory_space=pltpu.VMEM)
    shapes = [jax.ShapeDtypeStruct(*o) for o in outs]
    moved = sum(a.size * a.dtype.itemsize for a in list(arrays) + list(apart) + shapes)
    return pl.pallas_call(
        kernel,
        out_shape=shapes,
        in_specs=[smem] * len(scalars) + [vmem] * len(arrays) + [pl.BlockSpec(memory_space=pl.ANY)] * len(apart),
        out_specs=[vmem] * len(shapes),
        scratch_shapes=scratch,
        compiler_params=pltpu.CompilerParams(vmem_limit_bytes=limit * MIB),
        cost_estimate=pl.CostEstimate(flops=flops, bytes_accessed=moved, transcendentals=0),
        name=name,
    )(*scalars, *arrays, *apart)


def ring_order(count):
    if count % 2:
        return list(range(count))
    return list(range(0, count, 2)) + list(range(count - 1, 0, -2))


class Ring:
    def __init__(self, arrays, order, axis):
        count = len(order)
        self.count, self.axis, self.near = count, axis, (count - 1) // 2
        self.ahead = [(order[(p + 1) % count], order[p]) for p in range(count)]
        self.behind = [(order[p], order[(p + 1) % count]) for p in range(count)]
        self.found = [{0: a} for a in arrays]
        self.up, self.down = list(arrays), list(arrays)

    def step(self, number):
        for t in range(2):
            if number <= self.near or t == 0:
                self.up[t] = lax.ppermute(self.up[t], self.axis, self.ahead)
                self.found[t][number] = self.up[t]
            if number <= self.near or t == 1:
                self.down[t] = lax.ppermute(self.down[t], self.axis, self.behind)
                self.found[t][self.count - number] = self.down[t]

    def hold(self, value, t, number):
        if number > self.near:
            return value
        places = (number, self.count - number)
        value, *kept = lax.optimization_barrier((value, *(self.found[t][d] for d in places)))
        for d, block in zip(places, kept):
            self.found[t][d] = block
        return value

    def tie(self, value, number, which=(0, 1)):
        lists = [(self.up, t, number) for t in which if number <= self.near or t == 0]
        lists += [(self.down, t, self.count - number) for t in which if number <= self.near or t == 1]
        value, *held = lax.optimization_barrier((value, *(way[t] for way, t, _ in lists)))
        for (way, t, place), block in zip(lists, held):
            way[t] = self.found[t][place] = block
        return value

    def blocks(self, t):
        return [self.found[t][d] for d in range(self.count)]


def body(panel_u, panel_v, panel_rank, pivot_u, pivot_v, pivot_rank, orig_u, orig_v, sampler):
    order, width = panel_u.shape[2:]
    priors = panel_u.shape[1]
    pivots = pivot_u.shape[0]
    count = lax.axis_size("rows")
    cols = lax.axis_size("cols")
    pairs = cols // 2
    half, share = order // 2, order // cols
    me = lax.axis_index("cols")
    core, pair = me % 2, me // 2
    swap = [(i, i ^ 1) for i in range(cols)]

    ring = ring_order(count)
    place = np.argsort(np.array(ring))
    table = np.array([[ring[(place[r] + d) % count] for d in range(count)] for r in range(count)], np.int32)
    if count > RING_MOST:
        table = np.zeros((count, 1), np.int32)
    sources = jnp.asarray(table)[lax.axis_index("rows")]
    info = jnp.concatenate([jnp.stack([core, me]).astype(jnp.int32), sources])

    panel_u, panel_v, orig_u, orig_v = panel_u[0], panel_v[0], orig_u[:, 0], orig_v[:, 0]
    square = 2 * width * width
    panel_vt, sampler_t = run(
        turn_kernel, [], [panel_v, sampler], [((priors, width, order), BF16), ((sampler.shape[1], order), BF16)], [], 12,
        10 * square * order, "turn"
    )
    whole = count > RING_MOST
    if not whole:
        now = Ring([pivot_u[0], pivot_v[0]], ring, "rows")
        now.step(1)
        panel_vt = now.tie(panel_vt, 1, (1,))
        now.step(2)
    (start,) = run(
        start_kernel, [info], [sampler_t, orig_u, orig_v], [((pivots, width, half), F32)], [], 12,
        pivots * square * (order + half), "start"
    )
    if not whole:
        start = now.tie(start, 2, (1,))
        for number in range(3, count // 2 + 1):
            now.step(number)

    def shifted(x, shift):
        return lax.ppermute(x, "cols", [(i, (i + 2 * shift) % cols) for i in range(cols)])

    buffer = pltpu.VMEM((priors, order, width), BF16)
    matrix = pltpu.VMEM((width, width), F32)
    tall = pltpu.VMEM((width, order), F32)

    def updated(c, blocks_u, blocks_v):
        blocks = len(blocks_u)
        ranks = jnp.stack([panel_rank[0], pivot_rank[c]])
        return run(
            functools.partial(update_kernel, blocks), [info, ranks], [panel_vt, sampler_t, panel_u],
            [((priors, width, width), BF16), ((width, half), BF16), ((width, half), F32)],
            [buffer, buffer, pltpu.SemaphoreType.DMA((2, priors, blocks))], 20,
            3 * priors * square * (3 * order + width), "update", (*blocks_u, *blocks_v)
        )

    def finished(c, blocks_u, cross, give, keep, beside):
        blocks = len(blocks_u)
        chip = keep + lax.ppermute(give, "cols", swap).astype(F32)
        sent = chip.astype(BF16)
        for shift in range(1, pairs):
            chip = chip + shifted(sent, shift).astype(F32)
        if beside is not None:
            chip = beside.tie(chip, 2)
            beside.step(3)
        ymine = start[c] - chip
        yother = lax.ppermute(ymine, "cols", swap)
        finals = [((width, order), BF16), ((share, width), F32)]
        if beside is None:
            qt, rows = run(
                orthonormal_kernel, [info], [ymine, yother], finals, [tall, matrix], 12, 128 * square * order, "orthonormal"
            )
        else:
            yt, work = run(
                first_kernel, [info], [ymine, yother], [((width, order), F32), ((width, width), F32)], [matrix], 12,
                64 * square * order, "orthonormal_first"
            )
            work = beside.tie(work, 3)
            beside.step(4)
            qt, rows = run(
                last_kernel, [info], [yt, work], finals, [tall, matrix], 12, 64 * square * order, "orthonormal_last"
            )
            beside.found[0][0], qt = lax.optimization_barrier((beside.found[0][0], qt))
        give, keep = run(
            functools.partial(project_kernel, blocks), [info], [qt, panel_u, cross],
            [((pairs, share, width), BF16), ((pairs, share, width), F32)],
            [pltpu.VMEM((order, width), F32), buffer, pltpu.SemaphoreType.DMA((1, priors, blocks))], 16,
            3 * priors * square * (2 * order + width), "project", blocks_u
        )
        (own,) = run(
            left_kernel, [info], [qt, orig_u[c], orig_v[c]], [((share, width), F32)], [], 8,
            square * (order + share), "left"
        )
        chip = keep + lax.ppermute(give, "cols", swap).astype(F32)
        total = lax.dynamic_index_in_dim(chip, pair, 0, False)
        for shift in range(1, pairs):
            sent = lax.dynamic_index_in_dim(chip, (pair + shift) % pairs, 0, False).astype(BF16)
            total = total + shifted(sent, shift).astype(F32)
        return rows, own - total

    results = []
    if whole:
        for c in range(pivots):
            blocks_u, blocks_v = ([lax.all_gather(x[c], "rows", axis=1, tiled=True)] for x in (pivot_u, pivot_v))
            results.append(finished(c, blocks_u, *updated(c, blocks_u, blocks_v), None))
    else:
        for c in range(pivots):
            later = None
            if c + 1 < pivots:
                later = Ring([now.hold(pivot_u[c + 1], 0, now.near), now.hold(pivot_v[c + 1], 1, now.near)], ring, "rows")
                later.step(1)
            cross, give, keep = updated(c, now.blocks(0), now.blocks(1))
            if later is not None:
                give = later.tie(give, 1)
                later.step(2)
            results.append(finished(c, now.blocks(0), cross, give, keep, later))
            now = later
    basis, coeff = zip(*results)
    return (jnp.stack(basis)[:, None], jnp.stack(coeff)[:, None])


def solution(mesh):
    placed = (
        P("rows", "cols", None, None),
        P("rows", "cols", None, None),
        P("rows", "cols"),
        P(None, "cols", "rows", None),
        P(None, "cols", "rows", None),
        P(None, "cols"),
        P(None, "rows", None, None),
        P(None, "rows", None, None),
        P(),
    )
    return jax.shard_map(
        body,
        mesh=mesh,
        in_specs=placed,
        out_specs=(P(None, "rows", "cols", None), P(None, "rows", "cols", None)),
        check_vma=False,
    )
```

```python
import functools
import math

import jax
import jax.numpy as jnp
import numpy as np
from jax import lax
from jax.experimental import pallas as pl
from jax.experimental.pallas import tpu as pltpu
from jax.sharding import PartitionSpec as P

F32 = jnp.float32
BF16 = jnp.bfloat16
BLOCK = 32
GROUP = 4
SUB = 8
RING_MOST = 16
MIB = 1 << 20


def dot(a, b):
    return lax.dot_general(a, b, (((1,), (0,)), ((), ())), preferred_element_type=F32)


def dot00(a, b):
    return lax.dot_general(a, b, (((0,), (0,)), ((), ())), preferred_element_type=F32)


def dot11(a, b):
    return lax.dot_general(a, b, (((1,), (1,)), ((), ())), preferred_element_type=F32)


def split3(x):
    high = x.astype(BF16)
    rest = x - high.astype(F32)
    mid = rest.astype(BF16)
    low = (rest - mid.astype(F32)).astype(BF16)
    return high, mid, low


def reciprocal(x):
    guess = pl.reciprocal(x, approx=True)
    guess = guess * (2.0 - x * guess)
    return guess * (2.0 - x * guess)


def eliminate(panel, first):
    rows, width = panel.shape
    lanes = 128
    tile = (SUB, lanes)
    lane = lax.broadcasted_iota(jnp.int32, tile, 1)
    sub = lax.broadcasted_iota(jnp.int32, tile, 0)
    high = rows // SUB
    halves = width // lanes
    part = [
        [panel[v * SUB : (v + 1) * SUB, h * lanes : (h + 1) * lanes] for h in range(halves)]
        for v in range(high)
    ]
    mine = first // lanes
    pivots = [jnp.ones(tile, F32) for _ in range(high)]
    for k in range(0, rows, GROUP):
        at = first % lanes + k
        top, low = k // SUB, k % SUB
        inside = (lane >= at) & (lane < at + GROUP)
        column = [
            [jnp.broadcast_to(part[v][mine][:, at + m : at + m + 1], tile) for v in range(top, high)]
            for m in range(GROUP)
        ]
        small = [
            [jnp.broadcast_to(column[b][0][low + a : low + a + 1, :], tile) for b in range(a + 1)]
            for a in range(GROUP)
        ]
        row = []
        for a in range(GROUP):
            row.append([jnp.broadcast_to(part[top][h][low + a : low + a + 1, :], tile) for h in range(halves)])
            row[a][mine] = jnp.where(inside, jnp.where(lane == at + a, 1.0, 0.0), row[a][mine])
        factor = []
        for m in range(GROUP):
            inverse = reciprocal(small[m][m])
            pivots[top] = jnp.where(sub == low + m, small[m][m], pivots[top])
            for a in range(m + 1, GROUP):
                ratio = small[a][m] * inverse
                for b in range(m + 1, a + 1):
                    small[a][b] = small[a][b] - ratio * small[b][m]
                row[a] = [x - ratio * y for x, y in zip(row[a], row[m])]
            factor.append([c * inverse for c in column[m]])
            for b in range(m + 1, GROUP):
                column[b] = [c - f * small[b][m] for c, f in zip(column[b], factor[m])]
        for v in range(top, high):
            for h in range(halves):
                old = part[v][h]
                value = jnp.where(inside, 0.0, old) if h == mine else old
                for m in range(GROUP):
                    value = value - factor[m][v - top] * row[m][h]
                if v == top:
                    if low > 0:
                        value = jnp.where(sub < low, old, value)
                    for m in range(GROUP):
                        value = jnp.where(sub == low + m, row[m][h], value)
                part[v][h] = value
    done = []
    for v in range(high):
        scale = lax.rsqrt(pivots[v])
        cells = []
        for h in range(halves):
            value = part[v][h] * scale
            if h == mine:
                start = first % lanes
                value = jnp.where((lane > start + v * SUB + sub) & (lane < start + rows), 0.0, value)
            cells.append(value)
        done.append(jnp.concatenate(cells, 1))
    return jnp.concatenate(done, 0)


def invert_blocks(work, begin, end):
    width = work.shape[0]
    lane = lax.broadcasted_iota(jnp.int32, (1, width), 1)
    for first in range(begin, end, BLOCK):
        last = first + BLOCK
        panel = eliminate(work[first:last, :], first)
        work[first:last, :] = panel
        if last < width:
            base = last // 128 * 128
            high, mid, low = split3(panel)
            left = jnp.concatenate([high, high, mid, mid, high, low], 0)[:, base:]
            right = jnp.concatenate([high, mid, high, mid, low, high], 0)
            update = dot00(left, right)[last - base :, :]
            inside = (lane >= first) & (lane < last)
            work[last:, :] = jnp.where(inside, 0.0, work[last:, :]) - update


def gram_of(info, mine, other, yt, work):
    half = mine.shape[1]
    core = info[0]
    yt[:, pl.ds(pl.multiple_of(core * half, 128), half)] = mine[...]
    yt[:, pl.ds(pl.multiple_of((1 - core) * half, 128), half)] = other[...]
    high, mid, low = split3(yt[...])
    cross = dot11(high, mid) + dot11(high, low)
    work[...] = dot11(high, high) + (cross + cross.T + dot11(mid, mid))


def apply_factor(info, y, work, qt, basis, q):
    width, order = y.shape
    row = lax.broadcasted_iota(jnp.int32, (width, width), 0)
    col = lax.broadcasted_iota(jnp.int32, (width, width), 1)
    m_high, m_low, _ = split3(jnp.where(col <= row, work[...], 0.0))
    high, mid, _ = split3(y[...])
    product = dot(m_high, high) + (dot(m_high, mid) + dot(m_low, high))
    qt[...] = product.astype(BF16)
    q[...] = product
    share = basis.shape[0]
    rows = q[:, pl.ds(pl.multiple_of(info[1] * share, 128), share)]
    basis[...] = rows.T * math.sqrt(order)


def orthonormal_kernel(info, mine, other, qt, basis, yt, work):
    gram_of(info, mine, other, yt, work)
    invert_blocks(work, 0, work.shape[0])
    apply_factor(info, yt, work, qt, basis, yt)


def first_kernel(info, mine, other, yt, out, work):
    gram_of(info, mine, other, yt, work)
    invert_blocks(work, 0, work.shape[0] // 2)
    out[...] = work[...]


def last_kernel(info, y, begun, qt, basis, q, work):
    work[...] = begun[...]
    invert_blocks(work, work.shape[0] // 2, work.shape[0])
    apply_factor(info, y, work, qt, basis, q)


def gather_kernel(places, blocks, info, panel_vt, sampler_t, *refs):
    new = len(places)
    u, v = refs[:new], refs[new : 2 * new]
    kept = refs[2 * new : -3]
    sampled, met, u_all = refs[-3:]
    priors, order, width = u_all.shape
    slab = order // blocks
    spans = [pl.ds(pl.multiple_of(info[2 + p] * slab, 128), slab) for p in places]
    drawn = jnp.concatenate([sampler_t[:, span] for span in spans], 1)
    for j in range(priors):
        left = jnp.concatenate([panel_vt[j, :, span] for span in spans], 1)
        u_new = jnp.concatenate([block[j] for block in u], 0)
        v_new = jnp.concatenate([block[j] for block in v], 0)
        one, two = dot(drawn, u_new), dot(left, v_new)
        if kept:
            one, two = one + kept[0][j], two + kept[1][j]
        sampled[j] = one
        met[j] = two
        for n, p in enumerate(places):
            u_all[j, p * slab : (p + 1) * slab, :] = u_new[n * slab : (n + 1) * slab, :]


def update_kernel(info, ranks, sampled, met, panel_u, cross, give, keep):
    priors, width, _ = cross.shape
    half = keep.shape[1]
    core = info[0]
    row = lax.broadcasted_iota(jnp.int32, (width, width), 0)
    col = lax.broadcasted_iota(jnp.int32, (width, width), 1)
    terms = []
    for j in range(priors):
        inside = (row < ranks[0, j]) & (col < ranks[1, j])
        cross[j] = jnp.where(inside, met[j], 0.0).astype(BF16)
        terms.append(dot11(sampled[j].astype(BF16), cross[j]).astype(BF16))
    for out, which in ((give, 1 - core), (keep, core)):
        rows = pl.ds(pl.multiple_of(which * half, 128), half)
        total = jnp.zeros((width, half), F32)
        for j in range(priors):
            total += dot11(terms[j], panel_u[j, rows, :])
        out[...] = total.astype(out.dtype)


def project_kernel(blocks, info, qt, panel_u, cross, u_all, give, keep, work):
    priors, order, width = u_all.shape
    slab = order // blocks
    pairs, share, _ = keep.shape
    core = info[0]
    mids = []
    for j in range(priors):
        inner = dot(qt[...], panel_u[j]).astype(BF16)
        mids.append(dot(inner, cross[j]).astype(BF16))
    some = max(1, blocks // 2)
    for begin in range(0, blocks, some):
        total = jnp.zeros((some * slab, width), F32)
        for j in range(priors):
            total += dot11(u_all[j, begin * slab : (begin + some) * slab, :], mids[j])
        for n in range(some):
            rows = pl.ds(pl.multiple_of(info[2 + begin + n] * slab, SUB), slab)
            work[rows, :] = total[n * slab : (n + 1) * slab, :]
    for a in range(pairs):
        for out, which in ((give, 1 - core), (keep, core)):
            rows = pl.ds(pl.multiple_of((2 * a + which) * share, SUB), share)
            out[a] = work[rows, :].astype(out.dtype)


def left_kernel(info, qt, orig_u, orig_v, out):
    share = out.shape[0]
    left = dot(qt[...], orig_u[...]).astype(BF16)
    rows = orig_v[pl.ds(pl.multiple_of(info[1] * share, SUB), share), :]
    out[...] = dot11(rows, left)


def turn_kernel(panel_v, sampler, panel_vt, sampler_t):
    sampler_t[...] = sampler[...].T
    for j in range(panel_v.shape[0]):
        panel_vt[j] = panel_v[j].T


def start_kernel(info, sampler_t, orig_u, orig_v, out):
    half = out.shape[2]
    for c in range(out.shape[0]):
        proj = dot(sampler_t[...], orig_v[c]).astype(BF16)
        rows = pl.ds(pl.multiple_of(info[0] * half, SUB), half)
        out[c] = dot11(proj, orig_u[c, rows, :])


def run(kernel, scalars, arrays, outs, scratch, limit, flops, name, aliases={}):
    smem = pl.BlockSpec(memory_space=pltpu.SMEM)
    vmem = pl.BlockSpec(memory_space=pltpu.VMEM)
    shapes = [jax.ShapeDtypeStruct(*o) for o in outs]
    moved = sum(a.size * a.dtype.itemsize for a in list(arrays) + shapes)
    return pl.pallas_call(
        kernel,
        out_shape=shapes,
        in_specs=[smem] * len(scalars) + [vmem] * len(arrays),
        out_specs=[vmem] * len(shapes),
        scratch_shapes=scratch,
        input_output_aliases=aliases,
        compiler_params=pltpu.CompilerParams(vmem_limit_bytes=limit * MIB),
        cost_estimate=pl.CostEstimate(flops=flops, bytes_accessed=moved, transcendentals=0),
        name=name,
    )(*scalars, *arrays)


def ring_order(count):
    if count % 2:
        return list(range(count))
    return list(range(0, count, 2)) + list(range(count - 1, 0, -2))


class Ring:
    def __init__(self, arrays, order, axis):
        count = len(order)
        self.count, self.axis, self.near = count, axis, (count - 1) // 2
        self.ahead = [(order[(p + 1) % count], order[p]) for p in range(count)]
        self.behind = [(order[p], order[(p + 1) % count]) for p in range(count)]
        self.found = [{0: a} for a in arrays]
        self.up, self.down = list(arrays), list(arrays)

    def step(self, number):
        for t in range(2):
            if number <= self.near or t == 0:
                self.up[t] = lax.ppermute(self.up[t], self.axis, self.ahead)
                self.found[t][number] = self.up[t]
            if number <= self.near or t == 1:
                self.down[t] = lax.ppermute(self.down[t], self.axis, self.behind)
                self.found[t][self.count - number] = self.down[t]

    def hold(self, value, t, number):
        if number > self.near:
            return value
        places = (number, self.count - number)
        value, *kept = lax.optimization_barrier((value, *(self.found[t][d] for d in places)))
        for d, block in zip(places, kept):
            self.found[t][d] = block
        return value

    def tie(self, value, number, which=(0, 1)):
        lists = [(self.up, t, number) for t in which if number <= self.near or t == 0]
        lists += [(self.down, t, self.count - number) for t in which if number <= self.near or t == 1]
        value, *held = lax.optimization_barrier((value, *(way[t] for way, t, _ in lists)))
        for (way, t, place), block in zip(lists, held):
            way[t] = self.found[t][place] = block
        return value

    def blocks(self, t):
        return [self.found[t][d] for d in range(self.count)]


def body(panel_u, panel_v, panel_rank, pivot_u, pivot_v, pivot_rank, orig_u, orig_v, sampler):
    order, width = panel_u.shape[2:]
    priors = panel_u.shape[1]
    pivots = pivot_u.shape[0]
    count = lax.axis_size("rows")
    cols = lax.axis_size("cols")
    pairs = cols // 2
    half, share = order // 2, order // cols
    me = lax.axis_index("cols")
    core, pair = me % 2, me // 2
    swap = [(i, i ^ 1) for i in range(cols)]

    ring = ring_order(count)
    place = np.argsort(np.array(ring))
    table = np.array([[ring[(place[r] + d) % count] for d in range(count)] for r in range(count)], np.int32)
    last = count // 2
    whole = count % 2 == 1 or last < 4 or count > RING_MOST
    if whole:
        table = np.zeros((count, 1), np.int32)
    sources = jnp.asarray(table)[lax.axis_index("rows")]
    info = jnp.concatenate([jnp.stack([core, me]).astype(jnp.int32), sources])

    panel_u, panel_v, orig_u, orig_v = panel_u[0], panel_v[0], orig_u[:, 0], orig_v[:, 0]
    square = 2 * width * width
    panel_vt, sampler_t = run(
        turn_kernel, [], [panel_v, sampler], [((priors, width, order), BF16), ((sampler.shape[1], order), BF16)], [], 12,
        10 * square * order, "turn"
    )
    (start,) = run(
        start_kernel, [info], [sampler_t, orig_u, orig_v], [((pivots, width, half), F32)], [], 12,
        pivots * square * (order + half), "start"
    )

    def shifted(x, shift):
        return lax.ppermute(x, "cols", [(i, (i + 2 * shift) % cols) for i in range(cols)])

    matrix = pltpu.VMEM((width, width), F32)
    tall = pltpu.VMEM((width, order), F32)

    def gathered(places, blocks, new_u, new_v, kept):
        new = len(places)
        shapes = [((priors, width, width), F32), ((priors, width, width), F32), ((priors, order, width), BF16)]
        first = 3 + 2 * new
        return run(
            functools.partial(gather_kernel, places, blocks), [info], [panel_vt, sampler_t, *new_u, *new_v, *kept],
            shapes, [], 20, 2 * priors * square * order * new // blocks, "gather",
            {first + n: n for n in range(len(kept))}
        )

    def taken(source, number, kept):
        places = sorted({number, count - number} | ({0} if number == 1 else set()))
        new_u, new_v = ([source.found[t][p] for p in places] for t in range(2))
        return gathered(places, count, new_u, new_v, kept)

    def updated(c, sampled, met):
        ranks = jnp.stack([panel_rank[0], pivot_rank[c]])
        return run(
            update_kernel, [info, ranks], [sampled, met, panel_u],
            [((priors, width, width), BF16), ((width, half), BF16), ((width, half), F32)],
            [], 16, 2 * priors * square * (order + width), "update"
        )

    def summed(c, give, keep, beside, outs=()):
        chip = keep + lax.ppermute(give, "cols", swap).astype(F32)
        sent = chip.astype(BF16)
        for shift in range(1, pairs):
            chip = chip + shifted(sent, shift).astype(F32)
        if beside is not None:
            chip = beside.hold(beside.hold(chip, 1, 2), 0, 3)
        chip, *outs = lax.optimization_barrier((chip, *outs))
        ymine = start[c] - chip
        yother = lax.ppermute(ymine, "cols", swap)
        return ymine, yother, outs

    finals = [((width, order), BF16), ((share, width), F32)]

    def projected(c, blocks, qt, cross, u_all):
        give, keep = run(
            functools.partial(project_kernel, blocks), [info], [qt, panel_u, cross, u_all],
            [((pairs, share, width), BF16), ((pairs, share, width), F32)],
            [pltpu.VMEM((order, width), F32)], 16, 2 * priors * square * (2 * order + width), "project"
        )
        (own,) = run(
            left_kernel, [info], [qt, orig_u[c], orig_v[c]], [((share, width), F32)], [], 8,
            square * (order + share), "left"
        )
        return give, keep, own

    def halved(give, keep, own):
        chip = keep + lax.ppermute(give, "cols", swap).astype(F32)
        total = own - lax.dynamic_index_in_dim(chip, pair, 0, False)
        sent = [
            lax.dynamic_index_in_dim(chip, (pair + shift) % pairs, 0, False).astype(BF16) for shift in range(1, pairs)
        ]
        return total, *sent

    def closed(total, *sent):
        for shift, each in enumerate(sent, 1):
            total = total - shifted(each, shift).astype(F32)
        return total

    def orthonormal(ymine, yother):
        return run(
            orthonormal_kernel, [info], [ymine, yother], finals, [tall, matrix], 12, 128 * square * order, "orthonormal"
        )

    basis, coeff = [], []
    if whole:
        for c in range(pivots):
            new_u, new_v = ([lax.all_gather(x[c], "rows", axis=1, tiled=True)] for x in (pivot_u, pivot_v))
            sampled, met, u_all = gathered([0], 1, new_u, new_v, [])
            cross, give, keep = updated(c, sampled, met)
            ymine, yother, _ = summed(c, give, keep, None)
            qt, rows = orthonormal(ymine, yother)
            basis.append(rows)
            coeff.append(closed(*halved(*projected(c, 1, qt, cross, u_all))))
    else:
        now, kept = Ring([pivot_u[0], pivot_v[0]], ring, "rows"), []
        number = 1
        parts = None
        for c in range(pivots):
            later = None
            while number <= last:
                if number == last and c + 1 < pivots:
                    later = Ring(
                        [now.hold(pivot_u[c + 1], 0, last - 2), now.hold(pivot_v[c + 1], 1, last - 2)], ring, "rows"
                    )
                    later.step(1)
                    now.up[0] = later.hold(now.up[0], 0, 1)
                    now.down[1] = later.hold(now.down[1], 1, 1)
                now.step(number)
                if c == 0 and number < last:
                    if number == 2:
                        start = now.tie(start, 2, (1,))
                    if number > 1:
                        kept[0] = now.tie(kept[0], number, (0,))
                kept = list(taken(now, number, kept))
                number += 1
            if parts is not None:
                kept[1], *parts = lax.optimization_barrier((kept[1], *parts))
            sampled, met, u_all = kept
            cross, give, keep = updated(c, sampled, met)
            kept = []
            if later is not None:
                kept = list(taken(later, 1, kept))
                later.step(2)
                give = later.tie(give, 2, (0,))
                kept[0] = later.tie(kept[0], 2, (1,))
                later.step(3)
                kept = list(taken(later, 2, kept))
            outs = projected(c - 1, count, *parts) if parts is not None and later is None else ()
            ymine, yother, outs = summed(c, give, keep, later, outs)
            if later is None:
                if outs:
                    yother, *outs = lax.optimization_barrier((yother, *halved(*outs)))
                    coeff.append(closed(*outs))
                qt, rows = orthonormal(ymine, yother)
                coeff.append(closed(*halved(*projected(c, count, qt, cross, u_all))))
            else:
                yt, work = run(
                    first_kernel, [info], [ymine, yother], [((width, order), F32), ((width, width), F32)], [matrix], 12,
                    64 * square * order, "orthonormal_first"
                )
                work = later.tie(work, 3, (1,))
                kept[0] = later.tie(kept[0], 3, (0,))
                qt, rows = run(
                    last_kernel, [info], [yt, work], finals, [tall, matrix], 12, 64 * square * order, "orthonormal_last"
                )
                kept = list(taken(later, 3, [*kept[:2], kept[2]])) if last > 3 else kept
                parts = [qt, cross, u_all]
            basis.append(rows)
            now, number = later, 4
    return (jnp.stack(basis)[:, None], jnp.stack(coeff)[:, None])


def solution(mesh):
    placed = (
        P("rows", "cols", None, None),
        P("rows", "cols", None, None),
        P("rows", "cols"),
        P(None, "cols", "rows", None),
        P(None, "cols", "rows", None),
        P(None, "cols"),
        P(None, "rows", None, None),
        P(None, "rows", None, None),
        P(),
    )
    return jax.shard_map(
        body,
        mesh=mesh,
        in_specs=placed,
        out_specs=(P(None, "rows", "cols", None), P(None, "rows", "cols", None)),
        check_vma=False,
    )
```

```python
import functools
import math

import jax
import jax.numpy as jnp
import numpy as np
from jax import lax
from jax.experimental import pallas as pl
from jax.experimental.pallas import tpu as pltpu
from jax.sharding import PartitionSpec as P

F32 = jnp.float32
BF16 = jnp.bfloat16
BLOCK = 32
GROUP = 4
SUB = 8
RING_MOST = 16
MIB = 1 << 20


def dot(a, b):
    return lax.dot_general(a, b, (((1,), (0,)), ((), ())), preferred_element_type=F32)


def dot00(a, b):
    return lax.dot_general(a, b, (((0,), (0,)), ((), ())), preferred_element_type=F32)


def dot11(a, b):
    return lax.dot_general(a, b, (((1,), (1,)), ((), ())), preferred_element_type=F32)


def split3(x):
    high = x.astype(BF16)
    rest = x - high.astype(F32)
    mid = rest.astype(BF16)
    low = (rest - mid.astype(F32)).astype(BF16)
    return high, mid, low


def reciprocal(x):
    guess = pl.reciprocal(x, approx=True)
    guess = guess * (2.0 - x * guess)
    return guess * (2.0 - x * guess)


def eliminate(panel, first):
    rows, width = panel.shape
    lanes = 128
    tile = (SUB, lanes)
    lane = lax.broadcasted_iota(jnp.int32, tile, 1)
    sub = lax.broadcasted_iota(jnp.int32, tile, 0)
    high = rows // SUB
    halves = width // lanes
    part = [
        [panel[v * SUB : (v + 1) * SUB, h * lanes : (h + 1) * lanes] for h in range(halves)]
        for v in range(high)
    ]
    mine = first // lanes
    pivots = [jnp.ones(tile, F32) for _ in range(high)]
    for k in range(0, rows, GROUP):
        at = first % lanes + k
        top, low = k // SUB, k % SUB
        inside = (lane >= at) & (lane < at + GROUP)
        column = [
            [jnp.broadcast_to(part[v][mine][:, at + m : at + m + 1], tile) for v in range(top, high)]
            for m in range(GROUP)
        ]
        small = [
            [jnp.broadcast_to(column[b][0][low + a : low + a + 1, :], tile) for b in range(a + 1)]
            for a in range(GROUP)
        ]
        row = []
        for a in range(GROUP):
            row.append([jnp.broadcast_to(part[top][h][low + a : low + a + 1, :], tile) for h in range(halves)])
            row[a][mine] = jnp.where(inside, jnp.where(lane == at + a, 1.0, 0.0), row[a][mine])
        factor = []
        for m in range(GROUP):
            inverse = reciprocal(small[m][m])
            pivots[top] = jnp.where(sub == low + m, small[m][m], pivots[top])
            for a in range(m + 1, GROUP):
                ratio = small[a][m] * inverse
                for b in range(m + 1, a + 1):
                    small[a][b] = small[a][b] - ratio * small[b][m]
                row[a] = [x - ratio * y for x, y in zip(row[a], row[m])]
            factor.append([c * inverse for c in column[m]])
            for b in range(m + 1, GROUP):
                column[b] = [c - f * small[b][m] for c, f in zip(column[b], factor[m])]
        for v in range(top, high):
            for h in range(halves):
                old = part[v][h]
                value = jnp.where(inside, 0.0, old) if h == mine else old
                for m in range(GROUP):
                    value = value - factor[m][v - top] * row[m][h]
                if v == top:
                    if low > 0:
                        value = jnp.where(sub < low, old, value)
                    for m in range(GROUP):
                        value = jnp.where(sub == low + m, row[m][h], value)
                part[v][h] = value
    done = []
    for v in range(high):
        scale = lax.rsqrt(pivots[v])
        cells = []
        for h in range(halves):
            value = part[v][h] * scale
            if h == mine:
                start = first % lanes
                value = jnp.where((lane > start + v * SUB + sub) & (lane < start + rows), 0.0, value)
            cells.append(value)
        done.append(jnp.concatenate(cells, 1))
    return jnp.concatenate(done, 0)


def invert_blocks(work, begin, end):
    width = work.shape[0]
    lane = lax.broadcasted_iota(jnp.int32, (1, width), 1)
    for first in range(begin, end, BLOCK):
        last = first + BLOCK
        panel = eliminate(work[first:last, :], first)
        work[first:last, :] = panel
        if last < width:
            base = last // 128 * 128
            high, mid, low = split3(panel)
            left = jnp.concatenate([high, high, mid, mid, high, low], 0)[:, base:]
            right = jnp.concatenate([high, mid, high, mid, low, high], 0)
            update = dot00(left, right)[last - base :, :]
            inside = (lane >= first) & (lane < last)
            work[last:, :] = jnp.where(inside, 0.0, work[last:, :]) - update


def gram_of(info, mine, other, yt, work):
    half = mine.shape[1]
    core = info[0]
    yt[:, pl.ds(pl.multiple_of(core * half, 128), half)] = mine[...]
    yt[:, pl.ds(pl.multiple_of((1 - core) * half, 128), half)] = other[...]
    high, mid, low = split3(yt[...])
    cross = dot11(high, mid) + dot11(high, low)
    work[...] = dot11(high, high) + (cross + cross.T + dot11(mid, mid))


def apply_factor(info, y, work, qt, basis, q):
    width, order = y.shape
    row = lax.broadcasted_iota(jnp.int32, (width, width), 0)
    col = lax.broadcasted_iota(jnp.int32, (width, width), 1)
    m_high, m_low, _ = split3(jnp.where(col <= row, work[...], 0.0))
    high, mid, _ = split3(y[...])
    product = dot(m_high, high) + (dot(m_high, mid) + dot(m_low, high))
    qt[...] = product.astype(BF16)
    q[...] = product
    share = basis.shape[0]
    rows = q[:, pl.ds(pl.multiple_of(info[1] * share, 128), share)]
    basis[...] = rows.T * math.sqrt(order)


def orthonormal_kernel(info, mine, other, qt, basis, yt, work):
    gram_of(info, mine, other, yt, work)
    invert_blocks(work, 0, work.shape[0])
    apply_factor(info, yt, work, qt, basis, yt)


def first_kernel(info, mine, other, yt, out, work):
    gram_of(info, mine, other, yt, work)
    invert_blocks(work, 0, work.shape[0] // 2)
    out[...] = work[...]


def last_kernel(info, y, begun, qt, basis, q, work):
    work[...] = begun[...]
    invert_blocks(work, work.shape[0] // 2, work.shape[0])
    apply_factor(info, y, work, qt, basis, q)


def gather_kernel(places, blocks, info, panel_vt, sampler_t, *refs):
    new = len(places)
    u, v = refs[:new], refs[new : 2 * new]
    kept = refs[2 * new : -3]
    sampled, met, u_all = refs[-3:]
    priors, order, width = u_all.shape
    slab = order // blocks
    spans = [pl.ds(pl.multiple_of(info[2 + p] * slab, 128), slab) for p in places]
    drawn = jnp.concatenate([sampler_t[:, span] for span in spans], 1)
    for j in range(priors):
        left = jnp.concatenate([panel_vt[j, :, span] for span in spans], 1)
        u_new = jnp.concatenate([block[j] for block in u], 0)
        v_new = jnp.concatenate([block[j] for block in v], 0)
        one, two = dot(drawn, u_new), dot(left, v_new)
        if kept:
            one, two = one + kept[0][j], two + kept[1][j]
        sampled[j] = one
        met[j] = two
        for n, p in enumerate(places):
            u_all[j, p * slab : (p + 1) * slab, :] = u_new[n * slab : (n + 1) * slab, :]


def update_kernel(info, ranks, sampled, met, panel_u, cross, give, keep):
    priors, width, _ = cross.shape
    half = keep.shape[1]
    core = info[0]
    row = lax.broadcasted_iota(jnp.int32, (width, width), 0)
    col = lax.broadcasted_iota(jnp.int32, (width, width), 1)
    terms = []
    for j in range(priors):
        inside = (row < ranks[0, j]) & (col < ranks[1, j])
        cross[j] = jnp.where(inside, met[j], 0.0).astype(BF16)
        terms.append(dot11(sampled[j].astype(BF16), cross[j]).astype(BF16))
    for out, which in ((give, 1 - core), (keep, core)):
        rows = pl.ds(pl.multiple_of(which * half, 128), half)
        total = jnp.zeros((width, half), F32)
        for j in range(priors):
            total += dot11(terms[j], panel_u[j, rows, :])
        out[...] = total.astype(out.dtype)


def project_kernel(blocks, c, info, qt, panel_u, cross, u_all, orig_u, orig_v, give, keep, own, work, u_buf, v_buf, sems):
    priors, order, width = u_all.shape
    slab = order // blocks
    pairs, share, _ = keep.shape
    core = info[0]
    fetch_u = pltpu.make_async_copy(orig_u.at[c], u_buf, sems.at[0])
    rows = pl.ds(pl.multiple_of(info[1] * share, 16), share)
    fetch_v = pltpu.make_async_copy(orig_v.at[c, rows], v_buf, sems.at[1])
    fetch_u.start()
    fetch_v.start()
    mids = []
    for j in range(priors):
        inner = dot(qt[...], panel_u[j]).astype(BF16)
        mids.append(dot(inner, cross[j]).astype(BF16))
    some = max(1, blocks // 2)
    for begin in range(0, blocks, some):
        total = jnp.zeros((some * slab, width), F32)
        for j in range(priors):
            total += dot11(u_all[j, begin * slab : (begin + some) * slab, :], mids[j])
        for n in range(some):
            rows = pl.ds(pl.multiple_of(info[2 + begin + n] * slab, SUB), slab)
            work[rows, :] = total[n * slab : (n + 1) * slab, :]
    for a in range(pairs):
        for out, which in ((give, 1 - core), (keep, core)):
            rows = pl.ds(pl.multiple_of((2 * a + which) * share, SUB), share)
            out[a] = work[rows, :].astype(out.dtype)
    fetch_u.wait()
    fetch_v.wait()
    own[...] = dot11(v_buf[...], dot(qt[...], u_buf[...]).astype(BF16))


def turn_kernel(panel_v, sampler, panel_vt, sampler_t):
    sampler_t[...] = sampler[...].T
    for j in range(panel_v.shape[0]):
        panel_vt[j] = panel_v[j].T


def start_kernel(info, sampler_t, orig_u, orig_v, out):
    half = out.shape[2]
    for c in range(out.shape[0]):
        proj = dot(sampler_t[...], orig_v[c]).astype(BF16)
        rows = pl.ds(pl.multiple_of(info[0] * half, SUB), half)
        out[c] = dot11(proj, orig_u[c, rows, :])


def run(kernel, scalars, arrays, outs, scratch, limit, flops, name, aliases={}, apart=()):
    smem = pl.BlockSpec(memory_space=pltpu.SMEM)
    vmem = pl.BlockSpec(memory_space=pltpu.VMEM)
    shapes = [jax.ShapeDtypeStruct(*o) for o in outs]
    moved = sum(a.size * a.dtype.itemsize for a in list(arrays) + shapes)
    return pl.pallas_call(
        kernel,
        out_shape=shapes,
        in_specs=[smem] * len(scalars) + [vmem] * len(arrays) + [pl.BlockSpec(memory_space=pl.ANY)] * len(apart),
        out_specs=[vmem] * len(shapes),
        scratch_shapes=scratch,
        input_output_aliases=aliases,
        compiler_params=pltpu.CompilerParams(vmem_limit_bytes=limit * MIB),
        cost_estimate=pl.CostEstimate(flops=flops, bytes_accessed=moved, transcendentals=0),
        name=name,
    )(*scalars, *arrays, *apart)


def ring_order(count):
    if count % 2:
        return list(range(count))
    return list(range(0, count, 2)) + list(range(count - 1, 0, -2))


class Ring:
    def __init__(self, arrays, order, axis):
        count = len(order)
        self.count, self.axis, self.near = count, axis, (count - 1) // 2
        self.ahead = [(order[(p + 1) % count], order[p]) for p in range(count)]
        self.behind = [(order[p], order[(p + 1) % count]) for p in range(count)]
        self.found = [{0: a} for a in arrays]
        self.up, self.down = list(arrays), list(arrays)

    def step(self, number):
        for t in range(2):
            if number <= self.near or t == 0:
                self.up[t] = lax.ppermute(self.up[t], self.axis, self.ahead)
                self.found[t][number] = self.up[t]
            if number <= self.near or t == 1:
                self.down[t] = lax.ppermute(self.down[t], self.axis, self.behind)
                self.found[t][self.count - number] = self.down[t]

    def hold(self, value, t, number):
        if number > self.near:
            return value
        places = (number, self.count - number)
        value, *kept = lax.optimization_barrier((value, *(self.found[t][d] for d in places)))
        for d, block in zip(places, kept):
            self.found[t][d] = block
        return value

    def tie(self, value, number, which=(0, 1)):
        lists = [(self.up, t, number) for t in which if number <= self.near or t == 0]
        lists += [(self.down, t, self.count - number) for t in which if number <= self.near or t == 1]
        value, *held = lax.optimization_barrier((value, *(way[t] for way, t, _ in lists)))
        for (way, t, place), block in zip(lists, held):
            way[t] = self.found[t][place] = block
        return value

    def blocks(self, t):
        return [self.found[t][d] for d in range(self.count)]


def body(panel_u, panel_v, panel_rank, pivot_u, pivot_v, pivot_rank, orig_u, orig_v, sampler):
    order, width = panel_u.shape[2:]
    priors = panel_u.shape[1]
    pivots = pivot_u.shape[0]
    count = lax.axis_size("rows")
    cols = lax.axis_size("cols")
    pairs = cols // 2
    half, share = order // 2, order // cols
    me = lax.axis_index("cols")
    core, pair = me % 2, me // 2
    swap = [(i, i ^ 1) for i in range(cols)]

    ring = ring_order(count)
    place = np.argsort(np.array(ring))
    table = np.array([[ring[(place[r] + d) % count] for d in range(count)] for r in range(count)], np.int32)
    last = count // 2
    whole = count % 2 == 1 or last < 4 or count > RING_MOST
    if whole:
        table = np.zeros((count, 1), np.int32)
    sources = jnp.asarray(table)[lax.axis_index("rows")]
    info = jnp.concatenate([jnp.stack([core, me]).astype(jnp.int32), sources])

    panel_u, panel_v, orig_u, orig_v = panel_u[0], panel_v[0], orig_u[:, 0], orig_v[:, 0]
    square = 2 * width * width
    panel_vt, sampler_t = run(
        turn_kernel, [], [panel_v, sampler], [((priors, width, order), BF16), ((sampler.shape[1], order), BF16)], [], 12,
        10 * square * order, "turn"
    )
    (start,) = run(
        start_kernel, [info], [sampler_t, orig_u, orig_v], [((pivots, width, half), F32)], [], 12,
        pivots * square * (order + half), "start"
    )

    def shifted(x, shift):
        return lax.ppermute(x, "cols", [(i, (i + 2 * shift) % cols) for i in range(cols)])

    matrix = pltpu.VMEM((width, width), F32)
    tall = pltpu.VMEM((width, order), F32)

    def gathered(places, blocks, new_u, new_v, kept):
        new = len(places)
        shapes = [((priors, width, width), F32), ((priors, width, width), F32), ((priors, order, width), BF16)]
        first = 3 + 2 * new
        return run(
            functools.partial(gather_kernel, places, blocks), [info], [panel_vt, sampler_t, *new_u, *new_v, *kept],
            shapes, [], 20, 2 * priors * square * order * new // blocks, "gather",
            {first + n: n for n in range(len(kept))}
        )

    def taken(source, number, kept):
        places = sorted({number, count - number} | ({0} if number == 1 else set()))
        new_u, new_v = ([source.found[t][p] for p in places] for t in range(2))
        return gathered(places, count, new_u, new_v, kept)

    def updated(c, sampled, met):
        ranks = jnp.stack([panel_rank[0], pivot_rank[c]])
        return run(
            update_kernel, [info, ranks], [sampled, met, panel_u],
            [((priors, width, width), BF16), ((width, half), BF16), ((width, half), F32)],
            [], 16, 2 * priors * square * (order + width), "update"
        )

    def summed(c, give, keep, beside, outs=()):
        chip = keep + lax.ppermute(give, "cols", swap).astype(F32)
        sent = chip.astype(BF16)
        for shift in range(1, pairs):
            chip = chip + shifted(sent, shift).astype(F32)
        if beside is not None:
            chip = beside.hold(beside.hold(chip, 0, 2), 1, 3)
        chip, *outs = lax.optimization_barrier((chip, *outs))
        ymine = start[c] - chip
        yother = lax.ppermute(ymine, "cols", swap)
        return ymine, yother, outs

    finals = [((width, order), BF16), ((share, width), F32)]

    def projected(c, blocks, qt, cross, u_all):
        return run(
            functools.partial(project_kernel, blocks, c), [info], [qt, panel_u, cross, u_all],
            [((pairs, share, width), BF16), ((pairs, share, width), F32), ((share, width), F32)],
            [
                pltpu.VMEM((order, width), F32), pltpu.VMEM((order, width), BF16), pltpu.VMEM((share, width), BF16),
                pltpu.SemaphoreType.DMA((2,))
            ],
            16, 2 * priors * square * (2 * order + width), "project", apart=[orig_u, orig_v]
        )

    def halved(give, keep, own):
        chip = keep + lax.ppermute(give, "cols", swap).astype(F32)
        total = own - lax.dynamic_index_in_dim(chip, pair, 0, False)
        sent = [
            lax.dynamic_index_in_dim(chip, (pair + shift) % pairs, 0, False).astype(BF16) for shift in range(1, pairs)
        ]
        return total, *sent

    def closed(total, *sent):
        for shift, each in enumerate(sent, 1):
            total = total - shifted(each, shift).astype(F32)
        return total

    def orthonormal(ymine, yother):
        return run(
            orthonormal_kernel, [info], [ymine, yother], finals, [tall, matrix], 12, 128 * square * order, "orthonormal"
        )

    basis, coeff = [], []
    if whole:
        for c in range(pivots):
            new_u, new_v = ([lax.all_gather(x[c], "rows", axis=1, tiled=True)] for x in (pivot_u, pivot_v))
            sampled, met, u_all = gathered([0], 1, new_u, new_v, [])
            cross, give, keep = updated(c, sampled, met)
            ymine, yother, _ = summed(c, give, keep, None)
            qt, rows = orthonormal(ymine, yother)
            basis.append(rows)
            coeff.append(closed(*halved(*projected(c, 1, qt, cross, u_all))))
    else:
        now, kept = Ring([pivot_u[0], pivot_v[0]], ring, "rows"), []
        number = 1
        parts = None
        for c in range(pivots):
            later = None
            while number <= last:
                if number == last and c + 1 < pivots:
                    later = Ring(
                        [now.hold(pivot_u[c + 1], 0, last - 2), now.hold(pivot_v[c + 1], 1, last - 2)], ring, "rows"
                    )
                    later.step(1)
                    now.up[0] = later.hold(now.up[0], 1, 1)
                    now.down[1] = later.hold(now.down[1], 1, 1)
                now.step(number)
                if c == 0 and number < last:
                    if number == 2:
                        start = now.tie(start, 2, (1,))
                    if number > 1:
                        kept[0] = now.tie(kept[0], number, (0,))
                kept = list(taken(now, number, kept))
                number += 1
            if parts is not None:
                kept[1], *parts = lax.optimization_barrier((kept[1], *parts))
            sampled, met, u_all = kept
            cross, give, keep = updated(c, sampled, met)
            kept = []
            if later is not None:
                kept = list(taken(later, 1, kept))
                later.step(2)
                give = later.hold(later.hold(give, 0, 1), 1, 2)
                kept[0] = later.tie(kept[0], 2, (0,))
                later.step(3)
                kept = list(taken(later, 2, kept))
            outs = projected(c - 1, count, *parts) if parts is not None and later is None else ()
            ymine, yother, outs = summed(c, give, keep, later, outs)
            if later is None:
                if outs:
                    yother, *outs = lax.optimization_barrier((yother, *halved(*outs)))
                    coeff.append(closed(*outs))
                qt, rows = orthonormal(ymine, yother)
                coeff.append(closed(*halved(*projected(c, count, qt, cross, u_all))))
            else:
                yt, work = run(
                    first_kernel, [info], [ymine, yother], [((width, order), F32), ((width, width), F32)], [matrix], 12,
                    64 * square * order, "orthonormal_first"
                )
                work = later.tie(work, 3, (0,))
                kept[0] = later.tie(kept[0], 3, (0,))
                qt, rows = run(
                    last_kernel, [info], [yt, work], finals, [tall, matrix], 12, 64 * square * order, "orthonormal_last"
                )
                kept = list(taken(later, 3, [*kept[:2], kept[2]])) if last > 3 else kept
                parts = [qt, cross, u_all]
            basis.append(rows)
            now, number = later, 4
    return (jnp.stack(basis)[:, None], jnp.stack(coeff)[:, None])


def solution(mesh):
    placed = (
        P("rows", "cols", None, None),
        P("rows", "cols", None, None),
        P("rows", "cols"),
        P(None, "cols", "rows", None),
        P(None, "cols", "rows", None),
        P(None, "cols"),
        P(None, "rows", None, None),
        P(None, "rows", None, None),
        P(),
    )
    return jax.shard_map(
        body,
        mesh=mesh,
        in_specs=placed,
        out_specs=(P(None, "rows", "cols", None), P(None, "rows", "cols", None)),
        check_vma=False,
    )
```

```python
import functools
import math

import jax
import jax.numpy as jnp
import numpy as np
from jax import lax
from jax.experimental import pallas as pl
from jax.experimental.pallas import tpu as pltpu
from jax.sharding import PartitionSpec as P

F32 = jnp.float32
BF16 = jnp.bfloat16
BLOCK = 32
GROUP = 4
SUB = 8
RING_MOST = 16
MIB = 1 << 20


def dot(a, b):
    return lax.dot_general(a, b, (((1,), (0,)), ((), ())), preferred_element_type=F32)


def dot00(a, b):
    return lax.dot_general(a, b, (((0,), (0,)), ((), ())), preferred_element_type=F32)


def dot11(a, b):
    return lax.dot_general(a, b, (((1,), (1,)), ((), ())), preferred_element_type=F32)


def split3(x):
    high = x.astype(BF16)
    rest = x - high.astype(F32)
    mid = rest.astype(BF16)
    low = (rest - mid.astype(F32)).astype(BF16)
    return high, mid, low


def reciprocal(x):
    guess = pl.reciprocal(x, approx=True)
    guess = guess * (2.0 - x * guess)
    return guess * (2.0 - x * guess)


def eliminate(panel, first):
    rows, width = panel.shape
    lanes = 128
    tile = (SUB, lanes)
    lane = lax.broadcasted_iota(jnp.int32, tile, 1)
    sub = lax.broadcasted_iota(jnp.int32, tile, 0)
    high = rows // SUB
    halves = width // lanes
    part = [
        [panel[v * SUB : (v + 1) * SUB, h * lanes : (h + 1) * lanes] for h in range(halves)]
        for v in range(high)
    ]
    mine = first // lanes
    pivots = [jnp.ones(tile, F32) for _ in range(high)]
    for k in range(0, rows, GROUP):
        at = first % lanes + k
        top, low = k // SUB, k % SUB
        inside = (lane >= at) & (lane < at + GROUP)
        column = [
            [jnp.broadcast_to(part[v][mine][:, at + m : at + m + 1], tile) for v in range(top, high)]
            for m in range(GROUP)
        ]
        small = [
            [jnp.broadcast_to(column[b][0][low + a : low + a + 1, :], tile) for b in range(a + 1)]
            for a in range(GROUP)
        ]
        row = []
        for a in range(GROUP):
            row.append([jnp.broadcast_to(part[top][h][low + a : low + a + 1, :], tile) for h in range(halves)])
            row[a][mine] = jnp.where(inside, jnp.where(lane == at + a, 1.0, 0.0), row[a][mine])
        factor = []
        for m in range(GROUP):
            inverse = reciprocal(small[m][m])
            pivots[top] = jnp.where(sub == low + m, small[m][m], pivots[top])
            for a in range(m + 1, GROUP):
                ratio = small[a][m] * inverse
                for b in range(m + 1, a + 1):
                    small[a][b] = small[a][b] - ratio * small[b][m]
                row[a] = [x - ratio * y for x, y in zip(row[a], row[m])]
            factor.append([c * inverse for c in column[m]])
            for b in range(m + 1, GROUP):
                column[b] = [c - f * small[b][m] for c, f in zip(column[b], factor[m])]
        for v in range(top, high):
            for h in range(halves):
                old = part[v][h]
                value = jnp.where(inside, 0.0, old) if h == mine else old
                for m in range(GROUP):
                    value = value - factor[m][v - top] * row[m][h]
                if v == top:
                    if low > 0:
                        value = jnp.where(sub < low, old, value)
                    for m in range(GROUP):
                        value = jnp.where(sub == low + m, row[m][h], value)
                part[v][h] = value
    done = []
    for v in range(high):
        scale = lax.rsqrt(pivots[v])
        cells = []
        for h in range(halves):
            value = part[v][h] * scale
            if h == mine:
                start = first % lanes
                value = jnp.where((lane > start + v * SUB + sub) & (lane < start + rows), 0.0, value)
            cells.append(value)
        done.append(jnp.concatenate(cells, 1))
    return jnp.concatenate(done, 0)


def invert_blocks(work, begin, end):
    width = work.shape[0]
    lane = lax.broadcasted_iota(jnp.int32, (1, width), 1)
    for first in range(begin, end, BLOCK):
        last = first + BLOCK
        panel = eliminate(work[first:last, :], first)
        work[first:last, :] = panel
        if last < width:
            base = last // 128 * 128
            high, mid, low = split3(panel)
            left = jnp.concatenate([high, high, mid, mid, high, low], 0)[:, base:]
            right = jnp.concatenate([high, mid, high, mid, low, high], 0)
            update = dot00(left, right)[last - base :, :]
            inside = (lane >= first) & (lane < last)
            work[last:, :] = jnp.where(inside, 0.0, work[last:, :]) - update


def orthonormal_kernel(sums, info, start, *refs):
    parts, (qt, basis, given, yt, work) = refs[:-5], refs[-5:]
    width, order = yt.shape
    core = info[0]
    for c in range(len(parts) // sums):
        @pl.when(core == c)
        def _():
            total = start[...]
            for part in parts[c * sums : (c + 1) * sums]:
                total = total - part[...].astype(F32)
            yt[...] = total
    high, mid, low = split3(yt[...])
    cross = dot11(high, mid) + dot11(high, low)
    work[...] = dot11(high, high) + (cross + cross.T + dot11(mid, mid))
    invert_blocks(work, 0, width)
    row = lax.broadcasted_iota(jnp.int32, (width, width), 0)
    col = lax.broadcasted_iota(jnp.int32, (width, width), 1)
    m_high, m_low, _ = split3(jnp.where(col <= row, work[...], 0.0))
    high, mid, _ = split3(yt[...])
    product = dot(m_high, high) + (dot(m_high, mid) + dot(m_low, high))
    qt[...] = product.astype(BF16)
    yt[...] = product
    share = basis.shape[0]
    for out, index in ((basis, info[1]), (given, info[1] + 1 - 2 * core)):
        rows = yt[:, pl.ds(pl.multiple_of(index * share, 128), share)]
        out[...] = rows.T * math.sqrt(order)


def gather_kernel(places, blocks, info, panel_vt, sampler_t, *refs):
    new = len(places)
    u, v = refs[:new], refs[new : 2 * new]
    kept = refs[2 * new : -3]
    sampled, met, u_all = refs[-3:]
    priors, order, width = u_all.shape
    slab = order // blocks
    spans = [pl.ds(pl.multiple_of(info[2 + p] * slab, 128), slab) for p in places]
    drawn = jnp.concatenate([sampler_t[:, span] for span in spans], 1)
    for j in range(priors):
        left = jnp.concatenate([panel_vt[j, :, span] for span in spans], 1)
        u_new = jnp.concatenate([block[j] for block in u], 0)
        v_new = jnp.concatenate([block[j] for block in v], 0)
        one, two = dot(drawn, u_new), dot(left, v_new)
        if kept:
            one, two = one + kept[0][j], two + kept[1][j]
        sampled[j] = one
        met[j] = two
        for n, p in enumerate(places):
            u_all[j, p * slab : (p + 1) * slab, :] = u_new[n * slab : (n + 1) * slab, :]


def update_kernel(info, ranks, sampled, met, panel_u, cross, give, keep):
    priors, width, _ = cross.shape
    row = lax.broadcasted_iota(jnp.int32, (width, width), 0)
    col = lax.broadcasted_iota(jnp.int32, (width, width), 1)
    terms = []
    for j in range(priors):
        inside = (row < ranks[0, j]) & (col < ranks[1, j])
        cross[j] = jnp.where(inside, met[j], 0.0).astype(BF16)
        terms.append(dot11(sampled[j].astype(BF16), cross[j]).astype(BF16))
    half = keep.shape[1] // 2
    for at in (0, half):
        total = jnp.zeros((width, half), F32)
        for j in range(priors):
            total += dot11(terms[j], panel_u[j, at : at + half, :])
        keep[:, at : at + half] = total
        give[:, at : at + half] = total.astype(BF16)


def project_kernel(blocks, own_column, info, qt, panel_u, *refs):
    give, keep, own, work, u_buf, v_buf, sems = refs[-7:]
    orig_u, orig_v = refs[-9:-7]
    pivots = (len(refs) - 9) // 2
    crosses, tall = refs[:pivots], refs[pivots : 2 * pivots]
    priors, order, width = tall[0].shape
    slab = order // blocks
    pairs, share, _ = keep.shape
    core = info[0]
    column = core if own_column else 1 - core
    rows = pl.ds(pl.multiple_of(info[1] * share, 16), share)
    fetch_u = pltpu.make_async_copy(orig_u.at[column], u_buf, sems.at[0])
    fetch_v = pltpu.make_async_copy(orig_v.at[column, rows], v_buf, sems.at[1])
    fetch_u.start()
    fetch_v.start()
    for c in range(pivots):
        @pl.when(column == c)
        def _():
            mids = []
            for j in range(priors):
                inner = dot(qt[...], panel_u[j]).astype(BF16)
                mids.append(dot(inner, crosses[c][j]).astype(BF16))
            some = max(1, blocks // 2)
            for begin in range(0, blocks, some):
                total = jnp.zeros((some * slab, width), F32)
                for j in range(priors):
                    total += dot11(tall[c][j, begin * slab : (begin + some) * slab, :], mids[j])
                for n in range(some):
                    place = pl.ds(pl.multiple_of(info[2 + begin + n] * slab, SUB), slab)
                    work[place, :] = total[n * slab : (n + 1) * slab, :]
    for a in range(pairs):
        for out, which in ((give, 1 - core), (keep, core)):
            place = pl.ds(pl.multiple_of((2 * a + which) * share, SUB), share)
            out[a] = work[place, :].astype(out.dtype)
    fetch_u.wait()
    fetch_v.wait()
    own[...] = dot11(v_buf[...], dot(qt[...], u_buf[...]).astype(BF16))


def turn_kernel(panel_v, sampler, panel_vt, sampler_t):
    sampler_t[...] = sampler[...].T
    for j in range(panel_v.shape[0]):
        panel_vt[j] = panel_v[j].T


def start_kernel(info, sampler_t, orig_u, orig_v, out):
    core = info[0]
    proj = dot(sampler_t[...], orig_v[core]).astype(BF16)
    out[...] = dot11(proj, orig_u[core])


def run(kernel, scalars, arrays, outs, scratch, limit, flops, name, aliases={}, apart=()):
    smem = pl.BlockSpec(memory_space=pltpu.SMEM)
    vmem = pl.BlockSpec(memory_space=pltpu.VMEM)
    shapes = [jax.ShapeDtypeStruct(*o) for o in outs]
    moved = sum(a.size * a.dtype.itemsize for a in list(arrays) + shapes)
    return pl.pallas_call(
        kernel,
        out_shape=shapes,
        in_specs=[smem] * len(scalars) + [vmem] * len(arrays) + [pl.BlockSpec(memory_space=pl.ANY)] * len(apart),
        out_specs=[vmem] * len(shapes),
        scratch_shapes=scratch,
        input_output_aliases=aliases,
        compiler_params=pltpu.CompilerParams(vmem_limit_bytes=limit * MIB),
        cost_estimate=pl.CostEstimate(flops=flops, bytes_accessed=moved, transcendentals=0),
        name=name,
    )(*scalars, *arrays, *apart)


def ring_order(count):
    if count % 2:
        return list(range(count))
    return list(range(0, count, 2)) + list(range(count - 1, 0, -2))


class Ring:
    def __init__(self, arrays, order, axis):
        count = len(order)
        self.count, self.axis, self.near = count, axis, (count - 1) // 2
        self.ahead = [(order[(p + 1) % count], order[p]) for p in range(count)]
        self.behind = [(order[p], order[(p + 1) % count]) for p in range(count)]
        self.found = [{0: a} for a in arrays]
        self.up, self.down = list(arrays), list(arrays)

    def step(self, number):
        for t in range(2):
            if number <= self.near or t == 0:
                self.up[t] = lax.ppermute(self.up[t], self.axis, self.ahead)
                self.found[t][number] = self.up[t]
            if number <= self.near or t == 1:
                self.down[t] = lax.ppermute(self.down[t], self.axis, self.behind)
                self.found[t][self.count - number] = self.down[t]

    def hold(self, value, t, number):
        if number > self.near:
            return value
        places = (number, self.count - number)
        value, *kept = lax.optimization_barrier((value, *(self.found[t][d] for d in places)))
        for d, block in zip(places, kept):
            self.found[t][d] = block
        return value

    def tie(self, value, number, which=(0, 1)):
        lists = [(self.up, t, number) for t in which if number <= self.near or t == 0]
        lists += [(self.down, t, self.count - number) for t in which if number <= self.near or t == 1]
        value, *held = lax.optimization_barrier((value, *(way[t] for way, t, _ in lists)))
        for (way, t, place), block in zip(lists, held):
            way[t] = self.found[t][place] = block
        return value

    def blocks(self, t):
        return [self.found[t][d] for d in range(self.count)]


def body(panel_u, panel_v, panel_rank, pivot_u, pivot_v, pivot_rank, orig_u, orig_v, sampler):
    order, width = panel_u.shape[2:]
    priors = panel_u.shape[1]
    pivots = pivot_u.shape[0]
    count = lax.axis_size("rows")
    cols = lax.axis_size("cols")
    pairs = cols // 2
    half, share = order // 2, order // cols
    me = lax.axis_index("cols")
    core, pair = me % 2, me // 2
    swap = [(i, i ^ 1) for i in range(cols)]

    ring = ring_order(count)
    place = np.argsort(np.array(ring))
    table = np.array([[ring[(place[r] + d) % count] for d in range(count)] for r in range(count)], np.int32)
    last = count // 2
    whole = count % 2 == 1 or last < 4 or count > RING_MOST
    if whole:
        table = np.zeros((count, 1), np.int32)
    sources = jnp.asarray(table)[lax.axis_index("rows")]
    info = jnp.concatenate([jnp.stack([core, me]).astype(jnp.int32), sources])

    panel_u, panel_v, orig_u, orig_v = panel_u[0], panel_v[0], orig_u[:, 0], orig_v[:, 0]
    square = 2 * width * width
    panel_vt, sampler_t = run(
        turn_kernel, [], [panel_v, sampler], [((priors, width, order), BF16), ((sampler.shape[1], order), BF16)], [], 12,
        10 * square * order, "turn"
    )
    (start,) = run(
        start_kernel, [info], [sampler_t, orig_u, orig_v], [((width, order), F32)], [], 12,
        2 * square * order, "start"
    )

    def shifted(x, shift, core_of=None):
        return lax.ppermute(
            x, "cols", [(i, (i + 2 * shift) % cols) for i in range(cols) if core_of is None or i % 2 == core_of]
        )

    matrix = pltpu.VMEM((width, width), F32)
    tall = pltpu.VMEM((width, order), F32)

    def gathered(places, blocks, new_u, new_v, kept):
        new = len(places)
        shapes = [((priors, width, width), F32), ((priors, width, width), F32), ((priors, order, width), BF16)]
        first = 3 + 2 * new
        return run(
            functools.partial(gather_kernel, places, blocks), [info], [panel_vt, sampler_t, *new_u, *new_v, *kept],
            shapes, [], 20, 2 * priors * square * order * new // blocks, "gather",
            {first + n: n for n in range(len(kept))}
        )

    def taken(source, number, kept):
        places = sorted({number, count - number} | ({0} if number == 1 else set()))
        new_u, new_v = ([source.found[t][p] for p in places] for t in range(2))
        return gathered(places, count, new_u, new_v, kept)

    def updated(c, sampled, met):
        ranks = jnp.stack([panel_rank[0], pivot_rank[c]])
        return run(
            update_kernel, [info, ranks], [sampled, met, panel_u],
            [((priors, width, width), BF16), ((width, order), BF16), ((width, order), F32)],
            [], 16, 2 * priors * square * (order + width), "update"
        )

    def met(c, give):
        return lax.ppermute(give, "cols", [(i, i ^ 1) for i in range(cols) if i % 2 != c])

    def summed(c, keep, recv):
        sent = (keep + recv.astype(F32)).astype(BF16)
        return [shifted(sent, shift, c) for shift in range(1, pairs)]

    def projected(own_column, blocks, qt, crosses, u_alls):
        return run(
            functools.partial(project_kernel, blocks, own_column), [info], [qt, panel_u, *crosses, *u_alls],
            [((pairs, share, width), BF16), ((pairs, share, width), F32), ((share, width), F32)],
            [
                pltpu.VMEM((order, width), F32), pltpu.VMEM((order, width), BF16), pltpu.VMEM((share, width), BF16),
                pltpu.SemaphoreType.DMA((2,))
            ],
            20, 3 * priors * square * (2 * order + width), "project", apart=[orig_u, orig_v]
        )

    def placed(mine, other):
        return jnp.where(core == 0, jnp.stack([mine, other]), jnp.stack([other, mine]))

    crosses, u_alls, sums = [], [], []
    if whole:
        for c in range(pivots):
            new_u, new_v = ([lax.all_gather(x[c], "rows", axis=1, tiled=True)] for x in (pivot_u, pivot_v))
            sampled, cross, u_all = gathered([0], 1, new_u, new_v, [])
            cross, give, keep = updated(c, sampled, cross)
            recv = met(c, give)
            crosses.append(cross)
            u_alls.append(u_all)
            sums.append([keep, recv, *summed(c, keep, recv)])
    else:
        now, kept = Ring([pivot_u[0], pivot_v[0]], ring, "rows"), []
        number = 1
        for c in range(pivots):
            later = None
            while number <= last:
                if number == last and c + 1 < pivots:
                    later = Ring(
                        [now.hold(pivot_u[c + 1], 0, last - 2), now.hold(pivot_v[c + 1], 1, last - 2)], ring, "rows"
                    )
                    later.step(1)
                    now.up[0] = later.hold(now.up[0], 1, 1)
                    now.down[1] = later.hold(now.down[1], 1, 1)
                now.step(number)
                if number < last:
                    if number == 2 and c == 0:
                        start = now.tie(start, 2, (1,))
                    if number > 1:
                        kept[0] = now.tie(kept[0], number, (0,))
                kept = list(taken(now, number, kept))
                number += 1
            if sums:
                kept[1], *sums[0][1:] = lax.optimization_barrier((kept[1], *sums[0][1:]))
            sampled, cross, u_all = kept
            cross, give, keep = updated(c, sampled, cross)
            if later is not None:
                give = later.tie(give, 1, (0,))
                later.step(2)
                give = later.hold(give, 1, 2)
                kept = list(taken(later, 1, []))
            recv = met(c, give)
            if later is not None:
                recv = later.tie(recv, 2, (0,))
                kept[0] = later.tie(kept[0], 2, (0,))
                later.step(3)
                recv = later.hold(recv, 1, 3)
                kept = list(taken(later, 2, kept))
            others = summed(c, keep, recv)
            if later is not None:
                others[0] = later.tie(others[0], 3, (0,))
                kept[0] = later.tie(kept[0], 3, (1,))
                kept = list(taken(later, 3, kept))
                later.step(4)
                kept = list(taken(later, 4, kept))
            crosses.append(cross)
            u_alls.append(u_all)
            sums.append([keep, recv, *others])
            now, number = later, 5
    blocks = 1 if whole else count
    qt, rows, given = run(
        functools.partial(orthonormal_kernel, len(sums[0])), [info], [start, *(x for each in sums for x in each)],
        [((width, order), BF16), ((share, width), F32), ((share, width), F32)], [tall, matrix], 16,
        128 * square * order, "orthonormal"
    )
    qt_other = lax.ppermute(qt, "cols", swap)
    rows_other = lax.ppermute(given, "cols", swap)
    give_a, keep_a, own_a = projected(True, blocks, qt, crosses, u_alls)
    qt_other, give_a, keep_a, own_a = lax.optimization_barrier((qt_other, give_a, keep_a, own_a))
    give_b, keep_b, own_b = projected(False, blocks, qt_other, crosses, u_alls)
    results = []
    for keep, own, give in ((keep_b, own_b, give_a), (keep_a, own_a, give_b)):
        chip = keep + lax.ppermute(give, "cols", swap).astype(F32)
        total = own - lax.dynamic_index_in_dim(chip, pair, 0, False)
        for shift in range(1, pairs):
            sent = lax.dynamic_index_in_dim(chip, (pair + shift) % pairs, 0, False).astype(BF16)
            total = total - shifted(sent, shift).astype(F32)
        results.append(total)
    basis, coeff = placed(rows, rows_other), placed(results[1], results[0])
    return (basis[:, None], coeff[:, None])


def solution(mesh):
    placed = (
        P("rows", "cols", None, None),
        P("rows", "cols", None, None),
        P("rows", "cols"),
        P(None, "cols", "rows", None),
        P(None, "cols", "rows", None),
        P(None, "cols"),
        P(None, "rows", None, None),
        P(None, "rows", None, None),
        P(),
    )
    return jax.shard_map(
        body,
        mesh=mesh,
        in_specs=placed,
        out_specs=(P(None, "rows", "cols", None), P(None, "rows", "cols", None)),
        check_vma=False,
    )
```

```python
import functools
import math

import jax
import jax.numpy as jnp
import numpy as np
from jax import lax
from jax.experimental import pallas as pl
from jax.experimental.pallas import tpu as pltpu
from jax.sharding import PartitionSpec as P

F32 = jnp.float32
BF16 = jnp.bfloat16
BLOCK = 32
GROUP = 4
SUB = 8
RING_MOST = 16
MIB = 1 << 20


def dot(a, b):
    return lax.dot_general(a, b, (((1,), (0,)), ((), ())), preferred_element_type=F32)


def dot00(a, b):
    return lax.dot_general(a, b, (((0,), (0,)), ((), ())), preferred_element_type=F32)


def dot11(a, b):
    return lax.dot_general(a, b, (((1,), (1,)), ((), ())), preferred_element_type=F32)


def split3(x):
    high = x.astype(BF16)
    rest = x - high.astype(F32)
    mid = rest.astype(BF16)
    low = (rest - mid.astype(F32)).astype(BF16)
    return high, mid, low


def reciprocal(x):
    guess = pl.reciprocal(x, approx=True)
    guess = guess * (2.0 - x * guess)
    return guess * (2.0 - x * guess)


def eliminate(panel, first):
    rows, width = panel.shape
    lanes = 128
    tile = (SUB, lanes)
    lane = lax.broadcasted_iota(jnp.int32, tile, 1)
    sub = lax.broadcasted_iota(jnp.int32, tile, 0)
    high = rows // SUB
    halves = width // lanes
    part = [
        [panel[v * SUB : (v + 1) * SUB, h * lanes : (h + 1) * lanes] for h in range(halves)]
        for v in range(high)
    ]
    mine = first // lanes
    pivots = [jnp.ones(tile, F32) for _ in range(high)]
    for k in range(0, rows, GROUP):
        at = first % lanes + k
        top, low = k // SUB, k % SUB
        inside = (lane >= at) & (lane < at + GROUP)
        column = [
            [jnp.broadcast_to(part[v][mine][:, at + m : at + m + 1], tile) for v in range(top, high)]
            for m in range(GROUP)
        ]
        small = [
            [jnp.broadcast_to(column[b][0][low + a : low + a + 1, :], tile) for b in range(a + 1)]
            for a in range(GROUP)
        ]
        row = []
        for a in range(GROUP):
            row.append([jnp.broadcast_to(part[top][h][low + a : low + a + 1, :], tile) for h in range(halves)])
            row[a][mine] = jnp.where(inside, jnp.where(lane == at + a, 1.0, 0.0), row[a][mine])
        factor = []
        for m in range(GROUP):
            inverse = reciprocal(small[m][m])
            pivots[top] = jnp.where(sub == low + m, small[m][m], pivots[top])
            for a in range(m + 1, GROUP):
                ratio = small[a][m] * inverse
                for b in range(m + 1, a + 1):
                    small[a][b] = small[a][b] - ratio * small[b][m]
                row[a] = [x - ratio * y for x, y in zip(row[a], row[m])]
            factor.append([c * inverse for c in column[m]])
            for b in range(m + 1, GROUP):
                column[b] = [c - f * small[b][m] for c, f in zip(column[b], factor[m])]
        for v in range(top, high):
            for h in range(halves):
                old = part[v][h]
                value = jnp.where(inside, 0.0, old) if h == mine else old
                for m in range(GROUP):
                    value = value - factor[m][v - top] * row[m][h]
                if v == top:
                    if low > 0:
                        value = jnp.where(sub < low, old, value)
                    for m in range(GROUP):
                        value = jnp.where(sub == low + m, row[m][h], value)
                part[v][h] = value
    done = []
    for v in range(high):
        scale = lax.rsqrt(pivots[v])
        cells = []
        for h in range(halves):
            value = part[v][h] * scale
            if h == mine:
                start = first % lanes
                value = jnp.where((lane > start + v * SUB + sub) & (lane < start + rows), 0.0, value)
            cells.append(value)
        done.append(jnp.concatenate(cells, 1))
    return jnp.concatenate(done, 0)


def invert_blocks(work, begin, end):
    width = work.shape[0]
    lane = lax.broadcasted_iota(jnp.int32, (1, width), 1)
    for first in range(begin, end, BLOCK):
        last = first + BLOCK
        panel = eliminate(work[first:last, :], first)
        work[first:last, :] = panel
        if last < width:
            base = last // 128 * 128
            high, mid, low = split3(panel)
            left = jnp.concatenate([high, high, mid, mid, high, low], 0)[:, base:]
            right = jnp.concatenate([high, mid, high, mid, low, high], 0)
            update = dot00(left, right)[last - base :, :]
            inside = (lane >= first) & (lane < last)
            work[last:, :] = jnp.where(inside, 0.0, work[last:, :]) - update


def orthonormal_kernel(info, start, *refs):
    parts, (qt, basis, given, yt, work) = refs[:-5], refs[-5:]
    width, order = yt.shape
    core = info[0]
    total = start[...]
    for part in parts:
        total = total - part[...].astype(F32)
    yt[...] = total
    high, mid, low = split3(yt[...])
    cross = dot11(high, mid) + dot11(high, low)
    work[...] = dot11(high, high) + (cross + cross.T + dot11(mid, mid))
    invert_blocks(work, 0, width)
    row = lax.broadcasted_iota(jnp.int32, (width, width), 0)
    col = lax.broadcasted_iota(jnp.int32, (width, width), 1)
    m_high, m_low, _ = split3(jnp.where(col <= row, work[...], 0.0))
    high, mid, _ = split3(yt[...])
    product = dot(m_high, high) + (dot(m_high, mid) + dot(m_low, high))
    qt[...] = product.astype(BF16)
    yt[...] = product
    share = basis.shape[0]
    for out, index in ((basis, info[1]), (given, info[1] + 1 - 2 * core)):
        rows = yt[:, pl.ds(pl.multiple_of(index * share, 128), share)]
        out[...] = rows.T * math.sqrt(order)


def gather_kernel(places, blocks, info, panel_vt, sampler_t, *refs):
    new = len(places)
    u, v = refs[:new], refs[new : 2 * new]
    kept = refs[2 * new : -3]
    sampled, met, u_all = refs[-3:]
    pivots, priors, order, width = u_all.shape
    slab = order // blocks
    spans = [pl.ds(pl.multiple_of(info[2 + p] * slab, 128), slab) for p in places]
    drawn = jnp.concatenate([sampler_t[:, span] for span in spans], 1)
    for j in range(priors):
        left = jnp.concatenate([panel_vt[j, :, span] for span in spans], 1)
        for c in range(pivots):
            u_new = jnp.concatenate([block[c, j] for block in u], 0)
            v_new = jnp.concatenate([block[c, j] for block in v], 0)
            one, two = dot(drawn, u_new), dot(left, v_new)
            if kept:
                one, two = one + kept[0][c, j], two + kept[1][c, j]
            sampled[c, j] = one
            met[c, j] = two
            for n, p in enumerate(places):
                u_all[c, j, p * slab : (p + 1) * slab, :] = u_new[n * slab : (n + 1) * slab, :]


def update_kernel(own_column, info, panel_rank, pivot_rank, sampled, met, panel_u, cross, out):
    priors, width, _ = cross.shape
    column = info[0] if own_column else 1 - info[0]
    row = lax.broadcasted_iota(jnp.int32, (width, width), 0)
    col = lax.broadcasted_iota(jnp.int32, (width, width), 1)
    terms = []
    for j in range(priors):
        inside = (row < panel_rank[0, j]) & (col < pivot_rank[column, j])
        cross[j] = jnp.where(inside, met[column, j], 0.0).astype(BF16)
        terms.append(dot11(sampled[column, j].astype(BF16), cross[j]).astype(BF16))
    half = out.shape[1] // 2
    for at in (0, half):
        total = jnp.zeros((width, half), F32)
        for j in range(priors):
            total += dot11(terms[j], panel_u[j, at : at + half, :])
        out[:, at : at + half] = total.astype(out.dtype)


def project_kernel(blocks, own_column, info, qt, panel_u, cross, u_all, orig_u, orig_v, give, keep, own, work, u_buf, v_buf, sems):
    _, priors, order, width = u_all.shape
    slab = order // blocks
    pairs, share, _ = keep.shape
    core = info[0]
    column = core if own_column else 1 - core
    rows = pl.ds(pl.multiple_of(info[1] * share, 16), share)
    fetch_u = pltpu.make_async_copy(orig_u.at[column], u_buf, sems.at[0])
    fetch_v = pltpu.make_async_copy(orig_v.at[column, rows], v_buf, sems.at[1])
    fetch_u.start()
    fetch_v.start()
    mids = []
    for j in range(priors):
        inner = dot(qt[...], panel_u[j]).astype(BF16)
        mids.append(dot(inner, cross[j]).astype(BF16))
    some = max(1, blocks // 2)
    for begin in range(0, blocks, some):
        total = jnp.zeros((some * slab, width), F32)
        for j in range(priors):
            total += dot11(u_all[column, j, begin * slab : (begin + some) * slab, :], mids[j])
        for n in range(some):
            place = pl.ds(pl.multiple_of(info[2 + begin + n] * slab, SUB), slab)
            work[place, :] = total[n * slab : (n + 1) * slab, :]
    for a in range(pairs):
        for out, which in ((give, 1 - core), (keep, core)):
            place = pl.ds(pl.multiple_of((2 * a + which) * share, SUB), share)
            out[a] = work[place, :].astype(out.dtype)
    fetch_u.wait()
    fetch_v.wait()
    own[...] = dot11(v_buf[...], dot(qt[...], u_buf[...]).astype(BF16))


def turn_kernel(panel_v, sampler, panel_vt, sampler_t):
    sampler_t[...] = sampler[...].T
    for j in range(panel_v.shape[0]):
        panel_vt[j] = panel_v[j].T


def start_kernel(info, sampler_t, orig_u, orig_v, out):
    core = info[0]
    proj = dot(sampler_t[...], orig_v[core]).astype(BF16)
    out[...] = dot11(proj, orig_u[core])


def run(kernel, scalars, arrays, outs, scratch, limit, flops, name, aliases={}, apart=()):
    smem = pl.BlockSpec(memory_space=pltpu.SMEM)
    vmem = pl.BlockSpec(memory_space=pltpu.VMEM)
    shapes = [jax.ShapeDtypeStruct(*o) for o in outs]
    moved = sum(a.size * a.dtype.itemsize for a in list(arrays) + shapes)
    return pl.pallas_call(
        kernel,
        out_shape=shapes,
        in_specs=[smem] * len(scalars) + [vmem] * len(arrays) + [pl.BlockSpec(memory_space=pl.ANY)] * len(apart),
        out_specs=[vmem] * len(shapes),
        scratch_shapes=scratch,
        input_output_aliases=aliases,
        compiler_params=pltpu.CompilerParams(vmem_limit_bytes=limit * MIB),
        cost_estimate=pl.CostEstimate(flops=flops, bytes_accessed=moved, transcendentals=0),
        name=name,
    )(*scalars, *arrays, *apart)


def ring_order(count):
    if count % 2:
        return list(range(count))
    return list(range(0, count, 2)) + list(range(count - 1, 0, -2))


class Ring:
    def __init__(self, arrays, order, axis):
        count = len(order)
        self.count, self.axis, self.near = count, axis, (count - 1) // 2
        self.ahead = [(order[(p + 1) % count], order[p]) for p in range(count)]
        self.behind = [(order[p], order[(p + 1) % count]) for p in range(count)]
        self.found = [{0: a} for a in arrays]
        self.up, self.down = list(arrays), list(arrays)

    def step(self, number):
        for t in range(2):
            if number <= self.near or t == 0:
                self.up[t] = lax.ppermute(self.up[t], self.axis, self.ahead)
                self.found[t][number] = self.up[t]
            if number <= self.near or t == 1:
                self.down[t] = lax.ppermute(self.down[t], self.axis, self.behind)
                self.found[t][self.count - number] = self.down[t]

    def hold(self, value, t, number):
        if number > self.near:
            return value
        places = (number, self.count - number)
        value, *kept = lax.optimization_barrier((value, *(self.found[t][d] for d in places)))
        for d, block in zip(places, kept):
            self.found[t][d] = block
        return value

    def tie(self, value, number, which=(0, 1)):
        lists = [(self.up, t, number) for t in which if number <= self.near or t == 0]
        lists += [(self.down, t, self.count - number) for t in which if number <= self.near or t == 1]
        value, *held = lax.optimization_barrier((value, *(way[t] for way, t, _ in lists)))
        for (way, t, place), block in zip(lists, held):
            way[t] = self.found[t][place] = block
        return value

    def blocks(self, t):
        return [self.found[t][d] for d in range(self.count)]


def body(panel_u, panel_v, panel_rank, pivot_u, pivot_v, pivot_rank, orig_u, orig_v, sampler):
    order, width = panel_u.shape[2:]
    priors = panel_u.shape[1]
    pivots = pivot_u.shape[0]
    count = lax.axis_size("rows")
    cols = lax.axis_size("cols")
    pairs = cols // 2
    half, share = order // 2, order // cols
    me = lax.axis_index("cols")
    core, pair = me % 2, me // 2
    swap = [(i, i ^ 1) for i in range(cols)]

    ring = ring_order(count)
    place = np.argsort(np.array(ring))
    table = np.array([[ring[(place[r] + d) % count] for d in range(count)] for r in range(count)], np.int32)
    last = count // 2
    whole = count % 2 == 1 or last < 4 or count > RING_MOST
    if whole:
        table = np.zeros((count, 1), np.int32)
    sources = jnp.asarray(table)[lax.axis_index("rows")]
    info = jnp.concatenate([jnp.stack([core, me]).astype(jnp.int32), sources])

    panel_u, panel_v, orig_u, orig_v = panel_u[0], panel_v[0], orig_u[:, 0], orig_v[:, 0]
    square = 2 * width * width
    panel_vt, sampler_t = run(
        turn_kernel, [], [panel_v, sampler], [((priors, width, order), BF16), ((sampler.shape[1], order), BF16)], [], 12,
        10 * square * order, "turn"
    )
    (start,) = run(
        start_kernel, [info], [sampler_t, orig_u, orig_v], [((width, order), F32)], [], 12,
        2 * square * order, "start"
    )

    def shifted(x, shift):
        return lax.ppermute(x, "cols", [(i, (i + 2 * shift) % cols) for i in range(cols)])

    matrix = pltpu.VMEM((width, width), F32)
    tall = pltpu.VMEM((width, order), F32)

    def gathered(places, blocks, new_u, new_v, kept):
        new = len(places)
        shapes = [
            ((pivots, priors, width, width), F32), ((pivots, priors, width, width), F32),
            ((pivots, priors, order, width), BF16)
        ]
        first = 3 + 2 * new
        return run(
            functools.partial(gather_kernel, places, blocks), [info], [panel_vt, sampler_t, *new_u, *new_v, *kept],
            shapes, [], 28, 2 * pivots * priors * square * order * new // blocks, "gather",
            {first + n: n for n in range(len(kept))}
        )

    def updated(own_column, sampled, met):
        return run(
            functools.partial(update_kernel, own_column), [info, panel_rank, pivot_rank], [sampled, met, panel_u],
            [((priors, width, width), BF16), ((width, order), F32 if own_column else BF16)], [], 16,
            2 * priors * square * (order + width), "update"
        )

    def projected(own_column, blocks, qt, cross, u_all):
        return run(
            functools.partial(project_kernel, blocks, own_column), [info], [qt, panel_u, cross, u_all],
            [((pairs, share, width), BF16), ((pairs, share, width), F32), ((share, width), F32)],
            [
                pltpu.VMEM((order, width), F32), pltpu.VMEM((order, width), BF16), pltpu.VMEM((share, width), BF16),
                pltpu.SemaphoreType.DMA((2,))
            ],
            20, 3 * priors * square * (2 * order + width), "project", apart=[orig_u, orig_v]
        )

    def placed(mine, other):
        return jnp.where(core == 0, jnp.stack([mine, other]), jnp.stack([other, mine]))

    if whole:
        blocks = 1
        new_u, new_v = ([lax.all_gather(x, "rows", axis=2, tiled=True)] for x in (pivot_u, pivot_v))
        sampled, met, u_all = gathered([0], 1, new_u, new_v, [])
    else:
        blocks = count
        now, kept = Ring([pivot_u, pivot_v], ring, "rows"), []
        for number in range(1, last + 1):
            now.step(number)
            if 1 < number < last:
                kept[0] = now.tie(kept[0], number, (0,))
                if number == 2:
                    start = now.tie(start, number, (1,))
            places = sorted({number, count - number} | ({0} if number == 1 else set()))
            new_u, new_v = ([now.found[t][p] for p in places] for t in range(2))
            kept = list(gathered(places, count, new_u, new_v, kept))
        sampled, met, u_all = kept
    cross_other, give = updated(False, sampled, met)
    recv = lax.ppermute(give, "cols", swap)
    cross_own, keep = updated(True, sampled, met)
    sent = (keep + recv.astype(F32)).astype(BF16)
    parts = [keep, recv, *(shifted(sent, shift) for shift in range(1, pairs))]
    qt, rows, given = run(
        orthonormal_kernel, [info], [start, *parts],
        [((width, order), BF16), ((share, width), F32), ((share, width), F32)], [tall, matrix], 16,
        128 * square * order, "orthonormal"
    )
    qt_other = lax.ppermute(qt, "cols", swap)
    rows_other = lax.ppermute(given, "cols", swap)
    give_a, keep_a, own_a = projected(True, blocks, qt, cross_own, u_all)
    qt_other, give_a, keep_a, own_a = lax.optimization_barrier((qt_other, give_a, keep_a, own_a))
    give_b, keep_b, own_b = projected(False, blocks, qt_other, cross_other, u_all)
    results = []
    for keep, own, give in ((keep_b, own_b, give_a), (keep_a, own_a, give_b)):
        chip = keep + lax.ppermute(give, "cols", swap).astype(F32)
        total = own - lax.dynamic_index_in_dim(chip, pair, 0, False)
        for shift in range(1, pairs):
            sent = lax.dynamic_index_in_dim(chip, (pair + shift) % pairs, 0, False).astype(BF16)
            total = total - shifted(sent, shift).astype(F32)
        results.append(total)
    basis, coeff = placed(rows, rows_other), placed(results[1], results[0])
    return (basis[:, None], coeff[:, None])


def solution(mesh):
    placed = (
        P("rows", "cols", None, None),
        P("rows", "cols", None, None),
        P("rows", "cols"),
        P(None, "cols", "rows", None),
        P(None, "cols", "rows", None),
        P(None, "cols"),
        P(None, "rows", None, None),
        P(None, "rows", None, None),
        P(),
    )
    return jax.shard_map(
        body,
        mesh=mesh,
        in_specs=placed,
        out_specs=(P(None, "rows", "cols", None), P(None, "rows", "cols", None)),
        check_vma=False,
    )
```

```python
import functools
import math

import jax
import jax.numpy as jnp
import numpy as np
from jax import lax
from jax.experimental import pallas as pl
from jax.experimental.pallas import tpu as pltpu
from jax.sharding import PartitionSpec as P

F32 = jnp.float32
BF16 = jnp.bfloat16
BLOCK = 32
SUB = 8
RING_MOST = 16
MIB = 1 << 20


def dot(a, b):
    return lax.dot_general(a, b, (((1,), (0,)), ((), ())), preferred_element_type=F32)


def dot00(a, b):
    return lax.dot_general(a, b, (((0,), (0,)), ((), ())), preferred_element_type=F32)


def dot11(a, b):
    return lax.dot_general(a, b, (((1,), (1,)), ((), ())), preferred_element_type=F32)


def split3(x):
    high = x.astype(BF16)
    rest = x - high.astype(F32)
    mid = rest.astype(BF16)
    low = (rest - mid.astype(F32)).astype(BF16)
    return high, mid, low


def eliminate(panel, first):
    rows, width = panel.shape
    lanes = 128
    tile = (SUB, lanes)
    lane = lax.broadcasted_iota(jnp.int32, tile, 1)
    sub = lax.broadcasted_iota(jnp.int32, tile, 0)
    high = rows // SUB
    halves = width // lanes
    part = [
        [panel[v * SUB : (v + 1) * SUB, h * lanes : (h + 1) * lanes] for h in range(halves)]
        for v in range(high)
    ]
    mine, start = first // lanes, first % lanes
    scales = []
    for top in range(high):
        at = start + top * SUB
        inside = (lane >= at) & (lane < at + SUB)
        column = [
            [jnp.broadcast_to(part[v][mine][:, at + m : at + m + 1], tile) for v in range(top, high)]
            for m in range(SUB)
        ]
        small = [
            [jnp.broadcast_to(column[b][0][a : a + 1, :], tile) for b in range(a + 1)] for a in range(SUB)
        ]
        row = []
        for a in range(SUB):
            row.append([jnp.broadcast_to(part[top][h][a : a + 1, :], tile) for h in range(halves)])
            row[a][mine] = jnp.where(inside, jnp.where(lane == at + a, 1.0, 0.0), row[a][mine])
        pivots = small[0][0]
        factor = []
        for m in range(SUB):
            inverse = pl.reciprocal(small[m][m], approx=True)
            if m:
                pivots = jnp.where(sub == m, small[m][m], pivots)
            for a in range(m + 1, SUB):
                ratio = small[a][m] * inverse
                for b in range(m + 1, a + 1):
                    small[a][b] = small[a][b] - ratio * small[b][m]
                row[a] = [x - ratio * y for x, y in zip(row[a], row[m])]
            factor.append([c * inverse for c in column[m][1:]])
            for b in range(m + 1, SUB):
                column[b][1:] = [c - f * small[b][m] for c, f in zip(column[b][1:], factor[m])]
        for v in range(top + 1, high):
            for h in range(halves):
                value = jnp.where(inside, 0.0, part[v][h]) if h == mine else part[v][h]
                for m in range(SUB):
                    value = value - factor[m][v - top - 1] * row[m][h]
                part[v][h] = value
        for h in range(halves):
            value = row[0][h]
            for m in range(1, SUB):
                value = jnp.where(sub == m, row[m][h], value)
            part[top][h] = value
        scales.append(lax.rsqrt(pivots))
    done = []
    for v in range(high):
        cells = []
        for h in range(halves):
            value = part[v][h] * scales[v]
            if h == mine:
                value = jnp.where((lane > start + v * SUB + sub) & (lane < start + rows), 0.0, value)
            cells.append(value)
        done.append(jnp.concatenate(cells, 1))
    return jnp.concatenate(done, 0)


def invert_blocks(work, begin, end):
    width = work.shape[0]
    lane = lax.broadcasted_iota(jnp.int32, (1, width), 1)
    for first in range(begin, end, BLOCK):
        last = first + BLOCK
        panel = eliminate(work[first:last, :], first)
        work[first:last, :] = panel
        if last < width:
            base = last // 128 * 128
            high, mid, low = split3(panel)
            left = jnp.concatenate([high, high, mid, mid, high, low], 0)[:, base:]
            right = jnp.concatenate([high, mid, high, mid, low, high], 0)
            update = dot00(left, right)[last - base :, :]
            inside = (lane >= first) & (lane < last)
            work[last:, :] = jnp.where(inside, 0.0, work[last:, :]) - update


def orthonormal_kernel(info, start, *refs):
    parts, (qt, basis, given, yt, work) = refs[:-5], refs[-5:]
    width, order = yt.shape
    core = info[0]
    total = start[...]
    for part in parts:
        total = total - part[...].astype(F32)
    yt[...] = total
    high, mid, low = split3(yt[...])
    cross = dot11(high, mid) + dot11(high, low)
    work[...] = dot11(high, high) + (cross + cross.T + dot11(mid, mid))
    invert_blocks(work, 0, width)
    row = lax.broadcasted_iota(jnp.int32, (width, width), 0)
    col = lax.broadcasted_iota(jnp.int32, (width, width), 1)
    m_high, m_low, _ = split3(jnp.where(col <= row, work[...], 0.0))
    high, mid, _ = split3(yt[...])
    product = dot(m_high, high) + (dot(m_high, mid) + dot(m_low, high))
    qt[...] = product.astype(BF16)
    yt[...] = product
    share = basis.shape[0]
    for out, index in ((basis, info[1]), (given, info[1] + 1 - 2 * core)):
        rows = yt[:, pl.ds(pl.multiple_of(index * share, 128), share)]
        out[...] = rows.T * math.sqrt(order)


def gather_kernel(places, blocks, info, panel_vt, sampler_t, *refs):
    new = len(places)
    u, v = refs[:new], refs[new : 2 * new]
    kept = refs[2 * new : -3]
    sampled, met, u_all = refs[-3:]
    pivots, priors, order, width = u_all.shape
    slab = order // blocks
    spans = [pl.ds(pl.multiple_of(info[2 + p] * slab, 128), slab) for p in places]
    drawn = jnp.concatenate([sampler_t[:, span] for span in spans], 1)
    for j in range(priors):
        left = jnp.concatenate([panel_vt[j, :, span] for span in spans], 1)
        for c in range(pivots):
            u_new = jnp.concatenate([block[c, j] for block in u], 0)
            v_new = jnp.concatenate([block[c, j] for block in v], 0)
            one, two = dot(drawn, u_new), dot(left, v_new)
            if kept:
                one, two = one + kept[0][c, j], two + kept[1][c, j]
            sampled[c, j] = one
            met[c, j] = two
            for n, p in enumerate(places):
                u_all[c, j, p * slab : (p + 1) * slab, :] = u_new[n * slab : (n + 1) * slab, :]


def update_kernel(own_column, places, blocks, info, panel_rank, pivot_rank, sampled, met, panel_u, panel_vt, sampler_t, *refs):
    cross, out = refs[-2:]
    priors, width, _ = cross.shape
    slab = panel_vt.shape[2] // blocks
    column = info[0] if own_column else 1 - info[0]
    row = lax.broadcasted_iota(jnp.int32, (width, width), 0)
    col = lax.broadcasted_iota(jnp.int32, (width, width), 1)
    terms = []
    for j in range(priors):
        one, two = sampled[column, j], met[column, j]
        for n, place in enumerate(places):
            span = pl.ds(pl.multiple_of(info[2 + place] * slab, 128), slab)
            one += dot(sampler_t[:, span], refs[n][column, j])
            two += dot(panel_vt[j, :, span], refs[len(places) + n][column, j])
        inside = (row < panel_rank[0, j]) & (col < pivot_rank[column, j])
        cross[j] = jnp.where(inside, two, 0.0).astype(BF16)
        terms.append(dot11(one.astype(BF16), cross[j]).astype(BF16))
    half = out.shape[1] // 2
    for at in (0, half):
        total = jnp.zeros((width, half), F32)
        for j in range(priors):
            total += dot11(terms[j], panel_u[j, at : at + half, :])
        out[:, at : at + half] = total.astype(out.dtype)


def project_kernel(places, blocks, own_column, info, qt, panel_u, cross, u_all, *refs):
    give, keep, work = refs[-3:]
    _, priors, order, width = u_all.shape
    slab = order // blocks
    pairs, share, _ = keep.shape
    core = info[0]
    column = core if own_column else 1 - core
    mids = []
    for j in range(priors):
        inner = dot(qt[...], panel_u[j]).astype(BF16)
        mids.append(dot(inner, cross[j]).astype(BF16))

    def rows_of(j, b):
        if b in places:
            return refs[places.index(b)][column, j]
        return u_all[column, j, b * slab : (b + 1) * slab, :]

    some = max(1, blocks // 2)
    for begin in range(0, blocks, some):
        total = jnp.zeros((some * slab, width), F32)
        for j in range(priors):
            total += dot11(jnp.concatenate([rows_of(j, begin + n) for n in range(some)], 0), mids[j])
        for n in range(some):
            place = pl.ds(pl.multiple_of(info[2 + begin + n] * slab, SUB), slab)
            work[place, :] = total[n * slab : (n + 1) * slab, :]
    for a in range(pairs):
        for out, which in ((give, 1 - core), (keep, core)):
            place = pl.ds(pl.multiple_of((2 * a + which) * share, SUB), share)
            out[a] = work[place, :].astype(out.dtype)


def own_kernel(info, qt, qt_other, orig_u, orig_v, out, u_buf, v_buf, sems):
    share = out.shape[1]
    rows = pl.ds(pl.multiple_of(info[1] * share, 16), share)
    copies = []
    for n, column in enumerate((1 - info[0], info[0])):
        copies.append(pltpu.make_async_copy(orig_u.at[column], u_buf.at[n], sems.at[2 * n]))
        copies.append(pltpu.make_async_copy(orig_v.at[column, rows], v_buf.at[n], sems.at[2 * n + 1]))
    for copy in copies:
        copy.start()
    for n, q in enumerate((qt_other, qt)):
        copies[2 * n].wait()
        copies[2 * n + 1].wait()
        out[n] = dot11(v_buf[n], dot(q[...], u_buf[n]).astype(BF16))


def halve_kernel(info, keep_b, keep_a, give_a, give_b, kept, *sent):
    pair = info[1] // 2
    pairs = keep_a.shape[0]
    for n, (keep, recv) in enumerate(((keep_b, give_a), (keep_a, give_b))):
        for shift in range(pairs):
            a = lax.rem(pair + shift, pairs)
            total = keep[a] + recv[a].astype(F32)
            if shift:
                sent[shift - 1][n] = total.astype(BF16)
            else:
                kept[n] = total


def close_kernel(info, own, kept, *refs):
    out = refs[-1]
    for n, column in enumerate((1 - info[0], info[0])):
        total = own[n] - kept[n]
        for recv in refs[:-1]:
            total = total - recv[n].astype(F32)
        out[column] = total


def turn_kernel(panel_v, sampler, panel_vt, sampler_t):
    sampler_t[...] = sampler[...].T
    for j in range(panel_v.shape[0]):
        panel_vt[j] = panel_v[j].T


def start_kernel(info, sampler_t, orig_u, orig_v, out):
    core = info[0]
    proj = dot(sampler_t[...], orig_v[core]).astype(BF16)
    out[...] = dot11(proj, orig_u[core])


def run(kernel, scalars, arrays, outs, scratch, limit, flops, name, aliases={}, apart=()):
    smem = pl.BlockSpec(memory_space=pltpu.SMEM)
    vmem = pl.BlockSpec(memory_space=pltpu.VMEM)
    shapes = [jax.ShapeDtypeStruct(*o) for o in outs]
    moved = sum(a.size * a.dtype.itemsize for a in list(arrays) + shapes)
    return pl.pallas_call(
        kernel,
        out_shape=shapes,
        in_specs=[smem] * len(scalars) + [vmem] * len(arrays) + [pl.BlockSpec(memory_space=pl.ANY)] * len(apart),
        out_specs=[vmem] * len(shapes),
        scratch_shapes=scratch,
        input_output_aliases=aliases,
        compiler_params=pltpu.CompilerParams(vmem_limit_bytes=limit * MIB),
        cost_estimate=pl.CostEstimate(flops=flops, bytes_accessed=moved, transcendentals=0),
        name=name,
    )(*scalars, *arrays, *apart)


def ring_order(count):
    if count % 2:
        return list(range(count))
    return list(range(0, count, 2)) + list(range(count - 1, 0, -2))


class Ring:
    def __init__(self, arrays, order, axis):
        count = len(order)
        self.count, self.axis, self.near = count, axis, (count - 1) // 2
        self.ahead = [(order[(p + 1) % count], order[p]) for p in range(count)]
        self.behind = [(order[p], order[(p + 1) % count]) for p in range(count)]
        self.found = [{0: a} for a in arrays]
        self.up, self.down = list(arrays), list(arrays)

    def step(self, number):
        for t in range(2):
            if number <= self.near or t == 0:
                self.up[t] = lax.ppermute(self.up[t], self.axis, self.ahead)
                self.found[t][number] = self.up[t]
            if number <= self.near or t == 1:
                self.down[t] = lax.ppermute(self.down[t], self.axis, self.behind)
                self.found[t][self.count - number] = self.down[t]

    def hold(self, value, t, number):
        if number > self.near:
            return value
        places = (number, self.count - number)
        value, *kept = lax.optimization_barrier((value, *(self.found[t][d] for d in places)))
        for d, block in zip(places, kept):
            self.found[t][d] = block
        return value

    def tie(self, value, number, which=(0, 1)):
        lists = [(self.up, t, number) for t in which if number <= self.near or t == 0]
        lists += [(self.down, t, self.count - number) for t in which if number <= self.near or t == 1]
        value, *held = lax.optimization_barrier((value, *(way[t] for way, t, _ in lists)))
        for (way, t, place), block in zip(lists, held):
            way[t] = self.found[t][place] = block
        return value

    def blocks(self, t):
        return [self.found[t][d] for d in range(self.count)]


def body(panel_u, panel_v, panel_rank, pivot_u, pivot_v, pivot_rank, orig_u, orig_v, sampler):
    order, width = panel_u.shape[2:]
    priors = panel_u.shape[1]
    pivots = pivot_u.shape[0]
    count = lax.axis_size("rows")
    cols = lax.axis_size("cols")
    pairs = cols // 2
    half, share = order // 2, order // cols
    me = lax.axis_index("cols")
    core, pair = me % 2, me // 2
    swap = [(i, i ^ 1) for i in range(cols)]

    ring = ring_order(count)
    place = np.argsort(np.array(ring))
    table = np.array([[ring[(place[r] + d) % count] for d in range(count)] for r in range(count)], np.int32)
    last = count // 2
    whole = count % 2 == 1 or last < 4 or count > RING_MOST
    if whole:
        table = np.zeros((count, 1), np.int32)
    sources = jnp.asarray(table)[lax.axis_index("rows")]
    info = jnp.concatenate([jnp.stack([core, me]).astype(jnp.int32), sources])

    panel_u, panel_v, orig_u, orig_v = panel_u[0], panel_v[0], orig_u[:, 0], orig_v[:, 0]
    square = 2 * width * width
    panel_vt, sampler_t = run(
        turn_kernel, [], [panel_v, sampler], [((priors, width, order), BF16), ((sampler.shape[1], order), BF16)], [], 12,
        10 * square * order, "turn"
    )
    (start,) = run(
        start_kernel, [info], [sampler_t, orig_u, orig_v], [((width, order), F32)], [], 12,
        2 * square * order, "start"
    )

    def shifted(x, shift):
        return lax.ppermute(x, "cols", [(i, (i + 2 * shift) % cols) for i in range(cols)])

    matrix = pltpu.VMEM((width, width), F32)
    tall = pltpu.VMEM((width, order), F32)

    def gathered(places, blocks, new_u, new_v, kept):
        new = len(places)
        shapes = [
            ((pivots, priors, width, width), F32), ((pivots, priors, width, width), F32),
            ((pivots, priors, order, width), BF16)
        ]
        first = 3 + 2 * new
        return run(
            functools.partial(gather_kernel, places, blocks), [info], [panel_vt, sampler_t, *new_u, *new_v, *kept],
            shapes, [], 28, 2 * pivots * priors * square * order * new // blocks, "gather",
            {first + n: n for n in range(len(kept))}
        )

    def updated(own_column, sampled, met):
        return run(
            functools.partial(update_kernel, own_column, places, blocks), [info, panel_rank, pivot_rank],
            [sampled, met, panel_u, panel_vt, sampler_t, *new_u, *new_v],
            [((priors, width, width), BF16), ((width, order), F32 if own_column else BF16)], [], 20,
            2 * priors * square * (order + width), "update"
        )

    def projected(own_column, qt, cross):
        return run(
            functools.partial(project_kernel, places, blocks, own_column), [info], [qt, panel_u, cross, u_all, *new_u],
            [((pairs, share, width), BF16), ((pairs, share, width), F32)], [pltpu.VMEM((order, width), F32)],
            20, 3 * priors * square * (2 * order + width), "project"
        )

    def placed(mine, other):
        return jnp.where(core == 0, jnp.stack([mine, other]), jnp.stack([other, mine]))

    if whole:
        blocks, places = 1, []
        new_u, new_v = ([lax.all_gather(x, "rows", axis=2, tiled=True)] for x in (pivot_u, pivot_v))
        sampled, met, u_all = gathered([0], 1, new_u, new_v, [])
        new_u, new_v = [], []
    else:
        blocks = count
        now, kept = Ring([pivot_u, pivot_v], ring, "rows"), []
        for number in range(1, last + 1):
            now.step(number)
            if 1 < number < last:
                kept[0] = now.tie(kept[0], number, (0,))
                if number == 2:
                    start = now.tie(start, number, (1,))
            places = sorted({number, count - number} | ({0} if number == 1 else set()))
            new_u, new_v = ([now.found[t][p] for p in places] for t in range(2))
            if number < last:
                kept = list(gathered(places, count, new_u, new_v, kept))
        sampled, met, u_all = kept
    cross_other, give = updated(False, sampled, met)
    recv = lax.ppermute(give, "cols", swap)
    cross_own, keep = updated(True, sampled, met)
    sent = (keep + recv.astype(F32)).astype(BF16)
    parts = [keep, recv, *(shifted(sent, shift) for shift in range(1, pairs))]
    qt, rows, given = run(
        orthonormal_kernel, [info], [start, *parts],
        [((width, order), BF16), ((share, width), F32), ((share, width), F32)], [tall, matrix], 16,
        128 * square * order, "orthonormal"
    )
    qt_other = lax.ppermute(qt, "cols", swap)
    rows_other = lax.ppermute(given, "cols", swap)
    give_a, keep_a = projected(True, qt, cross_own)
    qt_other, give_a, keep_a = lax.optimization_barrier((qt_other, give_a, keep_a))
    give_b, keep_b = projected(False, qt_other, cross_other)
    give_a, give_b = lax.ppermute(give_a, "cols", swap), lax.ppermute(give_b, "cols", swap)
    both = (pivots, share, width)
    kept, *sent = run(
        halve_kernel, [info], [keep_b, keep_a, give_a, give_b], [(both, F32)] + [(both, BF16)] * (pairs - 1), [], 8,
        square, "halve"
    )
    recv = [shifted(each, shift) for shift, each in enumerate(sent, 1)]
    (own,) = run(
        own_kernel, [info], [qt, qt_other], [(both, F32)],
        [pltpu.VMEM((pivots, order, width), BF16), pltpu.VMEM((pivots, share, width), BF16), pltpu.SemaphoreType.DMA((4,))],
        12, 4 * square * order, "own", apart=[orig_u, orig_v]
    )
    (coeff,) = run(close_kernel, [info], [own, kept, *recv], [(both, F32)], [], 8, square, "close")
    basis = placed(rows, rows_other)
    return (basis[:, None], coeff[:, None])


def solution(mesh):
    placed = (
        P("rows", "cols", None, None),
        P("rows", "cols", None, None),
        P("rows", "cols"),
        P(None, "cols", "rows", None),
        P(None, "cols", "rows", None),
        P(None, "cols"),
        P(None, "rows", None, None),
        P(None, "rows", None, None),
        P(),
    )
    return jax.shard_map(
        body,
        mesh=mesh,
        in_specs=placed,
        out_specs=(P(None, "rows", "cols", None), P(None, "rows", "cols", None)),
        check_vma=False,
    )
```

```python
import functools
import math

import jax
import jax.numpy as jnp
import numpy as np
from jax import lax
from jax.experimental import pallas as pl
from jax.experimental.pallas import tpu as pltpu
from jax.sharding import PartitionSpec as P

F32 = jnp.float32
BF16 = jnp.bfloat16
BLOCK = 32
SUB = 8
RING_MOST = 16
MIB = 1 << 20


def dot(a, b):
    return lax.dot_general(a, b, (((1,), (0,)), ((), ())), preferred_element_type=F32)


def dot00(a, b):
    return lax.dot_general(a, b, (((0,), (0,)), ((), ())), preferred_element_type=F32)


def dot11(a, b):
    return lax.dot_general(a, b, (((1,), (1,)), ((), ())), preferred_element_type=F32)


def split3(x):
    high = x.astype(BF16)
    rest = x - high.astype(F32)
    mid = rest.astype(BF16)
    low = (rest - mid.astype(F32)).astype(BF16)
    return high, mid, low


def eliminate(panel, first):
    rows, width = panel.shape
    lanes = 128
    tile = (SUB, lanes)
    lane = lax.broadcasted_iota(jnp.int32, tile, 1)
    sub = lax.broadcasted_iota(jnp.int32, tile, 0)
    high = rows // SUB
    halves = width // lanes
    part = [
        [panel[v * SUB : (v + 1) * SUB, h * lanes : (h + 1) * lanes] for h in range(halves)]
        for v in range(high)
    ]
    mine, start = first // lanes, first % lanes
    scales = []
    for top in range(high):
        at = start + top * SUB
        inside = (lane >= at) & (lane < at + SUB)
        column = [
            [jnp.broadcast_to(part[v][mine][:, at + m : at + m + 1], tile) for v in range(top, high)]
            for m in range(SUB)
        ]
        small = [
            [jnp.broadcast_to(column[b][0][a : a + 1, :], tile) for b in range(a + 1)] for a in range(SUB)
        ]
        row = []
        for a in range(SUB):
            row.append([jnp.broadcast_to(part[top][h][a : a + 1, :], tile) for h in range(halves)])
            row[a][mine] = jnp.where(inside, jnp.where(lane == at + a, 1.0, 0.0), row[a][mine])
        pivots = small[0][0]
        factor = []
        for m in range(SUB):
            inverse = pl.reciprocal(small[m][m], approx=True)
            if m:
                pivots = jnp.where(sub == m, small[m][m], pivots)
            for a in range(m + 1, SUB):
                ratio = small[a][m] * inverse
                for b in range(m + 1, a + 1):
                    small[a][b] = small[a][b] - ratio * small[b][m]
                row[a] = [x - ratio * y for x, y in zip(row[a], row[m])]
            factor.append([c * inverse for c in column[m][1:]])
            for b in range(m + 1, SUB):
                column[b][1:] = [c - f * small[b][m] for c, f in zip(column[b][1:], factor[m])]
        for v in range(top + 1, high):
            for h in range(halves):
                value = jnp.where(inside, 0.0, part[v][h]) if h == mine else part[v][h]
                for m in range(SUB):
                    value = value - factor[m][v - top - 1] * row[m][h]
                part[v][h] = value
        for h in range(halves):
            value = row[0][h]
            for m in range(1, SUB):
                value = jnp.where(sub == m, row[m][h], value)
            part[top][h] = value
        scales.append(lax.rsqrt(pivots))
    done = []
    for v in range(high):
        cells = []
        for h in range(halves):
            value = part[v][h] * scales[v]
            if h == mine:
                value = jnp.where((lane > start + v * SUB + sub) & (lane < start + rows), 0.0, value)
            cells.append(value)
        done.append(jnp.concatenate(cells, 1))
    return jnp.concatenate(done, 0)


def invert_blocks(work, begin, end):
    width = work.shape[0]
    lane = lax.broadcasted_iota(jnp.int32, (1, width), 1)
    for first in range(begin, end, BLOCK):
        last = first + BLOCK
        panel = eliminate(work[first:last, :], first)
        work[first:last, :] = panel
        if last < width:
            base = last // 128 * 128
            high, mid, low = split3(panel)
            left = jnp.concatenate([high, high, mid, mid, high, low], 0)[:, base:]
            right = jnp.concatenate([high, mid, high, mid, low, high], 0)
            update = dot00(left, right)[last - base :, :]
            inside = (lane >= first) & (lane < last)
            work[last:, :] = jnp.where(inside, 0.0, work[last:, :]) - update


def orthonormal_kernel(info, start, *refs):
    parts, (qt, basis, given, yt, work) = refs[:-5], refs[-5:]
    width, order = yt.shape
    core = info[0]
    total = start[...]
    for part in parts:
        total = total - part[...].astype(F32)
    yt[...] = total
    high, mid, low = split3(yt[...])
    cross = dot11(high, mid) + dot11(high, low)
    work[...] = dot11(high, high) + (cross + cross.T + dot11(mid, mid))
    invert_blocks(work, 0, width)
    row = lax.broadcasted_iota(jnp.int32, (width, width), 0)
    col = lax.broadcasted_iota(jnp.int32, (width, width), 1)
    m_high, m_low, _ = split3(jnp.where(col <= row, work[...], 0.0))
    high, mid, _ = split3(yt[...])
    product = dot(m_high, high) + (dot(m_high, mid) + dot(m_low, high))
    qt[...] = product.astype(BF16)
    yt[...] = product
    share = basis.shape[0]
    for out, index in ((basis, info[1]), (given, info[1] + 1 - 2 * core)):
        rows = yt[:, pl.ds(pl.multiple_of(index * share, 128), share)]
        out[...] = rows.T * math.sqrt(order)


def gather_kernel(places, blocks, info, panel_vt, sampler_t, *refs):
    new = len(places)
    u, v = refs[:new], refs[new : 2 * new]
    kept = refs[2 * new : -3]
    sampled, met, u_all = refs[-3:]
    pivots, priors, order, width = u_all.shape
    slab = order // blocks
    spans = [pl.ds(pl.multiple_of(info[2 + p] * slab, 128), slab) for p in places]
    drawn = jnp.concatenate([sampler_t[:, span] for span in spans], 1)
    for j in range(priors):
        left = jnp.concatenate([panel_vt[j, :, span] for span in spans], 1)
        for c in range(pivots):
            u_new = jnp.concatenate([block[c, j] for block in u], 0)
            v_new = jnp.concatenate([block[c, j] for block in v], 0)
            one, two = dot(drawn, u_new), dot(left, v_new)
            if kept:
                one, two = one + kept[0][c, j], two + kept[1][c, j]
            sampled[c, j] = one
            met[c, j] = two
            for n, p in enumerate(places):
                u_all[c, j, p * slab : (p + 1) * slab, :] = u_new[n * slab : (n + 1) * slab, :]


def sampled_kernel(places, blocks, info, sampled, sampler_t, *refs):
    late, out = refs[:-1], refs[-1]
    slab = sampler_t.shape[1] // blocks
    for c in range(out.shape[0]):
        for j in range(out.shape[1]):
            total = sampled[c, j]
            for place in places:
                span = pl.ds(pl.multiple_of(info[2 + place] * slab, 128), slab)
                total += dot(sampler_t[:, span], late[c][j])
            out[c, j] = total.astype(BF16)


def update_kernel(own_column, places, blocks, info, panel_rank, pivot_rank, sampled, met, panel_u, panel_vt, *refs):
    late, (cross, out) = refs[:-2], refs[-2:]
    priors, width, _ = cross.shape
    slab = panel_vt.shape[2] // blocks
    column = info[0] if own_column else 1 - info[0]
    row = lax.broadcasted_iota(jnp.int32, (width, width), 0)
    col = lax.broadcasted_iota(jnp.int32, (width, width), 1)
    terms = []
    for j in range(priors):
        two = met[column, j]
        for place in places:
            span = pl.ds(pl.multiple_of(info[2 + place] * slab, 128), slab)
            two += dot(panel_vt[j, :, span], jnp.where(column == 0, late[0][j], late[1][j]))
        inside = (row < panel_rank[0, j]) & (col < pivot_rank[column, j])
        cross[j] = jnp.where(inside, two, 0.0).astype(BF16)
        terms.append(dot11(sampled[column, j], cross[j]).astype(BF16))
    half = out.shape[1] // 2
    for at in (0, half):
        total = jnp.zeros((width, half), F32)
        for j in range(priors):
            total += dot11(terms[j], panel_u[j, at : at + half, :])
        out[:, at : at + half] = total.astype(out.dtype)


def project_kernel(places, blocks, own_column, info, qt, panel_u, cross, u_all, *refs):
    give, keep, work = refs[-3:]
    _, priors, order, width = u_all.shape
    slab = order // blocks
    pairs, share, _ = keep.shape
    core = info[0]
    column = core if own_column else 1 - core
    mids = []
    for j in range(priors):
        inner = dot(qt[...], panel_u[j]).astype(BF16)
        mids.append(dot(inner, cross[j]).astype(BF16))

    def rows_of(j, b):
        if b in places:
            return jnp.where(column == 0, refs[0][j], refs[1][j])
        return u_all[column, j, b * slab : (b + 1) * slab, :]

    some = max(1, blocks // 2)
    for begin in range(0, blocks, some):
        total = jnp.zeros((some * slab, width), F32)
        for j in range(priors):
            total += dot11(jnp.concatenate([rows_of(j, begin + n) for n in range(some)], 0), mids[j])
        for n in range(some):
            place = pl.ds(pl.multiple_of(info[2 + begin + n] * slab, SUB), slab)
            work[place, :] = total[n * slab : (n + 1) * slab, :]
    for a in range(pairs):
        for out, which in ((give, 1 - core), (keep, core)):
            place = pl.ds(pl.multiple_of((2 * a + which) * share, SUB), share)
            out[a] = work[place, :].astype(out.dtype)


def own_kernel(info, qt, qt_other, orig_u, orig_v, out, u_buf, v_buf, sems):
    share = out.shape[1]
    rows = pl.ds(pl.multiple_of(info[1] * share, 16), share)
    copies = []
    for n, column in enumerate((1 - info[0], info[0])):
        copies.append(pltpu.make_async_copy(orig_u.at[column], u_buf.at[n], sems.at[2 * n]))
        copies.append(pltpu.make_async_copy(orig_v.at[column, rows], v_buf.at[n], sems.at[2 * n + 1]))
    for copy in copies:
        copy.start()
    for n, q in enumerate((qt_other, qt)):
        copies[2 * n].wait()
        copies[2 * n + 1].wait()
        out[n] = dot11(v_buf[n], dot(q[...], u_buf[n]).astype(BF16))


def halve_kernel(info, keep_b, keep_a, give_a, give_b, *sent):
    pairs = keep_a.shape[0]
    for shift in range(1, pairs):
        a = lax.rem(info[1] // 2 + shift, pairs)
        for n, (keep, recv) in enumerate(((keep_b, give_a), (keep_a, give_b))):
            sent[shift - 1][n] = (keep[a] + recv[a].astype(F32)).astype(BF16)


def turn_kernel(panel_v, sampler, panel_vt, sampler_t):
    sampler_t[...] = sampler[...].T
    for j in range(panel_v.shape[0]):
        panel_vt[j] = panel_v[j].T


def start_kernel(info, sampler_t, orig_u, orig_v, out):
    core = info[0]
    proj = dot(sampler_t[...], orig_v[core]).astype(BF16)
    out[...] = dot11(proj, orig_u[core])


def run(kernel, scalars, arrays, outs, scratch, limit, flops, name, aliases={}, apart=()):
    smem = pl.BlockSpec(memory_space=pltpu.SMEM)
    vmem = pl.BlockSpec(memory_space=pltpu.VMEM)
    shapes = [jax.ShapeDtypeStruct(*o) for o in outs]
    moved = sum(a.size * a.dtype.itemsize for a in list(arrays) + shapes)
    return pl.pallas_call(
        kernel,
        out_shape=shapes,
        in_specs=[smem] * len(scalars) + [vmem] * len(arrays) + [pl.BlockSpec(memory_space=pl.ANY)] * len(apart),
        out_specs=[vmem] * len(shapes),
        scratch_shapes=scratch,
        input_output_aliases=aliases,
        compiler_params=pltpu.CompilerParams(vmem_limit_bytes=limit * MIB),
        cost_estimate=pl.CostEstimate(flops=flops, bytes_accessed=moved, transcendentals=0),
        name=name,
    )(*scalars, *arrays, *apart)


def ring_order(count):
    if count % 2:
        return list(range(count))
    return list(range(0, count, 2)) + list(range(count - 1, 0, -2))


class Ring:
    def __init__(self, arrays, order, axis):
        count = len(order)
        self.count, self.axis, self.near = count, axis, (count - 1) // 2
        self.ahead = [(order[(p + 1) % count], order[p]) for p in range(count)]
        self.behind = [(order[p], order[(p + 1) % count]) for p in range(count)]
        self.found = [{0: a} for a in arrays]
        self.up, self.down = list(arrays), list(arrays)

    def step(self, number):
        for t in range(2):
            found = self.found[t]
            if number <= self.near:
                self.up[t] = found[number] = lax.ppermute(self.up[t], self.axis, self.ahead)
                self.down[t] = found[self.count - number] = lax.ppermute(self.down[t], self.axis, self.behind)
            else:
                found[number] = [
                    lax.ppermute(self.up[t][0], self.axis, self.ahead),
                    lax.ppermute(self.down[t][1], self.axis, self.behind),
                ]

    def tie(self, value, number, which=(0, 1)):
        lists = [(self.up, t, number) for t in which if number <= self.near or t == 0]
        lists += [(self.down, t, self.count - number) for t in which if number <= self.near or t == 1]
        value, *held = lax.optimization_barrier((value, *(way[t] for way, t, _ in lists)))
        for (way, t, place), block in zip(lists, held):
            way[t] = self.found[t][place] = block
        return value


def body(panel_u, panel_v, panel_rank, pivot_u, pivot_v, pivot_rank, orig_u, orig_v, sampler):
    order, width = panel_u.shape[2:]
    priors = panel_u.shape[1]
    pivots = pivot_u.shape[0]
    count = lax.axis_size("rows")
    cols = lax.axis_size("cols")
    pairs = cols // 2
    half, share = order // 2, order // cols
    me = lax.axis_index("cols")
    core, pair = me % 2, me // 2
    swap = [(i, i ^ 1) for i in range(cols)]

    ring = ring_order(count)
    place = np.argsort(np.array(ring))
    table = np.array([[ring[(place[r] + d) % count] for d in range(count)] for r in range(count)], np.int32)
    last = count // 2
    whole = count % 2 == 1 or last < 4 or count > RING_MOST
    if whole:
        table = np.zeros((count, 1), np.int32)
    sources = jnp.asarray(table)[lax.axis_index("rows")]
    info = jnp.concatenate([jnp.stack([core, me]).astype(jnp.int32), sources])

    panel_u, panel_v, orig_u, orig_v = panel_u[0], panel_v[0], orig_u[:, 0], orig_v[:, 0]
    square = 2 * width * width
    panel_vt, sampler_t = run(
        turn_kernel, [], [panel_v, sampler], [((priors, width, order), BF16), ((sampler.shape[1], order), BF16)], [], 12,
        10 * square * order, "turn"
    )
    (start,) = run(
        start_kernel, [info], [sampler_t, orig_u, orig_v], [((width, order), F32)], [], 12,
        2 * square * order, "start"
    )

    def shifted(x, shift):
        return lax.ppermute(x, "cols", [(i, (i + 2 * shift) % cols) for i in range(cols)])

    matrix = pltpu.VMEM((width, width), F32)
    tall = pltpu.VMEM((width, order), F32)

    def gathered(places, blocks, new_u, new_v, kept):
        new = len(places)
        shapes = [
            ((pivots, priors, width, width), F32), ((pivots, priors, width, width), F32),
            ((pivots, priors, order, width), BF16)
        ]
        first = 3 + 2 * new
        return run(
            functools.partial(gather_kernel, places, blocks), [info], [panel_vt, sampler_t, *new_u, *new_v, *kept],
            shapes, [], 28, 2 * pivots * priors * square * order * new // blocks, "gather",
            {first + n: n for n in range(len(kept))}
        )

    def updated(own_column, sampled, met):
        return run(
            functools.partial(update_kernel, own_column, places, blocks), [info, panel_rank, pivot_rank],
            [sampled, met, panel_u, panel_vt, *late_v],
            [((priors, width, width), BF16), ((width, order), F32 if own_column else BF16)], [], 20,
            2 * priors * square * (order + width), "update"
        )

    def projected(own_column, qt, cross):
        return run(
            functools.partial(project_kernel, places, blocks, own_column), [info], [qt, panel_u, cross, u_all, *late_u],
            [((pairs, share, width), BF16), ((pairs, share, width), F32)], [pltpu.VMEM((order, width), F32)],
            20, 3 * priors * square * (2 * order + width), "project"
        )

    def placed(mine, other):
        return jnp.where(core == 0, jnp.stack([mine, other]), jnp.stack([other, mine]))

    if whole:
        blocks, places = 1, []
        new_u, new_v = ([lax.all_gather(x, "rows", axis=2, tiled=True)] for x in (pivot_u, pivot_v))
        sampled, met, u_all = gathered([0], 1, new_u, new_v, [])
        late_u, late_v = [], []
    else:
        blocks = count
        now, kept = Ring([pivot_u, pivot_v], ring, "rows"), []
        for number in range(1, last + 1):
            now.step(number)
            if 1 < number < last:
                kept[0] = now.tie(kept[0], number, (0,))
                if number == 2:
                    start = now.tie(start, number, (1,))
            if number == last:
                places = [last]
                late_u, late_v = now.found[0][last], now.found[1][last]
            else:
                places = sorted({number, count - number} | ({0} if number == 1 else set()))
                new_u, new_v = ([now.found[t][p] for p in places] for t in range(2))
                kept = list(gathered(places, count, new_u, new_v, kept))
        sampled, met, u_all = kept
    (sampled,) = run(
        functools.partial(sampled_kernel, places, blocks), [info], [sampled, sampler_t, *late_u],
        [((pivots, priors, width, width), BF16)], [], 12, square * order, "sampled"
    )
    cross_other, give = updated(False, sampled, met)
    recv = lax.ppermute(give, "cols", swap)
    cross_own, keep = updated(True, sampled, met)
    sent = (keep + recv.astype(F32)).astype(BF16)
    parts = [keep, recv, *(shifted(sent, shift) for shift in range(1, pairs))]
    qt, rows, given = run(
        orthonormal_kernel, [info], [start, *parts],
        [((width, order), BF16), ((share, width), F32), ((share, width), F32)], [tall, matrix], 16,
        128 * square * order, "orthonormal"
    )
    qt_other = lax.ppermute(qt, "cols", swap)
    rows_other = lax.ppermute(given, "cols", swap)
    give_a, keep_a = projected(True, qt, cross_own)
    qt_other, give_a, keep_a = lax.optimization_barrier((qt_other, give_a, keep_a))
    give_b, keep_b = projected(False, qt_other, cross_other)
    give_a, give_b = lax.ppermute(give_a, "cols", swap), lax.ppermute(give_b, "cols", swap)

    sent = run(
        halve_kernel, [info], [keep_b, keep_a, give_a, give_b], [((pivots, share, width), BF16)] * (pairs - 1), [], 8,
        square, "halve"
    )
    recv = [shifted(each, shift) for shift, each in enumerate(sent, 1)]
    (own,) = run(
        own_kernel, [info], [qt, qt_other], [((pivots, share, width), F32)],
        [pltpu.VMEM((pivots, order, width), BF16), pltpu.VMEM((pivots, share, width), BF16), pltpu.SemaphoreType.DMA((4,))],
        12, 4 * square * order, "own", apart=[orig_u, orig_v]
    )
    other, mine = (
        own[n] - (lax.dynamic_index_in_dim(keep, pair, 0, False) + lax.dynamic_index_in_dim(part, pair, 0, False).astype(F32))
        for n, (keep, part) in enumerate(((keep_b, give_a), (keep_a, give_b)))
    )
    coeff = lax.optimization_barrier(placed(mine, other))
    for each in recv:
        coeff = coeff - jnp.where(core == 0, each[::-1], each).astype(F32)
    basis = placed(rows, rows_other)
    return (basis[:, None], coeff[:, None])


def solution(mesh):
    placed = (
        P("rows", "cols", None, None),
        P("rows", "cols", None, None),
        P("rows", "cols"),
        P(None, "cols", "rows", None),
        P(None, "cols", "rows", None),
        P(None, "cols"),
        P(None, "rows", None, None),
        P(None, "rows", None, None),
        P(),
    )
    return jax.shard_map(
        body,
        mesh=mesh,
        in_specs=placed,
        out_specs=(P(None, "rows", "cols", None), P(None, "rows", "cols", None)),
        check_vma=False,
    )
```

```python
import functools
import math

import jax
import jax.numpy as jnp
import numpy as np
from jax import lax
from jax.experimental import pallas as pl
from jax.experimental.pallas import tpu as pltpu
from jax.sharding import PartitionSpec as P

F32 = jnp.float32
BF16 = jnp.bfloat16
BLOCK = 32
SUB = 8
RING_MOST = 16
MIB = 1 << 20


def dot(a, b):
    return lax.dot_general(a, b, (((1,), (0,)), ((), ())), preferred_element_type=F32)


def dot00(a, b):
    return lax.dot_general(a, b, (((0,), (0,)), ((), ())), preferred_element_type=F32)


def dot11(a, b):
    return lax.dot_general(a, b, (((1,), (1,)), ((), ())), preferred_element_type=F32)


def split3(x):
    high = x.astype(BF16)
    rest = x - high.astype(F32)
    mid = rest.astype(BF16)
    low = (rest - mid.astype(F32)).astype(BF16)
    return high, mid, low


def eliminate(panel, first):
    rows, width = panel.shape
    lanes = 128
    tile = (SUB, lanes)
    lane = lax.broadcasted_iota(jnp.int32, tile, 1)
    sub = lax.broadcasted_iota(jnp.int32, tile, 0)
    high = rows // SUB
    halves = width // lanes
    part = [
        [panel[v * SUB : (v + 1) * SUB, h * lanes : (h + 1) * lanes] for h in range(halves)]
        for v in range(high)
    ]
    mine, start = first // lanes, first % lanes
    scales = []
    for top in range(high):
        at = start + top * SUB
        inside = (lane >= at) & (lane < at + SUB)
        column = [
            [jnp.broadcast_to(part[v][mine][:, at + m : at + m + 1], tile) for v in range(top, high)]
            for m in range(SUB)
        ]
        small = [
            [jnp.broadcast_to(column[b][0][a : a + 1, :], tile) for b in range(a + 1)] for a in range(SUB)
        ]
        row = []
        for a in range(SUB):
            row.append([jnp.broadcast_to(part[top][h][a : a + 1, :], tile) for h in range(halves)])
            row[a][mine] = jnp.where(inside, jnp.where(lane == at + a, 1.0, 0.0), row[a][mine])
        pivots = small[0][0]
        factor = []
        for m in range(SUB):
            inverse = pl.reciprocal(small[m][m], approx=True)
            if m:
                pivots = jnp.where(sub == m, small[m][m], pivots)
            for a in range(m + 1, SUB):
                ratio = small[a][m] * inverse
                for b in range(m + 1, a + 1):
                    small[a][b] = small[a][b] - ratio * small[b][m]
                row[a] = [x - ratio * y for x, y in zip(row[a], row[m])]
            factor.append([c * inverse for c in column[m][1:]])
            for b in range(m + 1, SUB):
                column[b][1:] = [c - f * small[b][m] for c, f in zip(column[b][1:], factor[m])]
        for v in range(top + 1, high):
            for h in range(halves):
                value = jnp.where(inside, 0.0, part[v][h]) if h == mine else part[v][h]
                for m in range(SUB):
                    value = value - factor[m][v - top - 1] * row[m][h]
                part[v][h] = value
        for h in range(halves):
            value = row[0][h]
            for m in range(1, SUB):
                value = jnp.where(sub == m, row[m][h], value)
            part[top][h] = value
        scales.append(lax.rsqrt(pivots))
    done = []
    for v in range(high):
        cells = []
        for h in range(halves):
            value = part[v][h] * scales[v]
            if h == mine:
                value = jnp.where((lane > start + v * SUB + sub) & (lane < start + rows), 0.0, value)
            cells.append(value)
        done.append(jnp.concatenate(cells, 1))
    return jnp.concatenate(done, 0)


def invert_blocks(work, begin, end):
    width = work.shape[0]
    lane = lax.broadcasted_iota(jnp.int32, (1, width), 1)
    for first in range(begin, end, BLOCK):
        last = first + BLOCK
        panel = eliminate(work[first:last, :], first)
        work[first:last, :] = panel
        if last < width:
            base = last // 128 * 128
            high, mid, low = split3(panel)
            left = jnp.concatenate([high, high, mid, mid, high, low], 0)[:, base:]
            right = jnp.concatenate([high, mid, high, mid, low, high], 0)
            update = dot00(left, right)[last - base :, :]
            inside = (lane >= first) & (lane < last)
            work[last:, :] = jnp.where(inside, 0.0, work[last:, :]) - update


def orthonormal_kernel(info, start, *refs):
    parts, (qt, basis, given, yt, work) = refs[:-5], refs[-5:]
    width, order = yt.shape
    core = info[0]
    total = start[...]
    for part in parts:
        total = total - part[...].astype(F32)
    yt[...] = total
    high, mid, low = split3(yt[...])
    cross = dot11(high, mid) + dot11(high, low)
    work[...] = dot11(high, high) + (cross + cross.T + dot11(mid, mid))
    invert_blocks(work, 0, width)
    row = lax.broadcasted_iota(jnp.int32, (width, width), 0)
    col = lax.broadcasted_iota(jnp.int32, (width, width), 1)
    m_high, m_low, _ = split3(jnp.where(col <= row, work[...], 0.0))
    high, mid, _ = split3(yt[...])
    product = dot(m_high, high) + (dot(m_high, mid) + dot(m_low, high))
    qt[...] = product.astype(BF16)
    yt[...] = product
    share = basis.shape[0]
    for out, index in ((basis, info[1]), (given, info[1] + 1 - 2 * core)):
        rows = yt[:, pl.ds(pl.multiple_of(index * share, 128), share)]
        out[...] = rows.T * math.sqrt(order)


def gather_kernel(places, blocks, info, panel_vt, sampler_t, *refs):
    new = len(places)
    u, v = refs[:new], refs[new : 2 * new]
    kept = refs[2 * new : -3]
    sampled, met, u_all = refs[-3:]
    pivots, priors, order, width = u_all.shape
    slab = order // blocks
    spans = [pl.ds(pl.multiple_of(info[2 + p] * slab, 128), slab) for p in places]
    drawn = jnp.concatenate([sampler_t[:, span] for span in spans], 1)
    for j in range(priors):
        left = jnp.concatenate([panel_vt[j, :, span] for span in spans], 1)
        for c in range(pivots):
            u_new = jnp.concatenate([block[c, j] for block in u], 0)
            v_new = jnp.concatenate([block[c, j] for block in v], 0)
            one, two = dot(drawn, u_new), dot(left, v_new)
            if kept:
                one, two = one + kept[0][c, j], two + kept[1][c, j]
            sampled[c, j] = one
            met[c, j] = two
            for n, p in enumerate(places):
                u_all[c, j, p * slab : (p + 1) * slab, :] = u_new[n * slab : (n + 1) * slab, :]


def sampled_kernel(places, blocks, info, sampled, sampler_t, *refs):
    late, (out, u_all) = refs[: len(refs) - 3], refs[-2:]
    slab = sampler_t.shape[1] // blocks
    for c in range(out.shape[0]):
        for j in range(out.shape[1]):
            total = sampled[c, j]
            for place in places:
                span = pl.ds(pl.multiple_of(info[2 + place] * slab, 128), slab)
                total += dot(sampler_t[:, span], late[c][j])
                u_all[c, j, place * slab : (place + 1) * slab, :] = late[c][j]
            out[c, j] = total.astype(BF16)


def update_kernel(own_column, places, blocks, info, panel_rank, pivot_rank, sampled, met, panel_u, panel_vt, *refs):
    late, (cross, out) = refs[:-2], refs[-2:]
    priors, width, _ = cross.shape
    slab = panel_vt.shape[2] // blocks
    column = info[0] if own_column else 1 - info[0]
    row = lax.broadcasted_iota(jnp.int32, (width, width), 0)
    col = lax.broadcasted_iota(jnp.int32, (width, width), 1)
    terms = []
    for j in range(priors):
        two = met[column, j]
        for place in places:
            span = pl.ds(pl.multiple_of(info[2 + place] * slab, 128), slab)
            two += dot(panel_vt[j, :, span], jnp.where(column == 0, late[0][j], late[1][j]))
        inside = (row < panel_rank[0, j]) & (col < pivot_rank[column, j])
        cross[j] = jnp.where(inside, two, 0.0).astype(BF16)
        terms.append(dot11(sampled[column, j], cross[j]).astype(BF16))
    half = out.shape[1] // 2
    for at in (0, half):
        total = jnp.zeros((width, half), F32)
        for j in range(priors):
            total += dot11(terms[j], panel_u[j, at : at + half, :])
        out[:, at : at + half] = total.astype(out.dtype)


def project_kernel(blocks, own_column, info, qt, panel_u, cross, u_all, give, keep, work):
    _, priors, order, width = u_all.shape
    slab = order // blocks
    pairs, share, _ = keep.shape
    core = info[0]
    column = core if own_column else 1 - core
    mids = []
    for j in range(priors):
        inner = dot(qt[...], panel_u[j]).astype(BF16)
        mids.append(dot(inner, cross[j]).astype(BF16))
    some = max(1, blocks // 2)
    for begin in range(0, blocks, some):
        total = jnp.zeros((some * slab, width), F32)
        for j in range(priors):
            total += dot11(u_all[column, j, begin * slab : (begin + some) * slab, :], mids[j])
        for n in range(some):
            place = pl.ds(pl.multiple_of(info[2 + begin + n] * slab, SUB), slab)
            work[place, :] = total[n * slab : (n + 1) * slab, :]
    for a in range(pairs):
        for out, which in ((give, 1 - core), (keep, core)):
            place = pl.ds(pl.multiple_of((2 * a + which) * share, SUB), share)
            out[a] = work[place, :].astype(out.dtype)


def own_kernel(info, qt, qt_other, keep_b, keep_a, give_a, give_b, orig_u, orig_v, out, u_buf, v_buf, sems):
    share = out.shape[1]
    pair = info[1] // 2
    rows = pl.ds(pl.multiple_of(info[1] * share, 16), share)
    work = ((1 - info[0], qt_other, keep_b, give_a), (info[0], qt, keep_a, give_b))
    copies = []
    for n, (column, *_) in enumerate(work):
        copies.append(pltpu.make_async_copy(orig_u.at[column], u_buf.at[n], sems.at[2 * n]))
        copies.append(pltpu.make_async_copy(orig_v.at[column, rows], v_buf.at[n], sems.at[2 * n + 1]))
    for copy in copies:
        copy.start()
    for n, (column, q, keep, recv) in enumerate(work):
        copies[2 * n].wait()
        copies[2 * n + 1].wait()
        total = dot11(v_buf[n], dot(q[...], u_buf[n]).astype(BF16))
        out[column] = total - (keep[pair] + recv[pair].astype(F32))


def halve_kernel(info, keep_b, keep_a, give_a, give_b, *sent):
    pairs = keep_a.shape[0]
    for shift in range(1, pairs):
        a = lax.rem(info[1] // 2 + shift, pairs)
        for n, (keep, recv) in enumerate(((keep_b, give_a), (keep_a, give_b))):
            sent[shift - 1][n] = (keep[a] + recv[a].astype(F32)).astype(BF16)


def turn_kernel(panel_v, sampler, panel_vt, sampler_t):
    sampler_t[...] = sampler[...].T
    for j in range(panel_v.shape[0]):
        panel_vt[j] = panel_v[j].T


def start_kernel(info, sampler_t, orig_u, orig_v, out):
    core = info[0]
    proj = dot(sampler_t[...], orig_v[core]).astype(BF16)
    out[...] = dot11(proj, orig_u[core])


def run(kernel, scalars, arrays, outs, scratch, limit, flops, name, aliases={}, apart=()):
    smem = pl.BlockSpec(memory_space=pltpu.SMEM)
    vmem = pl.BlockSpec(memory_space=pltpu.VMEM)
    shapes = [jax.ShapeDtypeStruct(*o) for o in outs]
    moved = sum(a.size * a.dtype.itemsize for a in list(arrays) + shapes)
    return pl.pallas_call(
        kernel,
        out_shape=shapes,
        in_specs=[smem] * len(scalars) + [vmem] * len(arrays) + [pl.BlockSpec(memory_space=pl.ANY)] * len(apart),
        out_specs=[vmem] * len(shapes),
        scratch_shapes=scratch,
        input_output_aliases=aliases,
        compiler_params=pltpu.CompilerParams(vmem_limit_bytes=limit * MIB),
        cost_estimate=pl.CostEstimate(flops=flops, bytes_accessed=moved, transcendentals=0),
        name=name,
    )(*scalars, *arrays, *apart)


def ring_order(count):
    if count % 2:
        return list(range(count))
    return list(range(0, count, 2)) + list(range(count - 1, 0, -2))


class Ring:
    def __init__(self, arrays, order, axis):
        count = len(order)
        self.count, self.axis, self.near = count, axis, (count - 1) // 2
        self.ahead = [(order[(p + 1) % count], order[p]) for p in range(count)]
        self.behind = [(order[p], order[(p + 1) % count]) for p in range(count)]
        self.found = [{0: a} for a in arrays]
        self.up, self.down = list(arrays), list(arrays)

    def step(self, number):
        for t in range(2):
            found = self.found[t]
            if number <= self.near:
                self.up[t] = found[number] = lax.ppermute(self.up[t], self.axis, self.ahead)
                self.down[t] = found[self.count - number] = lax.ppermute(self.down[t], self.axis, self.behind)
            else:
                found[number] = [
                    lax.ppermute(self.up[t][0], self.axis, self.ahead),
                    lax.ppermute(self.down[t][1], self.axis, self.behind),
                ]

    def tie(self, value, number, which=(0, 1)):
        lists = [(self.up, t, number) for t in which if number <= self.near or t == 0]
        lists += [(self.down, t, self.count - number) for t in which if number <= self.near or t == 1]
        value, *held = lax.optimization_barrier((value, *(way[t] for way, t, _ in lists)))
        for (way, t, place), block in zip(lists, held):
            way[t] = self.found[t][place] = block
        return value


def body(panel_u, panel_v, panel_rank, pivot_u, pivot_v, pivot_rank, orig_u, orig_v, sampler):
    order, width = panel_u.shape[2:]
    priors = panel_u.shape[1]
    pivots = pivot_u.shape[0]
    count = lax.axis_size("rows")
    cols = lax.axis_size("cols")
    pairs = cols // 2
    half, share = order // 2, order // cols
    me = lax.axis_index("cols")
    core, pair = me % 2, me // 2
    swap = [(i, i ^ 1) for i in range(cols)]

    ring = ring_order(count)
    place = np.argsort(np.array(ring))
    table = np.array([[ring[(place[r] + d) % count] for d in range(count)] for r in range(count)], np.int32)
    last = count // 2
    whole = count % 2 == 1 or last < 4 or count > RING_MOST
    if whole:
        table = np.zeros((count, 1), np.int32)
    sources = jnp.asarray(table)[lax.axis_index("rows")]
    info = jnp.concatenate([jnp.stack([core, me]).astype(jnp.int32), sources])

    panel_u, panel_v, orig_u, orig_v = panel_u[0], panel_v[0], orig_u[:, 0], orig_v[:, 0]
    square = 2 * width * width
    panel_vt, sampler_t = run(
        turn_kernel, [], [panel_v, sampler], [((priors, width, order), BF16), ((sampler.shape[1], order), BF16)], [], 12,
        10 * square * order, "turn"
    )
    (start,) = run(
        start_kernel, [info], [sampler_t, orig_u, orig_v], [((width, order), F32)], [], 12,
        2 * square * order, "start"
    )

    def shifted(x, shift):
        return lax.ppermute(x, "cols", [(i, (i + 2 * shift) % cols) for i in range(cols)])

    matrix = pltpu.VMEM((width, width), F32)
    tall = pltpu.VMEM((width, order), F32)

    def gathered(places, blocks, new_u, new_v, kept):
        new = len(places)
        shapes = [
            ((pivots, priors, width, width), F32), ((pivots, priors, width, width), F32),
            ((pivots, priors, order, width), BF16)
        ]
        first = 3 + 2 * new
        return run(
            functools.partial(gather_kernel, places, blocks), [info], [panel_vt, sampler_t, *new_u, *new_v, *kept],
            shapes, [], 28, 2 * pivots * priors * square * order * new // blocks, "gather",
            {first + n: n for n in range(len(kept))}
        )

    def updated(own_column, sampled, met):
        return run(
            functools.partial(update_kernel, own_column, places, blocks), [info, panel_rank, pivot_rank],
            [sampled, met, panel_u, panel_vt, *late_v],
            [((priors, width, width), BF16), ((width, order), F32 if own_column else BF16)], [], 20,
            2 * priors * square * (order + width), "update"
        )

    def projected(own_column, qt, cross):
        return run(
            functools.partial(project_kernel, blocks, own_column), [info], [qt, panel_u, cross, u_all],
            [((pairs, share, width), BF16), ((pairs, share, width), F32)], [pltpu.VMEM((order, width), F32)],
            20, 3 * priors * square * (2 * order + width), "project"
        )

    def placed(mine, other):
        return jnp.where(core == 0, jnp.stack([mine, other]), jnp.stack([other, mine]))

    if whole:
        blocks, places = 1, []
        new_u, new_v = ([lax.all_gather(x, "rows", axis=2, tiled=True)] for x in (pivot_u, pivot_v))
        sampled, met, u_all = gathered([0], 1, new_u, new_v, [])
        late_u, late_v = [], []
    else:
        blocks = count
        now, kept = Ring([pivot_u, pivot_v], ring, "rows"), []
        for number in range(1, last + 1):
            now.step(number)
            if 1 < number < last:
                kept[0] = now.tie(kept[0], number, (0,))
                if number == 2:
                    start = now.tie(start, number, (1,))
            if number == last:
                places = [last]
                late_u, late_v = now.found[0][last], now.found[1][last]
            else:
                places = sorted({number, count - number} | ({0} if number == 1 else set()))
                new_u, new_v = ([now.found[t][p] for p in places] for t in range(2))
                kept = list(gathered(places, count, new_u, new_v, kept))
        sampled, met, u_all = kept
    sampled, u_all = run(
        functools.partial(sampled_kernel, places, blocks), [info], [sampled, sampler_t, *late_u, u_all],
        [((pivots, priors, width, width), BF16), ((pivots, priors, order, width), BF16)], [], 16, square * order,
        "sampled", {3 + len(late_u): 1}
    )
    cross_other, give = updated(False, sampled, met)
    recv = lax.ppermute(give, "cols", swap)
    cross_own, keep = updated(True, sampled, met)
    sent = (keep + recv.astype(F32)).astype(BF16)
    parts = [keep, recv, *(shifted(sent, shift) for shift in range(1, pairs))]
    qt, rows, given = run(
        orthonormal_kernel, [info], [start, *parts],
        [((width, order), BF16), ((share, width), F32), ((share, width), F32)], [tall, matrix], 16,
        128 * square * order, "orthonormal"
    )
    qt_other = lax.ppermute(qt, "cols", swap)
    rows_other = lax.ppermute(given, "cols", swap)
    give_a, keep_a = projected(True, qt, cross_own)
    qt_other, give_a, keep_a = lax.optimization_barrier((qt_other, give_a, keep_a))
    give_b, keep_b = projected(False, qt_other, cross_other)
    give_a, give_b = lax.ppermute(give_a, "cols", swap), lax.ppermute(give_b, "cols", swap)

    sent = run(
        halve_kernel, [info], [keep_b, keep_a, give_a, give_b], [((pivots, share, width), BF16)] * (pairs - 1), [], 8,
        square, "halve"
    )
    rows, qt, *sent = lax.optimization_barrier((rows, qt, *sent))
    recv = [shifted(each, shift) for shift, each in enumerate(sent, 1)]
    (coeff,) = run(
        own_kernel, [info], [qt, qt_other, keep_b, keep_a, give_a, give_b], [((pivots, share, width), F32)],
        [pltpu.VMEM((pivots, order, width), BF16), pltpu.VMEM((pivots, share, width), BF16), pltpu.SemaphoreType.DMA((4,))],
        12, 4 * square * order, "own", apart=[orig_u, orig_v]
    )
    for each in recv:
        coeff = coeff - jnp.where(core == 0, each[::-1], each).astype(F32)
    basis = placed(rows, rows_other)
    return (basis[:, None], coeff[:, None])


def solution(mesh):
    placed = (
        P("rows", "cols", None, None),
        P("rows", "cols", None, None),
        P("rows", "cols"),
        P(None, "cols", "rows", None),
        P(None, "cols", "rows", None),
        P(None, "cols"),
        P(None, "rows", None, None),
        P(None, "rows", None, None),
        P(),
    )
    return jax.shard_map(
        body,
        mesh=mesh,
        in_specs=placed,
        out_specs=(P(None, "rows", "cols", None), P(None, "rows", "cols", None)),
        check_vma=False,
    )
```

```python
import functools
import math

import jax
import jax.numpy as jnp
import numpy as np
from jax import lax
from jax.experimental import pallas as pl
from jax.experimental.pallas import tpu as pltpu
from jax.sharding import PartitionSpec as P

F32 = jnp.float32
BF16 = jnp.bfloat16
BLOCK = 32
SUB = 8
RING_MOST = 16
MIB = 1 << 20


def dot(a, b):
    return lax.dot_general(a, b, (((1,), (0,)), ((), ())), preferred_element_type=F32)


def dot00(a, b):
    return lax.dot_general(a, b, (((0,), (0,)), ((), ())), preferred_element_type=F32)


def dot11(a, b):
    return lax.dot_general(a, b, (((1,), (1,)), ((), ())), preferred_element_type=F32)


def split3(x):
    high = x.astype(BF16)
    rest = x - high.astype(F32)
    mid = rest.astype(BF16)
    low = (rest - mid.astype(F32)).astype(BF16)
    return high, mid, low


def eliminate(panel, first):
    rows, width = panel.shape
    lanes = 128
    tile = (SUB, lanes)
    lane = lax.broadcasted_iota(jnp.int32, tile, 1)
    sub = lax.broadcasted_iota(jnp.int32, tile, 0)
    high = rows // SUB
    halves = width // lanes
    part = [
        [panel[v * SUB : (v + 1) * SUB, h * lanes : (h + 1) * lanes] for h in range(halves)]
        for v in range(high)
    ]
    mine, start = first // lanes, first % lanes
    scales = []
    for top in range(high):
        at = start + top * SUB
        inside = (lane >= at) & (lane < at + SUB)
        column = [
            [jnp.broadcast_to(part[v][mine][:, at + m : at + m + 1], tile) for v in range(top, high)]
            for m in range(SUB)
        ]
        small = [
            [jnp.broadcast_to(column[b][0][a : a + 1, :], tile) for b in range(a + 1)] for a in range(SUB)
        ]
        row = []
        for a in range(SUB):
            row.append([jnp.broadcast_to(part[top][h][a : a + 1, :], tile) for h in range(halves)])
            row[a][mine] = jnp.where(inside, jnp.where(lane == at + a, 1.0, 0.0), row[a][mine])
        pivots = small[0][0]
        factor = []
        for m in range(SUB):
            inverse = pl.reciprocal(small[m][m], approx=True)
            if m:
                pivots = jnp.where(sub == m, small[m][m], pivots)
            for a in range(m + 1, SUB):
                ratio = small[a][m] * inverse
                for b in range(m + 1, a + 1):
                    small[a][b] = small[a][b] - ratio * small[b][m]
                row[a] = [x - ratio * y for x, y in zip(row[a], row[m])]
            factor.append([c * inverse for c in column[m][1:]])
            for b in range(m + 1, SUB):
                column[b][1:] = [c - f * small[b][m] for c, f in zip(column[b][1:], factor[m])]
        for v in range(top + 1, high):
            for h in range(halves):
                value = jnp.where(inside, 0.0, part[v][h]) if h == mine else part[v][h]
                for m in range(SUB):
                    value = value - factor[m][v - top - 1] * row[m][h]
                part[v][h] = value
        for h in range(halves):
            value = row[0][h]
            for m in range(1, SUB):
                value = jnp.where(sub == m, row[m][h], value)
            part[top][h] = value
        scales.append(lax.rsqrt(pivots))
    done = []
    for v in range(high):
        cells = []
        for h in range(halves):
            value = part[v][h] * scales[v]
            if h == mine:
                value = jnp.where((lane > start + v * SUB + sub) & (lane < start + rows), 0.0, value)
            cells.append(value)
        done.append(jnp.concatenate(cells, 1))
    return jnp.concatenate(done, 0)


def invert_blocks(work, begin, end):
    width = work.shape[0]
    lane = lax.broadcasted_iota(jnp.int32, (1, width), 1)
    for first in range(begin, end, BLOCK):
        last = first + BLOCK
        panel = eliminate(work[first:last, :], first)
        work[first:last, :] = panel
        if last < width:
            base = last // 128 * 128
            high, mid, low = split3(panel)
            left = jnp.concatenate([high, high, mid, mid, high, low], 0)[:, base:]
            right = jnp.concatenate([high, mid, high, mid, low, high], 0)
            update = dot00(left, right)[last - base :, :]
            inside = (lane >= first) & (lane < last)
            work[last:, :] = jnp.where(inside, 0.0, work[last:, :]) - update


def orthonormal_kernel(info, start, *refs):
    parts, (qt, given, basis, yt, work, rows, sem) = refs[:-7], refs[-7:]
    width, order = yt.shape
    core = info[0]
    total = start[...]
    for part in parts:
        total = total - part[...].astype(F32)
    yt[...] = total
    high, mid, low = split3(yt[...])
    cross = dot11(high, mid) + dot11(high, low)
    work[...] = dot11(high, high) + (cross + cross.T + dot11(mid, mid))
    invert_blocks(work, 0, width)
    row = lax.broadcasted_iota(jnp.int32, (width, width), 0)
    col = lax.broadcasted_iota(jnp.int32, (width, width), 1)
    m_high, m_low, _ = split3(jnp.where(col <= row, work[...], 0.0))
    high, mid, _ = split3(yt[...])
    product = dot(m_high, high) + (dot(m_high, mid) + dot(m_low, high))
    yt[...] = product
    share = given.shape[0]

    def rows_at(index):
        return yt[:, pl.ds(pl.multiple_of(index * share, 128), share)].T * math.sqrt(order)

    rows[...] = rows_at(info[1])
    copy = pltpu.make_async_copy(rows, basis.at[core], sem.at[0])
    copy.start()
    given[...] = rows_at(info[1] + 1 - 2 * core)
    qt[...] = product.astype(BF16)
    copy.wait()


def place_kernel(info, given, basis, out, sem):
    copy = pltpu.make_async_copy(given, out.at[1 - info[0]], sem.at[0])
    copy.start()
    copy.wait()


def gather_kernel(places, blocks, info, panel_vt, sampler_t, *refs):
    new = len(places)
    u, v = refs[:new], refs[new : 2 * new]
    kept = refs[2 * new : -3]
    sampled, met, u_all = refs[-3:]
    pivots, priors, order, width = u_all.shape
    slab = order // blocks
    spans = [pl.ds(pl.multiple_of(info[2 + p] * slab, 128), slab) for p in places]
    drawn = jnp.concatenate([sampler_t[:, span] for span in spans], 1)
    for j in range(priors):
        left = jnp.concatenate([panel_vt[j, :, span] for span in spans], 1)
        for c in range(pivots):
            u_new = jnp.concatenate([block[c, j] for block in u], 0)
            v_new = jnp.concatenate([block[c, j] for block in v], 0)
            one, two = dot(drawn, u_new), dot(left, v_new)
            if kept:
                one, two = one + kept[0][c, j], two + kept[1][c, j]
            sampled[c, j] = one
            met[c, j] = two
            for n, p in enumerate(places):
                u_all[c, j, p * slab : (p + 1) * slab, :] = u_new[n * slab : (n + 1) * slab, :]


def sampled_kernel(places, blocks, info, sampled, sampler_t, *refs):
    late, (out, u_all) = refs[: len(refs) - 3], refs[-2:]
    slab = sampler_t.shape[1] // blocks
    for c in range(out.shape[0]):
        for j in range(out.shape[1]):
            total = sampled[c, j]
            for place in places:
                span = pl.ds(pl.multiple_of(info[2 + place] * slab, 128), slab)
                total += dot(sampler_t[:, span], late[c][j])
                u_all[c, j, place * slab : (place + 1) * slab, :] = late[c][j]
            out[c, j] = total.astype(BF16)


def update_kernel(own_column, places, blocks, info, panel_rank, pivot_rank, sampled, met, panel_u, panel_vt, *refs):
    late, (cross, out) = refs[:-2], refs[-2:]
    priors, width, _ = cross.shape
    slab = panel_vt.shape[2] // blocks
    column = info[0] if own_column else 1 - info[0]
    row = lax.broadcasted_iota(jnp.int32, (width, width), 0)
    col = lax.broadcasted_iota(jnp.int32, (width, width), 1)
    terms = []
    for j in range(priors):
        two = met[column, j]
        for place in places:
            span = pl.ds(pl.multiple_of(info[2 + place] * slab, 128), slab)
            two += dot(panel_vt[j, :, span], jnp.where(column == 0, late[0][j], late[1][j]))
        inside = (row < panel_rank[0, j]) & (col < pivot_rank[column, j])
        cross[j] = jnp.where(inside, two, 0.0).astype(BF16)
        terms.append(dot11(sampled[column, j], cross[j]).astype(BF16))
    half = out.shape[1] // 2
    for at in (0, half):
        total = jnp.zeros((width, half), F32)
        for j in range(priors):
            total += dot11(terms[j], panel_u[j, at : at + half, :])
        out[:, at : at + half] = total.astype(out.dtype)


def project_kernel(blocks, own_column, info, qt, panel_u, cross, u_all, orig_u, give, keep, left, work, u_buf, sem):
    _, priors, order, width = u_all.shape
    slab = order // blocks
    pairs, share, _ = keep.shape
    core = info[0]
    column = core if own_column else 1 - core
    copy = pltpu.make_async_copy(orig_u.at[column], u_buf, sem.at[0])
    copy.start()
    mids = []
    for j in range(priors):
        inner = dot(qt[...], panel_u[j]).astype(BF16)
        mids.append(dot(inner, cross[j]).astype(BF16))
    some = max(1, blocks // 2)
    for begin in range(0, blocks, some):
        total = jnp.zeros((some * slab, width), F32)
        for j in range(priors):
            total += dot11(u_all[column, j, begin * slab : (begin + some) * slab, :], mids[j])
        for n in range(some):
            place = pl.ds(pl.multiple_of(info[2 + begin + n] * slab, SUB), slab)
            work[place, :] = total[n * slab : (n + 1) * slab, :]
    for a in range(pairs):
        for out, which in ((give, 1 - core), (keep, core)):
            place = pl.ds(pl.multiple_of((2 * a + which) * share, SUB), share)
            out[a] = work[place, :].astype(out.dtype)
    copy.wait()
    left[...] = dot(qt[...], u_buf[...]).astype(BF16)


def halve_kernel(info, keep_b, keep_a, give_a, give_b, *sent):
    pairs = keep_a.shape[0]
    for shift in range(1, pairs):
        a = lax.rem(info[1] // 2 + shift, pairs)
        for column, keep, recv in ((1 - info[0], keep_b, give_a), (info[0], keep_a, give_b)):
            sent[shift - 1][column] = (keep[a] + recv[a].astype(F32)).astype(BF16)


def own_kernel(info, left_b, left_a, keep_b, keep_a, give_a, give_b, orig_v, out, v_buf, sems):
    share = out.shape[1]
    pair = info[1] // 2
    rows = pl.ds(pl.multiple_of(info[1] * share, 16), share)
    work = ((1 - info[0], left_b, keep_b, give_a), (info[0], left_a, keep_a, give_b))
    copies = [
        pltpu.make_async_copy(orig_v.at[column, rows], v_buf.at[n], sems.at[n]) for n, (column, *_) in enumerate(work)
    ]
    for copy in copies:
        copy.start()
    for n, (column, left, keep, recv) in enumerate(work):
        copies[n].wait()
        out[column] = dot11(v_buf[n], left[...]) - (keep[pair] + recv[pair].astype(F32))


def turn_kernel(panel_v, sampler, panel_vt, sampler_t):
    sampler_t[...] = sampler[...].T
    for j in range(panel_v.shape[0]):
        panel_vt[j] = panel_v[j].T


def start_kernel(info, sampler_t, orig_u, orig_v, out):
    core = info[0]
    proj = dot(sampler_t[...], orig_v[core]).astype(BF16)
    out[...] = dot11(proj, orig_u[core])


def run(kernel, scalars, arrays, outs, scratch, limit, flops, name, aliases={}, apart=(), away=0):
    smem = pl.BlockSpec(memory_space=pltpu.SMEM)
    vmem = pl.BlockSpec(memory_space=pltpu.VMEM)
    shapes = [jax.ShapeDtypeStruct(*o) for o in outs]
    moved = sum(a.size * a.dtype.itemsize for a in list(arrays) + shapes)
    return pl.pallas_call(
        kernel,
        out_shape=shapes,
        in_specs=[smem] * len(scalars) + [vmem] * len(arrays) + [pl.BlockSpec(memory_space=pl.ANY)] * len(apart),
        out_specs=[vmem] * (len(shapes) - away) + [pl.BlockSpec(memory_space=pl.ANY)] * away,
        scratch_shapes=scratch,
        input_output_aliases=aliases,
        compiler_params=pltpu.CompilerParams(vmem_limit_bytes=limit * MIB),
        cost_estimate=pl.CostEstimate(flops=flops, bytes_accessed=moved, transcendentals=0),
        name=name,
    )(*scalars, *arrays, *apart)


def ring_order(count):
    if count % 2:
        return list(range(count))
    return list(range(0, count, 2)) + list(range(count - 1, 0, -2))


class Ring:
    def __init__(self, arrays, order, axis):
        count = len(order)
        self.count, self.axis, self.near = count, axis, (count - 1) // 2
        self.ahead = [(order[(p + 1) % count], order[p]) for p in range(count)]
        self.behind = [(order[p], order[(p + 1) % count]) for p in range(count)]
        self.found = [{0: a} for a in arrays]
        self.up, self.down = list(arrays), list(arrays)

    def step(self, number):
        for t in range(2):
            found = self.found[t]
            if number <= self.near:
                self.up[t] = found[number] = lax.ppermute(self.up[t], self.axis, self.ahead)
                self.down[t] = found[self.count - number] = lax.ppermute(self.down[t], self.axis, self.behind)
            else:
                found[number] = [
                    lax.ppermute(self.up[t][0], self.axis, self.ahead),
                    lax.ppermute(self.down[t][1], self.axis, self.behind),
                ]

    def tie(self, value, number, which=(0, 1)):
        lists = [(self.up, t, number) for t in which if number <= self.near or t == 0]
        lists += [(self.down, t, self.count - number) for t in which if number <= self.near or t == 1]
        value, *held = lax.optimization_barrier((value, *(way[t] for way, t, _ in lists)))
        for (way, t, place), block in zip(lists, held):
            way[t] = self.found[t][place] = block
        return value


def body(panel_u, panel_v, panel_rank, pivot_u, pivot_v, pivot_rank, orig_u, orig_v, sampler):
    order, width = panel_u.shape[2:]
    priors = panel_u.shape[1]
    pivots = pivot_u.shape[0]
    count = lax.axis_size("rows")
    cols = lax.axis_size("cols")
    pairs = cols // 2
    half, share = order // 2, order // cols
    me = lax.axis_index("cols")
    core, pair = me % 2, me // 2
    swap = [(i, i ^ 1) for i in range(cols)]

    ring = ring_order(count)
    place = np.argsort(np.array(ring))
    table = np.array([[ring[(place[r] + d) % count] for d in range(count)] for r in range(count)], np.int32)
    last = count // 2
    whole = count % 2 == 1 or last < 4 or count > RING_MOST
    if whole:
        table = np.zeros((count, 1), np.int32)
    sources = jnp.asarray(table)[lax.axis_index("rows")]
    info = jnp.concatenate([jnp.stack([core, me]).astype(jnp.int32), sources])

    panel_u, panel_v, orig_u, orig_v = panel_u[0], panel_v[0], orig_u[:, 0], orig_v[:, 0]
    square = 2 * width * width
    panel_vt, sampler_t = run(
        turn_kernel, [], [panel_v, sampler], [((priors, width, order), BF16), ((sampler.shape[1], order), BF16)], [], 12,
        10 * square * order, "turn"
    )
    (start,) = run(
        start_kernel, [info], [sampler_t, orig_u, orig_v], [((width, order), F32)], [], 12,
        2 * square * order, "start"
    )

    def shifted(x, shift):
        return lax.ppermute(x, "cols", [(i, (i + 2 * shift) % cols) for i in range(cols)])

    matrix = pltpu.VMEM((width, width), F32)
    tall = pltpu.VMEM((width, order), F32)

    def gathered(places, blocks, new_u, new_v, kept):
        new = len(places)
        shapes = [
            ((pivots, priors, width, width), F32), ((pivots, priors, width, width), F32),
            ((pivots, priors, order, width), BF16)
        ]
        first = 3 + 2 * new
        return run(
            functools.partial(gather_kernel, places, blocks), [info], [panel_vt, sampler_t, *new_u, *new_v, *kept],
            shapes, [], 28, 2 * pivots * priors * square * order * new // blocks, "gather",
            {first + n: n for n in range(len(kept))}
        )

    def updated(own_column, sampled, met):
        return run(
            functools.partial(update_kernel, own_column, places, blocks), [info, panel_rank, pivot_rank],
            [sampled, met, panel_u, panel_vt, *late_v],
            [((priors, width, width), BF16), ((width, order), F32 if own_column else BF16)], [], 20,
            2 * priors * square * (order + width), "update"
        )

    def projected(own_column, qt, cross):
        return run(
            functools.partial(project_kernel, blocks, own_column), [info], [qt, panel_u, cross, u_all],
            [((pairs, share, width), BF16), ((pairs, share, width), F32), ((width, width), BF16)],
            [pltpu.VMEM((order, width), F32), pltpu.VMEM((order, width), BF16), pltpu.SemaphoreType.DMA((1,))],
            20, 3 * priors * square * (2 * order + width), "project", apart=[orig_u]
        )

    if whole:
        blocks, places = 1, []
        new_u, new_v = ([lax.all_gather(x, "rows", axis=2, tiled=True)] for x in (pivot_u, pivot_v))
        sampled, met, u_all = gathered([0], 1, new_u, new_v, [])
        late_u, late_v = [], []
    else:
        blocks = count
        now, kept = Ring([pivot_u, pivot_v], ring, "rows"), []
        for number in range(1, last + 1):
            now.step(number)
            if 1 < number < last:
                kept[0] = now.tie(kept[0], number, (0,))
                if number == 2:
                    start = now.tie(start, number, (1,))
            if number == last:
                places = [last]
                late_u, late_v = now.found[0][last], now.found[1][last]
            else:
                places = sorted({number, count - number} | ({0} if number == 1 else set()))
                new_u, new_v = ([now.found[t][p] for p in places] for t in range(2))
                kept = list(gathered(places, count, new_u, new_v, kept))
        sampled, met, u_all = kept
    sampled, u_all = run(
        functools.partial(sampled_kernel, places, blocks), [info], [sampled, sampler_t, *late_u, u_all],
        [((pivots, priors, width, width), BF16), ((pivots, priors, order, width), BF16)], [], 16, square * order,
        "sampled", {3 + len(late_u): 1}
    )
    cross_other, give = updated(False, sampled, met)
    recv = lax.ppermute(give, "cols", swap)
    cross_own, keep = updated(True, sampled, met)
    sent = (keep + recv.astype(F32)).astype(BF16)
    parts = [keep, recv, *(shifted(sent, shift) for shift in range(1, pairs))]
    qt, given, basis = run(
        orthonormal_kernel, [info], [start, *parts],
        [((width, order), BF16), ((share, width), F32), ((pivots, share, width), F32)],
        [tall, matrix, pltpu.VMEM((share, width), F32), pltpu.SemaphoreType.DMA((1,))], 16,
        128 * square * order, "orthonormal", away=1
    )
    qt_other = lax.ppermute(qt, "cols", swap)
    give_a, keep_a, left_a = projected(True, qt, cross_own)
    qt_other, give_a, keep_a = lax.optimization_barrier((qt_other, give_a, keep_a))
    give_b, keep_b, left_b = projected(False, qt_other, cross_other)
    give_a, give_b = lax.ppermute(give_a, "cols", swap), lax.ppermute(give_b, "cols", swap)
    sent = run(
        halve_kernel, [info], [keep_b, keep_a, give_a, give_b], [((pivots, share, width), BF16)] * (pairs - 1), [], 8,
        square, "halve"
    )
    left_b, *sent = lax.optimization_barrier((left_b, *sent))
    recv = [shifted(each, shift) for shift, each in enumerate(sent, 1)]
    (coeff,) = run(
        own_kernel, [info], [left_b, left_a, keep_b, keep_a, give_a, give_b], [((pivots, share, width), F32)],
        [pltpu.VMEM((pivots, share, width), BF16), pltpu.SemaphoreType.DMA((2,))], 8, square * width, "own", apart=[orig_v]
    )
    (basis,) = run(
        place_kernel, [info], [lax.ppermute(given, "cols", swap)], [((pivots, share, width), F32)],
        [pltpu.SemaphoreType.DMA((1,))], 4, 1, "place", {2: 0}, [basis], 1
    )
    for each in recv:
        coeff = coeff - each.astype(F32)
    return (basis[:, None], coeff[:, None])


def solution(mesh):
    placed = (
        P("rows", "cols", None, None),
        P("rows", "cols", None, None),
        P("rows", "cols"),
        P(None, "cols", "rows", None),
        P(None, "cols", "rows", None),
        P(None, "cols"),
        P(None, "rows", None, None),
        P(None, "rows", None, None),
        P(),
    )
    return jax.shard_map(
        body,
        mesh=mesh,
        in_specs=placed,
        out_specs=(P(None, "rows", "cols", None), P(None, "rows", "cols", None)),
        check_vma=False,
    )
```

```python
import functools
import math

import jax
import jax.numpy as jnp
import numpy as np
from jax import lax
from jax.experimental import pallas as pl
from jax.experimental.pallas import tpu as pltpu
from jax.sharding import PartitionSpec as P

F32 = jnp.float32
BF16 = jnp.bfloat16
BLOCK = 32
SUB = 8
RING_MOST = 16
MIB = 1 << 20


def dot(a, b):
    return lax.dot_general(a, b, (((1,), (0,)), ((), ())), preferred_element_type=F32)


def dot00(a, b):
    return lax.dot_general(a, b, (((0,), (0,)), ((), ())), preferred_element_type=F32)


def dot11(a, b):
    return lax.dot_general(a, b, (((1,), (1,)), ((), ())), preferred_element_type=F32)


def split3(x):
    high = x.astype(BF16)
    rest = x - high.astype(F32)
    mid = rest.astype(BF16)
    low = (rest - mid.astype(F32)).astype(BF16)
    return high, mid, low


def eliminate(panel, first):
    rows, width = panel.shape
    lanes = 128
    tile = (SUB, lanes)
    lane = lax.broadcasted_iota(jnp.int32, tile, 1)
    sub = lax.broadcasted_iota(jnp.int32, tile, 0)
    high = rows // SUB
    halves = width // lanes
    part = [
        [panel[v * SUB : (v + 1) * SUB, h * lanes : (h + 1) * lanes] for h in range(halves)]
        for v in range(high)
    ]
    mine, start = first // lanes, first % lanes
    scales = []
    for top in range(high):
        at = start + top * SUB
        inside = (lane >= at) & (lane < at + SUB)
        column = [
            [jnp.broadcast_to(part[v][mine][:, at + m : at + m + 1], tile) for v in range(top, high)]
            for m in range(SUB)
        ]
        small = [
            [jnp.broadcast_to(column[b][0][a : a + 1, :], tile) for b in range(a + 1)] for a in range(SUB)
        ]
        row = []
        for a in range(SUB):
            row.append([jnp.broadcast_to(part[top][h][a : a + 1, :], tile) for h in range(halves)])
            row[a][mine] = jnp.where(inside, jnp.where(lane == at + a, 1.0, 0.0), row[a][mine])
        pivots = small[0][0]
        factor = []
        for m in range(SUB):
            inverse = pl.reciprocal(small[m][m], approx=True)
            if m:
                pivots = jnp.where(sub == m, small[m][m], pivots)
            for a in range(m + 1, SUB):
                ratio = small[a][m] * inverse
                for b in range(m + 1, a + 1):
                    small[a][b] = small[a][b] - ratio * small[b][m]
                row[a] = [x - ratio * y for x, y in zip(row[a], row[m])]
            factor.append([c * inverse for c in column[m][1:]])
            for b in range(m + 1, SUB):
                column[b][1:] = [c - f * small[b][m] for c, f in zip(column[b][1:], factor[m])]
        for v in range(top + 1, high):
            for h in range(halves):
                value = jnp.where(inside, 0.0, part[v][h]) if h == mine else part[v][h]
                for m in range(SUB):
                    value = value - factor[m][v - top - 1] * row[m][h]
                part[v][h] = value
        for h in range(halves):
            value = row[0][h]
            for m in range(1, SUB):
                value = jnp.where(sub == m, row[m][h], value)
            part[top][h] = value
        scales.append(lax.rsqrt(pivots))
    done = []
    for v in range(high):
        cells = []
        for h in range(halves):
            value = part[v][h] * scales[v]
            if h == mine:
                value = jnp.where((lane > start + v * SUB + sub) & (lane < start + rows), 0.0, value)
            cells.append(value)
        done.append(jnp.concatenate(cells, 1))
    return jnp.concatenate(done, 0)


def invert_blocks(work, begin, end):
    width = work.shape[0]
    lane = lax.broadcasted_iota(jnp.int32, (1, width), 1)
    for first in range(begin, end, BLOCK):
        last = first + BLOCK
        panel = eliminate(work[first:last, :], first)
        work[first:last, :] = panel
        if last < width:
            base = last // 128 * 128
            high, mid, low = split3(panel)
            left = jnp.concatenate([high, high, mid, mid, high, low], 0)[:, base:]
            right = jnp.concatenate([high, mid, high, mid, low, high], 0)
            update = dot00(left, right)[last - base :, :]
            inside = (lane >= first) & (lane < last)
            work[last:, :] = jnp.where(inside, 0.0, work[last:, :]) - update


def orthonormal_kernel(sums, info, start, *refs):
    parts, (qt, given, basis, yt, work, rows, sem) = refs[:-7], refs[-7:]
    width, order = yt.shape
    core = info[0]
    for c in range(len(parts) // sums):
        @pl.when(core == c)
        def _():
            total = start[...]
            for part in parts[c * sums : (c + 1) * sums]:
                total = total - part[...].astype(F32)
            yt[...] = total
    high, mid, low = split3(yt[...])
    cross = dot11(high, mid) + dot11(high, low)
    work[...] = dot11(high, high) + (cross + cross.T + dot11(mid, mid))
    invert_blocks(work, 0, width)
    row = lax.broadcasted_iota(jnp.int32, (width, width), 0)
    col = lax.broadcasted_iota(jnp.int32, (width, width), 1)
    m_high, m_low, _ = split3(jnp.where(col <= row, work[...], 0.0))
    high, mid, _ = split3(yt[...])
    product = dot(m_high, high) + (dot(m_high, mid) + dot(m_low, high))
    yt[...] = product
    share = given.shape[0]

    def rows_at(index):
        return yt[:, pl.ds(pl.multiple_of(index * share, 128), share)].T * math.sqrt(order)

    rows[...] = rows_at(info[1])
    copy = pltpu.make_async_copy(rows, basis.at[core], sem.at[0])
    copy.start()
    given[...] = rows_at(info[1] + 1 - 2 * core)
    qt[...] = product.astype(BF16)
    copy.wait()


def place_kernel(info, given, basis, out, sem):
    copy = pltpu.make_async_copy(given, out.at[1 - info[0]], sem.at[0])
    copy.start()
    copy.wait()


def gather_kernel(places, blocks, info, panel_vt, sampler_t, *refs):
    new = len(places)
    u, v = refs[:new], refs[new : 2 * new]
    kept = refs[2 * new : -3]
    sampled, met, u_all = refs[-3:]
    pivots, priors, order, width = u_all.shape
    slab = order // blocks
    spans = [pl.ds(pl.multiple_of(info[2 + p] * slab, 128), slab) for p in places]
    drawn = jnp.concatenate([sampler_t[:, span] for span in spans], 1)
    for j in range(priors):
        left = jnp.concatenate([panel_vt[j, :, span] for span in spans], 1)
        for c in range(pivots):
            u_new = jnp.concatenate([block[c, j] for block in u], 0)
            v_new = jnp.concatenate([block[c, j] for block in v], 0)
            one, two = dot(drawn, u_new), dot(left, v_new)
            if kept:
                one, two = one + kept[0][c, j], two + kept[1][c, j]
            sampled[c, j] = one
            met[c, j] = two
            for n, p in enumerate(places):
                u_all[c, j, p * slab : (p + 1) * slab, :] = u_new[n * slab : (n + 1) * slab, :]


def update_kernel(c, place, blocks, info, panel_rank, pivot_rank, sampled, met, panel_u, panel_vt, sampler_t, u_all, *refs):
    cross, u_out, give, keep = refs[-4:]
    _, priors, width, _ = cross.shape
    slab = panel_vt.shape[2] // blocks
    row = lax.broadcasted_iota(jnp.int32, (width, width), 0)
    col = lax.broadcasted_iota(jnp.int32, (width, width), 1)
    terms = []
    for j in range(priors):
        one, two = sampled[c, j], met[c, j]
        if place is not None:
            span = pl.ds(pl.multiple_of(info[2 + place] * slab, 128), slab)
            one += dot(sampler_t[:, span], refs[0][j])
            two += dot(panel_vt[j, :, span], refs[1][j])
            u_out[c, j, place * slab : (place + 1) * slab, :] = refs[0][j]
        inside = (row < panel_rank[0, j]) & (col < pivot_rank[c, j])
        cross[c, j] = jnp.where(inside, two, 0.0).astype(BF16)
        terms.append(dot11(one.astype(BF16), cross[c, j]).astype(BF16))
    half = keep.shape[1] // 2
    for at in (0, half):
        total = jnp.zeros((width, half), F32)
        for j in range(priors):
            total += dot11(terms[j], panel_u[j, at : at + half, :])
        keep[:, at : at + half] = total
        give[:, at : at + half] = total.astype(BF16)


def project_kernel(blocks, own_column, info, qt, panel_u, cross, u_all, orig_u, give, keep, left, work, u_buf, sem):
    _, priors, order, width = u_all.shape
    slab = order // blocks
    pairs, share, _ = keep.shape
    core = info[0]
    column = core if own_column else 1 - core
    copy = pltpu.make_async_copy(orig_u.at[column], u_buf, sem.at[0])
    copy.start()
    mids = []
    for j in range(priors):
        inner = dot(qt[...], panel_u[j]).astype(BF16)
        mids.append(dot(inner, cross[column, j]).astype(BF16))
    some = max(1, blocks // 2)
    for begin in range(0, blocks, some):
        total = jnp.zeros((some * slab, width), F32)
        for j in range(priors):
            total += dot11(u_all[column, j, begin * slab : (begin + some) * slab, :], mids[j])
        for n in range(some):
            place = pl.ds(pl.multiple_of(info[2 + begin + n] * slab, SUB), slab)
            work[place, :] = total[n * slab : (n + 1) * slab, :]
    for a in range(pairs):
        for out, which in ((give, 1 - core), (keep, core)):
            place = pl.ds(pl.multiple_of((2 * a + which) * share, SUB), share)
            out[a] = work[place, :].astype(out.dtype)
    copy.wait()
    left[...] = dot(qt[...], u_buf[...]).astype(BF16)


def halve_kernel(info, keep_b, keep_a, give_a, give_b, *sent):
    pairs = keep_a.shape[0]
    for shift in range(1, pairs):
        a = lax.rem(info[1] // 2 + shift, pairs)
        for column, keep, recv in ((1 - info[0], keep_b, give_a), (info[0], keep_a, give_b)):
            sent[shift - 1][column] = (keep[a] + recv[a].astype(F32)).astype(BF16)


def own_kernel(info, left_b, left_a, keep_b, keep_a, give_a, give_b, orig_v, out, v_buf, sems):
    share = out.shape[1]
    pair = info[1] // 2
    rows = pl.ds(pl.multiple_of(info[1] * share, 16), share)
    work = ((1 - info[0], left_b, keep_b, give_a), (info[0], left_a, keep_a, give_b))
    copies = [
        pltpu.make_async_copy(orig_v.at[column, rows], v_buf.at[n], sems.at[n]) for n, (column, *_) in enumerate(work)
    ]
    for copy in copies:
        copy.start()
    for n, (column, left, keep, recv) in enumerate(work):
        copies[n].wait()
        out[column] = dot11(v_buf[n], left[...]) - (keep[pair] + recv[pair].astype(F32))


def turn_kernel(panel_v, sampler, panel_vt, sampler_t):
    sampler_t[...] = sampler[...].T
    for j in range(panel_v.shape[0]):
        panel_vt[j] = panel_v[j].T


def start_kernel(info, sampler_t, orig_u, orig_v, out):
    core = info[0]
    proj = dot(sampler_t[...], orig_v[core]).astype(BF16)
    out[...] = dot11(proj, orig_u[core])


def run(kernel, scalars, arrays, outs, scratch, limit, flops, name, aliases={}, apart=(), away=0):
    smem = pl.BlockSpec(memory_space=pltpu.SMEM)
    vmem = pl.BlockSpec(memory_space=pltpu.VMEM)
    shapes = [jax.ShapeDtypeStruct(*o) for o in outs]
    moved = sum(a.size * a.dtype.itemsize for a in list(arrays) + shapes)
    return pl.pallas_call(
        kernel,
        out_shape=shapes,
        in_specs=[smem] * len(scalars) + [vmem] * len(arrays) + [pl.BlockSpec(memory_space=pl.ANY)] * len(apart),
        out_specs=[vmem] * (len(shapes) - away) + [pl.BlockSpec(memory_space=pl.ANY)] * away,
        scratch_shapes=scratch,
        input_output_aliases=aliases,
        compiler_params=pltpu.CompilerParams(vmem_limit_bytes=limit * MIB),
        cost_estimate=pl.CostEstimate(flops=flops, bytes_accessed=moved, transcendentals=0),
        name=name,
    )(*scalars, *arrays, *apart)


def ring_order(count):
    if count % 2:
        return list(range(count))
    return list(range(0, count, 2)) + list(range(count - 1, 0, -2))


class Ring:
    def __init__(self, arrays, order, axis):
        count = len(order)
        self.count, self.axis, self.near = count, axis, (count - 1) // 2
        self.ahead = [(order[(p + 1) % count], order[p]) for p in range(count)]
        self.behind = [(order[p], order[(p + 1) % count]) for p in range(count)]
        self.found = [{0: a} for a in arrays]
        self.up, self.down = list(arrays), list(arrays)

    def step(self, number):
        for t in range(2):
            found = self.found[t]
            if number <= self.near:
                self.up[t] = found[number] = lax.ppermute(self.up[t], self.axis, self.ahead)
                self.down[t] = found[self.count - number] = lax.ppermute(self.down[t], self.axis, self.behind)
            else:
                way, pairs = (self.down, self.behind) if t else (self.up, self.ahead)
                found[number] = [lax.ppermute(way[t][c], self.axis, pairs) for c in range(way[t].shape[0])]

    def tie(self, value, number, which=(0, 1)):
        lists = [(self.up, t, number) for t in which if number <= self.near or t == 0]
        lists += [(self.down, t, self.count - number) for t in which if number <= self.near or t == 1]
        value, *held = lax.optimization_barrier((value, *(way[t] for way, t, _ in lists)))
        for (way, t, place), block in zip(lists, held):
            way[t] = self.found[t][place] = block
        return value


def body(panel_u, panel_v, panel_rank, pivot_u, pivot_v, pivot_rank, orig_u, orig_v, sampler):
    order, width = panel_u.shape[2:]
    priors = panel_u.shape[1]
    pivots = pivot_u.shape[0]
    count = lax.axis_size("rows")
    cols = lax.axis_size("cols")
    pairs = cols // 2
    half, share = order // 2, order // cols
    me = lax.axis_index("cols")
    core, pair = me % 2, me // 2
    swap = [(i, i ^ 1) for i in range(cols)]

    ring = ring_order(count)
    place = np.argsort(np.array(ring))
    table = np.array([[ring[(place[r] + d) % count] for d in range(count)] for r in range(count)], np.int32)
    last = count // 2
    whole = count % 2 == 1 or last < 4 or count > RING_MOST
    if whole:
        table = np.zeros((count, 1), np.int32)
    sources = jnp.asarray(table)[lax.axis_index("rows")]
    info = jnp.concatenate([jnp.stack([core, me]).astype(jnp.int32), sources])

    panel_u, panel_v, orig_u, orig_v = panel_u[0], panel_v[0], orig_u[:, 0], orig_v[:, 0]
    square = 2 * width * width
    panel_vt, sampler_t = run(
        turn_kernel, [], [panel_v, sampler], [((priors, width, order), BF16), ((sampler.shape[1], order), BF16)], [], 12,
        10 * square * order, "turn"
    )
    (start,) = run(
        start_kernel, [info], [sampler_t, orig_u, orig_v], [((width, order), F32)], [], 12,
        2 * square * order, "start"
    )

    def shifted(x, shift, core_of=None):
        return lax.ppermute(
            x, "cols", [(i, (i + 2 * shift) % cols) for i in range(cols) if core_of is None or i % 2 == core_of]
        )

    matrix = pltpu.VMEM((width, width), F32)
    tall = pltpu.VMEM((width, order), F32)

    def gathered(places, blocks, new_u, new_v, kept):
        new = len(places)
        shapes = [
            ((pivots, priors, width, width), F32), ((pivots, priors, width, width), F32),
            ((pivots, priors, order, width), BF16)
        ]
        first = 3 + 2 * new
        return run(
            functools.partial(gather_kernel, places, blocks), [info], [panel_vt, sampler_t, *new_u, *new_v, *kept],
            shapes, [], 28, 2 * pivots * priors * square * order * new // blocks, "gather",
            {first + n: n for n in range(len(kept))}
        )

    def updated(c, u_all, late, cross):
        fixed = 3
        arrays = [sampled, met, panel_u, panel_vt, sampler_t, u_all, *late, *cross]
        aliases = {fixed + 5: 1}
        if cross:
            aliases[fixed + len(arrays) - 1] = 0
        return run(
            functools.partial(update_kernel, c, place, blocks), [info, panel_rank, pivot_rank], arrays,
            [
                ((pivots, priors, width, width), BF16), ((pivots, priors, order, width), BF16), ((width, order), BF16),
                ((width, order), F32)
            ],
            [], 24, 2 * priors * square * (order + width), "update", aliases
        )

    def projected(own_column, qt):
        return run(
            functools.partial(project_kernel, blocks, own_column), [info], [qt, panel_u, cross, u_all],
            [((pairs, share, width), BF16), ((pairs, share, width), F32), ((width, width), BF16)],
            [pltpu.VMEM((order, width), F32), pltpu.VMEM((order, width), BF16), pltpu.SemaphoreType.DMA((1,))],
            20, 3 * priors * square * (2 * order + width), "project", apart=[orig_u]
        )

    if whole:
        blocks, place = 1, None
        new_u, new_v = ([lax.all_gather(x, "rows", axis=2, tiled=True)] for x in (pivot_u, pivot_v))
        sampled, met, u_all = gathered([0], 1, new_u, new_v, [])
        late = [[] for _ in range(pivots)]
    else:
        blocks = count
        now, kept = Ring([pivot_u, pivot_v], ring, "rows"), []
        for number in range(1, last + 1):
            now.step(number)
            if 1 < number < last:
                kept[0] = now.tie(kept[0], number, (0,))
                if number == 2:
                    start = now.tie(start, number, (1,))
            if number == last:
                place = last
                late = list(zip(now.found[0][last], now.found[1][last]))
            else:
                places = sorted({number, count - number} | ({0} if number == 1 else set()))
                new_u, new_v = ([now.found[t][p] for p in places] for t in range(2))
                kept = list(gathered(places, count, new_u, new_v, kept))
        sampled, met, u_all = kept
    cross, parts = [], []
    for c in range(pivots):
        *cross, u_all, give, keep = updated(c, u_all, late[c], cross)
        recv = lax.ppermute(give, "cols", [(i, i ^ 1) for i in range(cols) if i % 2 != c])
        sent = (keep + recv.astype(F32)).astype(BF16)
        parts += [keep, recv, *(shifted(sent, shift, c) for shift in range(1, pairs))]
    (cross,) = cross
    qt, given, basis = run(
        functools.partial(orthonormal_kernel, len(parts) // pivots), [info], [start, *parts],
        [((width, order), BF16), ((share, width), F32), ((pivots, share, width), F32)],
        [tall, matrix, pltpu.VMEM((share, width), F32), pltpu.SemaphoreType.DMA((1,))], 16,
        128 * square * order, "orthonormal", away=1
    )
    qt_other = lax.ppermute(qt, "cols", swap)
    give_a, keep_a, left_a = projected(True, qt)
    qt_other, give_a, keep_a = lax.optimization_barrier((qt_other, give_a, keep_a))
    give_b, keep_b, left_b = projected(False, qt_other)
    give_a, give_b = lax.ppermute(give_a, "cols", swap), lax.ppermute(give_b, "cols", swap)
    sent = run(
        halve_kernel, [info], [keep_b, keep_a, give_a, give_b], [((pivots, share, width), BF16)] * (pairs - 1), [], 8,
        square, "halve"
    )
    left_b, *sent = lax.optimization_barrier((left_b, *sent))
    recv = [shifted(each, shift) for shift, each in enumerate(sent, 1)]
    (coeff,) = run(
        own_kernel, [info], [left_b, left_a, keep_b, keep_a, give_a, give_b], [((pivots, share, width), F32)],
        [pltpu.VMEM((pivots, share, width), BF16), pltpu.SemaphoreType.DMA((2,))], 8, square * width, "own", apart=[orig_v]
    )
    (basis,) = run(
        place_kernel, [info], [lax.ppermute(given, "cols", swap)], [((pivots, share, width), F32)],
        [pltpu.SemaphoreType.DMA((1,))], 4, 1, "place", {2: 0}, [basis], 1
    )
    for each in recv:
        coeff = coeff - each.astype(F32)
    return (basis[:, None], coeff[:, None])


def solution(mesh):
    placed = (
        P("rows", "cols", None, None),
        P("rows", "cols", None, None),
        P("rows", "cols"),
        P(None, "cols", "rows", None),
        P(None, "cols", "rows", None),
        P(None, "cols"),
        P(None, "rows", None, None),
        P(None, "rows", None, None),
        P(),
    )
    return jax.shard_map(
        body,
        mesh=mesh,
        in_specs=placed,
        out_specs=(P(None, "rows", "cols", None), P(None, "rows", "cols", None)),
        check_vma=False,
    )
```

```python
import functools
import math

import jax
import jax.numpy as jnp
import numpy as np
from jax import lax
from jax.experimental import pallas as pl
from jax.experimental.pallas import tpu as pltpu
from jax.sharding import PartitionSpec as P

F32 = jnp.float32
BF16 = jnp.bfloat16
BLOCK = 32
SUB = 8
RING_MOST = 16
MIB = 1 << 20


def dot(a, b):
    return lax.dot_general(a, b, (((1,), (0,)), ((), ())), preferred_element_type=F32)


def dot00(a, b):
    return lax.dot_general(a, b, (((0,), (0,)), ((), ())), preferred_element_type=F32)


def dot11(a, b):
    return lax.dot_general(a, b, (((1,), (1,)), ((), ())), preferred_element_type=F32)


def split3(x):
    high = x.astype(BF16)
    rest = x - high.astype(F32)
    mid = rest.astype(BF16)
    low = (rest - mid.astype(F32)).astype(BF16)
    return high, mid, low


def eliminate(panel, first, store):
    rows, width = panel.shape
    lanes = 128
    tile = (SUB, lanes)
    lane = lax.broadcasted_iota(jnp.int32, tile, 1)
    sub = lax.broadcasted_iota(jnp.int32, tile, 0)
    high = rows // SUB
    halves = width // lanes
    part = [
        [panel[v * SUB : (v + 1) * SUB, h * lanes : (h + 1) * lanes] for h in range(halves)]
        for v in range(high)
    ]
    mine, start = first // lanes, first % lanes
    scales = []
    for top in range(high):
        at = start + top * SUB
        inside = (lane >= at) & (lane < at + SUB)
        column = [
            [jnp.broadcast_to(part[v][mine][:, at + m : at + m + 1], tile) for v in range(top, high)]
            for m in range(SUB)
        ]
        for n, value in enumerate([c[0] for c in column] + part[top]):
            store[top, n * SUB : (n + 1) * SUB, :] = value

        def spread(n, a):
            return jnp.broadcast_to(store[top, n * SUB + a : n * SUB + a + 1, :], tile)

        small = [[spread(b, a) for b in range(a + 1)] for a in range(SUB)]
        row = []
        for a in range(SUB):
            row.append([spread(SUB + h, a) for h in range(halves)])
            row[a][mine] = jnp.where(inside, jnp.where(lane == at + a, 1.0, 0.0), row[a][mine])
        pivots = small[0][0]
        factor = []
        for m in range(SUB):
            inverse = pl.reciprocal(small[m][m], approx=True)
            if m:
                pivots = jnp.where(sub == m, small[m][m], pivots)
            for a in range(m + 1, SUB):
                ratio = small[a][m] * inverse
                for b in range(m + 1, a + 1):
                    small[a][b] = small[a][b] - ratio * small[b][m]
                row[a] = [x - ratio * y for x, y in zip(row[a], row[m])]
            factor.append([c * inverse for c in column[m][1:]])
            for b in range(m + 1, SUB):
                column[b][1:] = [c - f * small[b][m] for c, f in zip(column[b][1:], factor[m])]
        for v in range(top + 1, high):
            for h in range(halves):
                value = jnp.where(inside, 0.0, part[v][h]) if h == mine else part[v][h]
                for m in range(SUB):
                    value = value - factor[m][v - top - 1] * row[m][h]
                part[v][h] = value
        for h in range(halves):
            value = row[0][h]
            for m in range(1, SUB):
                value = jnp.where(sub == m, row[m][h], value)
            part[top][h] = value
        scales.append(lax.rsqrt(pivots))
    done = []
    for v in range(high):
        cells = []
        for h in range(halves):
            value = part[v][h] * scales[v]
            if h == mine:
                value = jnp.where((lane > start + v * SUB + sub) & (lane < start + rows), 0.0, value)
            cells.append(value)
        done.append(jnp.concatenate(cells, 1))
    return jnp.concatenate(done, 0)


def invert_blocks(work, store, begin, end):
    width = work.shape[0]
    lane = lax.broadcasted_iota(jnp.int32, (1, width), 1)
    for first in range(begin, end, BLOCK):
        last = first + BLOCK
        panel = eliminate(work[first:last, :], first, store)
        work[first:last, :] = panel
        if last < width:
            base = last // 128 * 128
            high, mid, low = split3(panel)
            left = jnp.concatenate([high, high, mid, mid, high, low], 0)[:, base:]
            right = jnp.concatenate([high, mid, high, mid, low, high], 0)
            update = dot00(left, right)[last - base :, :]
            inside = (lane >= first) & (lane < last)
            work[last:, :] = jnp.where(inside, 0.0, work[last:, :]) - update


def orthonormal_kernel(info, start, *refs):
    parts, (qt, given, basis, yt, work, store, rows, sem) = refs[:-8], refs[-8:]
    width, order = yt.shape
    core = info[0]
    total = start[...]
    for part in parts:
        total = total - part[...].astype(F32)
    yt[...] = total
    high, mid, low = split3(yt[...])
    cross = dot11(high, mid) + dot11(high, low)
    work[...] = dot11(high, high) + (cross + cross.T + dot11(mid, mid))
    invert_blocks(work, store, 0, width)
    row = lax.broadcasted_iota(jnp.int32, (width, width), 0)
    col = lax.broadcasted_iota(jnp.int32, (width, width), 1)
    m_high, m_low, _ = split3(jnp.where(col <= row, work[...], 0.0))
    high, mid, _ = split3(yt[...])
    product = dot(m_high, high) + (dot(m_high, mid) + dot(m_low, high))
    yt[...] = product
    share = given.shape[0]

    def rows_at(index):
        return yt[:, pl.ds(pl.multiple_of(index * share, 128), share)].T * math.sqrt(order)

    rows[...] = rows_at(info[1])
    copy = pltpu.make_async_copy(rows, basis.at[core], sem.at[0])
    copy.start()
    given[...] = rows_at(info[1] + 1 - 2 * core)
    qt[...] = product.astype(BF16)
    copy.wait()


def place_kernel(info, given, basis, out, sem):
    copy = pltpu.make_async_copy(given, out.at[1 - info[0]], sem.at[0])
    copy.start()
    copy.wait()


def gather_kernel(places, blocks, info, panel_vt, sampler_t, *refs):
    new = len(places)
    u, v = refs[:new], refs[new : 2 * new]
    kept = refs[2 * new : -3]
    sampled, met, u_all = refs[-3:]
    pivots, priors, order, width = u_all.shape
    slab = order // blocks
    spans = [pl.ds(pl.multiple_of(info[2 + p] * slab, 128), slab) for p in places]
    drawn = jnp.concatenate([sampler_t[:, span] for span in spans], 1)
    for j in range(priors):
        left = jnp.concatenate([panel_vt[j, :, span] for span in spans], 1)
        for c in range(pivots):
            u_new = jnp.concatenate([block[c, j] for block in u], 0)
            v_new = jnp.concatenate([block[c, j] for block in v], 0)
            one, two = dot(drawn, u_new), dot(left, v_new)
            if kept:
                one, two = one + kept[0][c, j], two + kept[1][c, j]
            sampled[c, j] = one
            met[c, j] = two
            for n, p in enumerate(places):
                u_all[c, j, p * slab : (p + 1) * slab, :] = u_new[n * slab : (n + 1) * slab, :]


def sampled_kernel(places, blocks, info, sampled, sampler_t, *refs):
    late, (out, u_all) = refs[: len(refs) - 3], refs[-2:]
    slab = sampler_t.shape[1] // blocks
    for c in range(out.shape[0]):
        for j in range(out.shape[1]):
            total = sampled[c, j]
            for place in places:
                span = pl.ds(pl.multiple_of(info[2 + place] * slab, 128), slab)
                total += dot(sampler_t[:, span], late[c][j])
                u_all[c, j, place * slab : (place + 1) * slab, :] = late[c][j]
            out[c, j] = total.astype(BF16)


def update_kernel(own_column, places, blocks, info, panel_rank, pivot_rank, sampled, met, panel_u, panel_vt, *refs):
    late, (cross, out) = refs[:-2], refs[-2:]
    priors, width, _ = cross.shape
    slab = panel_vt.shape[2] // blocks
    column = info[0] if own_column else 1 - info[0]
    row = lax.broadcasted_iota(jnp.int32, (width, width), 0)
    col = lax.broadcasted_iota(jnp.int32, (width, width), 1)
    terms = []
    for j in range(priors):
        two = met[column, j]
        for place in places:
            span = pl.ds(pl.multiple_of(info[2 + place] * slab, 128), slab)
            two += dot(panel_vt[j, :, span], jnp.where(column == 0, late[0][j], late[1][j]))
        inside = (row < panel_rank[0, j]) & (col < pivot_rank[column, j])
        cross[j] = jnp.where(inside, two, 0.0).astype(BF16)
        terms.append(dot11(sampled[column, j], cross[j]).astype(BF16))
    half = out.shape[1] // 2
    for at in (0, half):
        total = jnp.zeros((width, half), F32)
        for j in range(priors):
            total += dot11(terms[j], panel_u[j, at : at + half, :])
        out[:, at : at + half] = total.astype(out.dtype)


def project_kernel(blocks, own_column, info, qt, panel_u, cross, u_all, orig_u, give, keep, left, work, u_buf, sem):
    _, priors, order, width = u_all.shape
    slab = order // blocks
    pairs, share, _ = keep.shape
    core = info[0]
    column = core if own_column else 1 - core
    copy = pltpu.make_async_copy(orig_u.at[column], u_buf, sem.at[0])
    copy.start()
    mids = []
    for j in range(priors):
        inner = dot(qt[...], panel_u[j]).astype(BF16)
        mids.append(dot(inner, cross[j]).astype(BF16))
    some = max(1, blocks // 2)
    for begin in range(0, blocks, some):
        total = jnp.zeros((some * slab, width), F32)
        for j in range(priors):
            total += dot11(u_all[column, j, begin * slab : (begin + some) * slab, :], mids[j])
        for n in range(some):
            place = pl.ds(pl.multiple_of(info[2 + begin + n] * slab, SUB), slab)
            work[place, :] = total[n * slab : (n + 1) * slab, :]
    for a in range(pairs):
        for out, which in ((give, 1 - core), (keep, core)):
            place = pl.ds(pl.multiple_of((2 * a + which) * share, SUB), share)
            out[a] = work[place, :].astype(out.dtype)
    copy.wait()
    left[...] = dot(qt[...], u_buf[...]).astype(BF16)


def halve_kernel(info, keep_b, keep_a, give_a, give_b, *sent):
    pairs = keep_a.shape[0]
    for shift in range(1, pairs):
        a = lax.rem(info[1] // 2 + shift, pairs)
        for column, keep, recv in ((1 - info[0], keep_b, give_a), (info[0], keep_a, give_b)):
            sent[shift - 1][column] = (keep[a] + recv[a].astype(F32)).astype(BF16)


def own_kernel(info, left_b, left_a, keep_b, keep_a, give_a, give_b, orig_v, out, v_buf, sems):
    share = out.shape[1]
    pair = info[1] // 2
    rows = pl.ds(pl.multiple_of(info[1] * share, 16), share)
    work = ((1 - info[0], left_b, keep_b, give_a), (info[0], left_a, keep_a, give_b))
    copies = [
        pltpu.make_async_copy(orig_v.at[column, rows], v_buf.at[n], sems.at[n]) for n, (column, *_) in enumerate(work)
    ]
    for copy in copies:
        copy.start()
    for n, (column, left, keep, recv) in enumerate(work):
        copies[n].wait()
        out[column] = dot11(v_buf[n], left[...]) - (keep[pair] + recv[pair].astype(F32))


def turn_kernel(panel_v, sampler, panel_vt, sampler_t):
    sampler_t[...] = sampler[...].T
    for j in range(panel_v.shape[0]):
        panel_vt[j] = panel_v[j].T


def start_kernel(info, sampler_t, orig_u, orig_v, out):
    core = info[0]
    proj = dot(sampler_t[...], orig_v[core]).astype(BF16)
    out[...] = dot11(proj, orig_u[core])


def run(kernel, scalars, arrays, outs, scratch, limit, flops, name, aliases={}, apart=(), away=0):
    smem = pl.BlockSpec(memory_space=pltpu.SMEM)
    vmem = pl.BlockSpec(memory_space=pltpu.VMEM)
    shapes = [jax.ShapeDtypeStruct(*o) for o in outs]
    moved = sum(a.size * a.dtype.itemsize for a in list(arrays) + shapes)
    return pl.pallas_call(
        kernel,
        out_shape=shapes,
        in_specs=[smem] * len(scalars) + [vmem] * len(arrays) + [pl.BlockSpec(memory_space=pl.ANY)] * len(apart),
        out_specs=[vmem] * (len(shapes) - away) + [pl.BlockSpec(memory_space=pl.ANY)] * away,
        scratch_shapes=scratch,
        input_output_aliases=aliases,
        compiler_params=pltpu.CompilerParams(vmem_limit_bytes=limit * MIB),
        cost_estimate=pl.CostEstimate(flops=flops, bytes_accessed=moved, transcendentals=0),
        name=name,
    )(*scalars, *arrays, *apart)


def ring_order(count):
    if count % 2:
        return list(range(count))
    return list(range(0, count, 2)) + list(range(count - 1, 0, -2))


class Ring:
    def __init__(self, arrays, order, axis):
        count = len(order)
        self.count, self.axis, self.near = count, axis, (count - 1) // 2
        self.ahead = [(order[(p + 1) % count], order[p]) for p in range(count)]
        self.behind = [(order[p], order[(p + 1) % count]) for p in range(count)]
        self.found = [{0: a} for a in arrays]
        self.up, self.down = list(arrays), list(arrays)

    def step(self, number):
        for t in range(2):
            found = self.found[t]
            if number <= self.near:
                self.up[t] = found[number] = lax.ppermute(self.up[t], self.axis, self.ahead)
                self.down[t] = found[self.count - number] = lax.ppermute(self.down[t], self.axis, self.behind)
            else:
                found[number] = [
                    lax.ppermute(self.up[t][0], self.axis, self.ahead),
                    lax.ppermute(self.down[t][1], self.axis, self.behind),
                ]

    def tie(self, value, number, which=(0, 1)):
        lists = [(self.up, t, number) for t in which if number <= self.near or t == 0]
        lists += [(self.down, t, self.count - number) for t in which if number <= self.near or t == 1]
        value, *held = lax.optimization_barrier((value, *(way[t] for way, t, _ in lists)))
        for (way, t, place), block in zip(lists, held):
            way[t] = self.found[t][place] = block
        return value


def body(panel_u, panel_v, panel_rank, pivot_u, pivot_v, pivot_rank, orig_u, orig_v, sampler):
    order, width = panel_u.shape[2:]
    priors = panel_u.shape[1]
    pivots = pivot_u.shape[0]
    count = lax.axis_size("rows")
    cols = lax.axis_size("cols")
    pairs = cols // 2
    half, share = order // 2, order // cols
    me = lax.axis_index("cols")
    core, pair = me % 2, me // 2
    swap = [(i, i ^ 1) for i in range(cols)]

    ring = ring_order(count)
    place = np.argsort(np.array(ring))
    table = np.array([[ring[(place[r] + d) % count] for d in range(count)] for r in range(count)], np.int32)
    last = count // 2
    whole = count % 2 == 1 or last < 4 or count > RING_MOST
    if whole:
        table = np.zeros((count, 1), np.int32)
    sources = jnp.asarray(table)[lax.axis_index("rows")]
    info = jnp.concatenate([jnp.stack([core, me]).astype(jnp.int32), sources])

    panel_u, panel_v, orig_u, orig_v = panel_u[0], panel_v[0], orig_u[:, 0], orig_v[:, 0]
    square = 2 * width * width
    panel_vt, sampler_t = run(
        turn_kernel, [], [panel_v, sampler], [((priors, width, order), BF16), ((sampler.shape[1], order), BF16)], [], 12,
        10 * square * order, "turn"
    )
    (start,) = run(
        start_kernel, [info], [sampler_t, orig_u, orig_v], [((width, order), F32)], [], 12,
        2 * square * order, "start"
    )

    def shifted(x, shift):
        return lax.ppermute(x, "cols", [(i, (i + 2 * shift) % cols) for i in range(cols)])

    matrix = pltpu.VMEM((width, width), F32)
    tall = pltpu.VMEM((width, order), F32)

    def gathered(places, blocks, new_u, new_v, kept):
        new = len(places)
        shapes = [
            ((pivots, priors, width, width), F32), ((pivots, priors, width, width), F32),
            ((pivots, priors, order, width), BF16)
        ]
        first = 3 + 2 * new
        return run(
            functools.partial(gather_kernel, places, blocks), [info], [panel_vt, sampler_t, *new_u, *new_v, *kept],
            shapes, [], 28, 2 * pivots * priors * square * order * new // blocks, "gather",
            {first + n: n for n in range(len(kept))}
        )

    def updated(own_column, sampled, met):
        return run(
            functools.partial(update_kernel, own_column, places, blocks), [info, panel_rank, pivot_rank],
            [sampled, met, panel_u, panel_vt, *late_v],
            [((priors, width, width), BF16), ((width, order), F32 if own_column else BF16)], [], 20,
            2 * priors * square * (order + width), "update"
        )

    def projected(own_column, qt, cross):
        return run(
            functools.partial(project_kernel, blocks, own_column), [info], [qt, panel_u, cross, u_all],
            [((pairs, share, width), BF16), ((pairs, share, width), F32), ((width, width), BF16)],
            [pltpu.VMEM((order, width), F32), pltpu.VMEM((order, width), BF16), pltpu.SemaphoreType.DMA((1,))],
            20, 3 * priors * square * (2 * order + width), "project", apart=[orig_u]
        )

    if whole:
        blocks, places = 1, []
        new_u, new_v = ([lax.all_gather(x, "rows", axis=2, tiled=True)] for x in (pivot_u, pivot_v))
        sampled, met, u_all = gathered([0], 1, new_u, new_v, [])
        late_u, late_v = [], []
    else:
        blocks = count
        now, kept = Ring([pivot_u, pivot_v], ring, "rows"), []
        for number in range(1, last + 1):
            now.step(number)
            if 1 < number < last:
                kept[0] = now.tie(kept[0], number, (0,))
                if number == 2:
                    start = now.tie(start, number, (1,))
            if number == last:
                places = [last]
                late_u, late_v = now.found[0][last], now.found[1][last]
            else:
                places = sorted({number, count - number} | ({0} if number == 1 else set()))
                new_u, new_v = ([now.found[t][p] for p in places] for t in range(2))
                kept = list(gathered(places, count, new_u, new_v, kept))
        sampled, met, u_all = kept
    sampled, u_all = run(
        functools.partial(sampled_kernel, places, blocks), [info], [sampled, sampler_t, *late_u, u_all],
        [((pivots, priors, width, width), BF16), ((pivots, priors, order, width), BF16)], [], 16, square * order,
        "sampled", {3 + len(late_u): 1}
    )
    cross_other, give = updated(False, sampled, met)
    recv = lax.ppermute(give, "cols", swap)
    cross_own, keep = updated(True, sampled, met)
    sent = (keep + recv.astype(F32)).astype(BF16)
    parts = [keep, recv, *(shifted(sent, shift) for shift in range(1, pairs))]
    qt, given, basis = run(
        orthonormal_kernel, [info], [start, *parts],
        [((width, order), BF16), ((share, width), F32), ((pivots, share, width), F32)],
        [
            tall, matrix, pltpu.VMEM((BLOCK // SUB, (SUB + width // 128) * SUB, 128), F32), pltpu.VMEM((share, width), F32),
            pltpu.SemaphoreType.DMA((1,))
        ],
        16,
        128 * square * order, "orthonormal", away=1
    )
    qt_other = lax.ppermute(qt, "cols", swap)
    give_a, keep_a, left_a = projected(True, qt, cross_own)
    qt_other, give_a, keep_a = lax.optimization_barrier((qt_other, give_a, keep_a))
    give_b, keep_b, left_b = projected(False, qt_other, cross_other)
    give_a, give_b = lax.ppermute(give_a, "cols", swap), lax.ppermute(give_b, "cols", swap)
    sent = run(
        halve_kernel, [info], [keep_b, keep_a, give_a, give_b], [((pivots, share, width), BF16)] * (pairs - 1), [], 8,
        square, "halve"
    )
    left_b, *sent = lax.optimization_barrier((left_b, *sent))
    recv = [shifted(each, shift) for shift, each in enumerate(sent, 1)]
    (coeff,) = run(
        own_kernel, [info], [left_b, left_a, keep_b, keep_a, give_a, give_b], [((pivots, share, width), F32)],
        [pltpu.VMEM((pivots, share, width), BF16), pltpu.SemaphoreType.DMA((2,))], 8, square * width, "own", apart=[orig_v]
    )
    (basis,) = run(
        place_kernel, [info], [lax.ppermute(given, "cols", swap)], [((pivots, share, width), F32)],
        [pltpu.SemaphoreType.DMA((1,))], 4, 1, "place", {2: 0}, [basis], 1
    )
    for each in recv:
        coeff = coeff - each.astype(F32)
    return (basis[:, None], coeff[:, None])


def solution(mesh):
    placed = (
        P("rows", "cols", None, None),
        P("rows", "cols", None, None),
        P("rows", "cols"),
        P(None, "cols", "rows", None),
        P(None, "cols", "rows", None),
        P(None, "cols"),
        P(None, "rows", None, None),
        P(None, "rows", None, None),
        P(),
    )
    return jax.shard_map(
        body,
        mesh=mesh,
        in_specs=placed,
        out_specs=(P(None, "rows", "cols", None), P(None, "rows", "cols", None)),
        check_vma=False,
    )
```

```python
import functools
import math

import jax
import jax.numpy as jnp
import numpy as np
from jax import lax
from jax.experimental import pallas as pl
from jax.experimental.pallas import tpu as pltpu
from jax.sharding import PartitionSpec as P

F32 = jnp.float32
BF16 = jnp.bfloat16
BLOCK = 64
SUB = 8
RING_MOST = 16
MIB = 1 << 20


def dot(a, b):
    return lax.dot_general(a, b, (((1,), (0,)), ((), ())), preferred_element_type=F32)


def dot00(a, b):
    return lax.dot_general(a, b, (((0,), (0,)), ((), ())), preferred_element_type=F32)


def dot11(a, b):
    return lax.dot_general(a, b, (((1,), (1,)), ((), ())), preferred_element_type=F32)


def split3(x):
    high = x.astype(BF16)
    rest = x - high.astype(F32)
    mid = rest.astype(BF16)
    low = (rest - mid.astype(F32)).astype(BF16)
    return high, mid, low


def eliminate(panel, first, store):
    rows, width = panel.shape
    lanes = 128
    tile = (SUB, lanes)
    lane = lax.broadcasted_iota(jnp.int32, tile, 1)
    sub = lax.broadcasted_iota(jnp.int32, tile, 0)
    high = rows // SUB
    halves = width // lanes
    part = [
        [panel[v * SUB : (v + 1) * SUB, h * lanes : (h + 1) * lanes] for h in range(halves)]
        for v in range(high)
    ]
    mine, start = first // lanes, first % lanes
    scales = []
    for top in range(high):
        at = start + top * SUB
        inside = (lane >= at) & (lane < at + SUB)
        column = [
            [jnp.broadcast_to(part[v][mine][:, at + m : at + m + 1], tile) for v in range(top, high)]
            for m in range(SUB)
        ]
        for n, value in enumerate([c[0] for c in column] + part[top]):
            store[top, n * SUB : (n + 1) * SUB, :] = value

        def spread(n, a):
            return jnp.broadcast_to(store[top, n * SUB + a : n * SUB + a + 1, :], tile)

        small = [[spread(b, a) for b in range(a + 1)] for a in range(SUB)]
        row = []
        for a in range(SUB):
            row.append([spread(SUB + h, a) for h in range(halves)])
            row[a][mine] = jnp.where(inside, jnp.where(lane == at + a, 1.0, 0.0), row[a][mine])
        pivots = small[0][0]
        factor = []
        for m in range(SUB):
            inverse = pl.reciprocal(small[m][m], approx=True)
            if m:
                pivots = jnp.where(sub == m, small[m][m], pivots)
            for a in range(m + 1, SUB):
                ratio = small[a][m] * inverse
                for b in range(m + 1, a + 1):
                    small[a][b] = small[a][b] - ratio * small[b][m]
                row[a] = [x - ratio * y for x, y in zip(row[a], row[m])]
            factor.append([c * inverse for c in column[m][1:]])
            for b in range(m + 1, SUB):
                column[b][1:] = [c - f * small[b][m] for c, f in zip(column[b][1:], factor[m])]
        for v in range(top + 1, high):
            for h in range(halves):
                value = jnp.where(inside, 0.0, part[v][h]) if h == mine else part[v][h]
                for m in range(SUB):
                    value = value - factor[m][v - top - 1] * row[m][h]
                part[v][h] = value
        for h in range(halves):
            value = row[0][h]
            for m in range(1, SUB):
                value = jnp.where(sub == m, row[m][h], value)
            part[top][h] = value
        scales.append(lax.rsqrt(pivots))
    done = []
    for v in range(high):
        cells = []
        for h in range(halves):
            value = part[v][h] * scales[v]
            if h == mine:
                value = jnp.where((lane > start + v * SUB + sub) & (lane < start + rows), 0.0, value)
            cells.append(value)
        done.append(jnp.concatenate(cells, 1))
    return jnp.concatenate(done, 0)


def invert_blocks(work, store, begin, end):
    width = work.shape[0]
    lane = lax.broadcasted_iota(jnp.int32, (1, width), 1)
    for first in range(begin, end, BLOCK):
        last = first + BLOCK
        panel = eliminate(work[first:last, :], first, store)
        work[first:last, :] = panel
        if last < width:
            base = last // 128 * 128
            high, mid, low = split3(panel)
            left = jnp.concatenate([high, high, mid, mid, high, low], 0)[:, base:]
            right = jnp.concatenate([high, mid, high, mid, low, high], 0)
            update = dot00(left, right)[last - base :, :]
            inside = (lane >= first) & (lane < last)
            work[last:, :] = jnp.where(inside, 0.0, work[last:, :]) - update


def orthonormal_kernel(info, start, *refs):
    parts, (qt, given, basis, yt, work, store, rows, sem) = refs[:-8], refs[-8:]
    width, order = yt.shape
    core = info[0]
    total = start[...]
    for part in parts:
        total = total - part[...].astype(F32)
    yt[...] = total
    high, mid, low = split3(yt[...])
    cross = dot11(high, mid) + dot11(high, low)
    work[...] = dot11(high, high) + (cross + cross.T + dot11(mid, mid))
    invert_blocks(work, store, 0, width)
    row = lax.broadcasted_iota(jnp.int32, (width, width), 0)
    col = lax.broadcasted_iota(jnp.int32, (width, width), 1)
    m_high, m_low, _ = split3(jnp.where(col <= row, work[...], 0.0))
    high, mid, _ = split3(yt[...])
    product = dot(m_high, high) + (dot(m_high, mid) + dot(m_low, high))
    yt[...] = product
    share = given.shape[0]

    def rows_at(index):
        return yt[:, pl.ds(pl.multiple_of(index * share, 128), share)].T * math.sqrt(order)

    rows[...] = rows_at(info[1])
    copy = pltpu.make_async_copy(rows, basis.at[core], sem.at[0])
    copy.start()
    given[...] = rows_at(info[1] + 1 - 2 * core)
    qt[...] = product.astype(BF16)
    copy.wait()


def place_kernel(info, given, basis, out, sem):
    copy = pltpu.make_async_copy(given, out.at[1 - info[0]], sem.at[0])
    copy.start()
    copy.wait()


def gather_kernel(places, blocks, info, panel_vt, sampler_t, *refs):
    new = len(places)
    u, v = refs[:new], refs[new : 2 * new]
    kept = refs[2 * new : -3]
    sampled, met, u_all = refs[-3:]
    pivots, priors, order, width = u_all.shape
    slab = order // blocks
    spans = [pl.ds(pl.multiple_of(info[2 + p] * slab, 128), slab) for p in places]
    drawn = jnp.concatenate([sampler_t[:, span] for span in spans], 1)
    for j in range(priors):
        left = jnp.concatenate([panel_vt[j, :, span] for span in spans], 1)
        for c in range(pivots):
            u_new = jnp.concatenate([block[c, j] for block in u], 0)
            v_new = jnp.concatenate([block[c, j] for block in v], 0)
            one, two = dot(drawn, u_new), dot(left, v_new)
            if kept:
                one, two = one + kept[0][c, j], two + kept[1][c, j]
            sampled[c, j] = one
            met[c, j] = two
            for n, p in enumerate(places):
                u_all[c, j, p * slab : (p + 1) * slab, :] = u_new[n * slab : (n + 1) * slab, :]


def sampled_kernel(places, blocks, info, sampled, sampler_t, *refs):
    late, (out, u_all) = refs[: len(refs) - 3], refs[-2:]
    slab = sampler_t.shape[1] // blocks
    for c in range(out.shape[0]):
        for j in range(out.shape[1]):
            total = sampled[c, j]
            for place in places:
                span = pl.ds(pl.multiple_of(info[2 + place] * slab, 128), slab)
                total += dot(sampler_t[:, span], late[c][j])
                u_all[c, j, place * slab : (place + 1) * slab, :] = late[c][j]
            out[c, j] = total.astype(BF16)


def update_kernel(own_column, places, blocks, info, panel_rank, pivot_rank, sampled, met, panel_u, panel_vt, *refs):
    late, (cross, out) = refs[:-2], refs[-2:]
    priors, width, _ = cross.shape
    slab = panel_vt.shape[2] // blocks
    column = info[0] if own_column else 1 - info[0]
    row = lax.broadcasted_iota(jnp.int32, (width, width), 0)
    col = lax.broadcasted_iota(jnp.int32, (width, width), 1)
    terms = []
    for j in range(priors):
        two = met[column, j]
        for place in places:
            span = pl.ds(pl.multiple_of(info[2 + place] * slab, 128), slab)
            two += dot(panel_vt[j, :, span], jnp.where(column == 0, late[0][j], late[1][j]))
        inside = (row < panel_rank[0, j]) & (col < pivot_rank[column, j])
        cross[j] = jnp.where(inside, two, 0.0).astype(BF16)
        terms.append(dot11(sampled[column, j], cross[j]).astype(BF16))
    half = out.shape[1] // 2
    for at in (0, half):
        total = jnp.zeros((width, half), F32)
        for j in range(priors):
            total += dot11(terms[j], panel_u[j, at : at + half, :])
        out[:, at : at + half] = total.astype(out.dtype)


def project_kernel(blocks, own_column, info, qt, panel_u, cross, u_all, orig_u, give, keep, left, work, u_buf, sem):
    _, priors, order, width = u_all.shape
    slab = order // blocks
    pairs, share, _ = keep.shape
    core = info[0]
    column = core if own_column else 1 - core
    copy = pltpu.make_async_copy(orig_u.at[column], u_buf, sem.at[0])
    copy.start()
    mids = []
    for j in range(priors):
        inner = dot(qt[...], panel_u[j]).astype(BF16)
        mids.append(dot(inner, cross[j]).astype(BF16))
    some = max(1, blocks // 2)
    for begin in range(0, blocks, some):
        total = jnp.zeros((some * slab, width), F32)
        for j in range(priors):
            total += dot11(u_all[column, j, begin * slab : (begin + some) * slab, :], mids[j])
        for n in range(some):
            place = pl.ds(pl.multiple_of(info[2 + begin + n] * slab, SUB), slab)
            work[place, :] = total[n * slab : (n + 1) * slab, :]
    for a in range(pairs):
        for out, which in ((give, 1 - core), (keep, core)):
            place = pl.ds(pl.multiple_of((2 * a + which) * share, SUB), share)
            out[a] = work[place, :].astype(out.dtype)
    copy.wait()
    left[...] = dot(qt[...], u_buf[...]).astype(BF16)


def halve_kernel(info, keep_b, keep_a, give_a, give_b, *sent):
    pairs = keep_a.shape[0]
    for shift in range(1, pairs):
        a = lax.rem(info[1] // 2 + shift, pairs)
        for column, keep, recv in ((1 - info[0], keep_b, give_a), (info[0], keep_a, give_b)):
            sent[shift - 1][column] = (keep[a] + recv[a].astype(F32)).astype(BF16)


def own_kernel(info, left_b, left_a, keep_b, keep_a, give_a, give_b, orig_v, out, v_buf, sems):
    share = out.shape[1]
    pair = info[1] // 2
    rows = pl.ds(pl.multiple_of(info[1] * share, 16), share)
    work = ((1 - info[0], left_b, keep_b, give_a), (info[0], left_a, keep_a, give_b))
    copies = [
        pltpu.make_async_copy(orig_v.at[column, rows], v_buf.at[n], sems.at[n]) for n, (column, *_) in enumerate(work)
    ]
    for copy in copies:
        copy.start()
    for n, (column, left, keep, recv) in enumerate(work):
        copies[n].wait()
        out[column] = dot11(v_buf[n], left[...]) - (keep[pair] + recv[pair].astype(F32))


def turn_kernel(panel_v, sampler, panel_vt, sampler_t):
    sampler_t[...] = sampler[...].T
    for j in range(panel_v.shape[0]):
        panel_vt[j] = panel_v[j].T


def start_kernel(info, sampler_t, orig_u, orig_v, out):
    core = info[0]
    proj = dot(sampler_t[...], orig_v[core]).astype(BF16)
    out[...] = dot11(proj, orig_u[core])


def run(kernel, scalars, arrays, outs, scratch, limit, flops, name, aliases={}, apart=(), away=0):
    smem = pl.BlockSpec(memory_space=pltpu.SMEM)
    vmem = pl.BlockSpec(memory_space=pltpu.VMEM)
    shapes = [jax.ShapeDtypeStruct(*o) for o in outs]
    moved = sum(a.size * a.dtype.itemsize for a in list(arrays) + shapes)
    return pl.pallas_call(
        kernel,
        out_shape=shapes,
        in_specs=[smem] * len(scalars) + [vmem] * len(arrays) + [pl.BlockSpec(memory_space=pl.ANY)] * len(apart),
        out_specs=[vmem] * (len(shapes) - away) + [pl.BlockSpec(memory_space=pl.ANY)] * away,
        scratch_shapes=scratch,
        input_output_aliases=aliases,
        compiler_params=pltpu.CompilerParams(vmem_limit_bytes=limit * MIB),
        cost_estimate=pl.CostEstimate(flops=flops, bytes_accessed=moved, transcendentals=0),
        name=name,
    )(*scalars, *arrays, *apart)


def ring_order(count):
    if count % 2:
        return list(range(count))
    return list(range(0, count, 2)) + list(range(count - 1, 0, -2))


class Ring:
    def __init__(self, arrays, order, axis):
        count = len(order)
        self.count, self.axis, self.near = count, axis, (count - 1) // 2
        self.ahead = [(order[(p + 1) % count], order[p]) for p in range(count)]
        self.behind = [(order[p], order[(p + 1) % count]) for p in range(count)]
        self.found = [{0: a} for a in arrays]
        self.up, self.down = list(arrays), list(arrays)

    def step(self, number):
        for t in range(2):
            found = self.found[t]
            if number <= self.near:
                self.up[t] = found[number] = lax.ppermute(self.up[t], self.axis, self.ahead)
                self.down[t] = found[self.count - number] = lax.ppermute(self.down[t], self.axis, self.behind)
            else:
                found[number] = [
                    lax.ppermute(self.up[t][0], self.axis, self.ahead),
                    lax.ppermute(self.down[t][1], self.axis, self.behind),
                ]

    def tie(self, value, number, which=(0, 1)):
        lists = [(self.up, t, number) for t in which if number <= self.near or t == 0]
        lists += [(self.down, t, self.count - number) for t in which if number <= self.near or t == 1]
        value, *held = lax.optimization_barrier((value, *(way[t] for way, t, _ in lists)))
        for (way, t, place), block in zip(lists, held):
            way[t] = self.found[t][place] = block
        return value


def body(panel_u, panel_v, panel_rank, pivot_u, pivot_v, pivot_rank, orig_u, orig_v, sampler):
    order, width = panel_u.shape[2:]
    priors = panel_u.shape[1]
    pivots = pivot_u.shape[0]
    count = lax.axis_size("rows")
    cols = lax.axis_size("cols")
    pairs = cols // 2
    half, share = order // 2, order // cols
    me = lax.axis_index("cols")
    core, pair = me % 2, me // 2
    swap = [(i, i ^ 1) for i in range(cols)]

    ring = ring_order(count)
    place = np.argsort(np.array(ring))
    table = np.array([[ring[(place[r] + d) % count] for d in range(count)] for r in range(count)], np.int32)
    last = count // 2
    whole = count % 2 == 1 or last < 4 or count > RING_MOST
    if whole:
        table = np.zeros((count, 1), np.int32)
    sources = jnp.asarray(table)[lax.axis_index("rows")]
    info = jnp.concatenate([jnp.stack([core, me]).astype(jnp.int32), sources])

    panel_u, panel_v, orig_u, orig_v = panel_u[0], panel_v[0], orig_u[:, 0], orig_v[:, 0]
    square = 2 * width * width
    panel_vt, sampler_t = run(
        turn_kernel, [], [panel_v, sampler], [((priors, width, order), BF16), ((sampler.shape[1], order), BF16)], [], 12,
        10 * square * order, "turn"
    )
    (start,) = run(
        start_kernel, [info], [sampler_t, orig_u, orig_v], [((width, order), F32)], [], 12,
        2 * square * order, "start"
    )

    def shifted(x, shift):
        return lax.ppermute(x, "cols", [(i, (i + 2 * shift) % cols) for i in range(cols)])

    matrix = pltpu.VMEM((width, width), F32)
    tall = pltpu.VMEM((width, order), F32)

    def gathered(places, blocks, new_u, new_v, kept):
        new = len(places)
        shapes = [
            ((pivots, priors, width, width), F32), ((pivots, priors, width, width), F32),
            ((pivots, priors, order, width), BF16)
        ]
        first = 3 + 2 * new
        return run(
            functools.partial(gather_kernel, places, blocks), [info], [panel_vt, sampler_t, *new_u, *new_v, *kept],
            shapes, [], 28, 2 * pivots * priors * square * order * new // blocks, "gather",
            {first + n: n for n in range(len(kept))}
        )

    def updated(own_column, sampled, met):
        return run(
            functools.partial(update_kernel, own_column, places, blocks), [info, panel_rank, pivot_rank],
            [sampled, met, panel_u, panel_vt, *late_v],
            [((priors, width, width), BF16), ((width, order), F32 if own_column else BF16)], [], 20,
            2 * priors * square * (order + width), "update"
        )

    def projected(own_column, qt, cross):
        return run(
            functools.partial(project_kernel, blocks, own_column), [info], [qt, panel_u, cross, u_all],
            [((pairs, share, width), BF16), ((pairs, share, width), F32), ((width, width), BF16)],
            [pltpu.VMEM((order, width), F32), pltpu.VMEM((order, width), BF16), pltpu.SemaphoreType.DMA((1,))],
            20, 3 * priors * square * (2 * order + width), "project", apart=[orig_u]
        )

    if whole:
        blocks, places = 1, []
        new_u, new_v = ([lax.all_gather(x, "rows", axis=2, tiled=True)] for x in (pivot_u, pivot_v))
        sampled, met, u_all = gathered([0], 1, new_u, new_v, [])
        late_u, late_v = [], []
    else:
        blocks = count
        now, kept = Ring([pivot_u, pivot_v], ring, "rows"), []
        for number in range(1, last + 1):
            now.step(number)
            if 1 < number < last:
                kept[0] = now.tie(kept[0], number, (0,))
                if number == 2:
                    start = now.tie(start, number, (1,))
            if number == last:
                places = [last]
                late_u, late_v = now.found[0][last], now.found[1][last]
            else:
                places = sorted({number, count - number} | ({0} if number == 1 else set()))
                new_u, new_v = ([now.found[t][p] for p in places] for t in range(2))
                kept = list(gathered(places, count, new_u, new_v, kept))
        sampled, met, u_all = kept
    sampled, u_all = run(
        functools.partial(sampled_kernel, places, blocks), [info], [sampled, sampler_t, *late_u, u_all],
        [((pivots, priors, width, width), BF16), ((pivots, priors, order, width), BF16)], [], 16, square * order,
        "sampled", {3 + len(late_u): 1}
    )
    cross_other, give = updated(False, sampled, met)
    recv = lax.ppermute(give, "cols", swap)
    cross_own, keep = updated(True, sampled, met)
    sent = (keep + recv.astype(F32)).astype(BF16)
    parts = [keep, recv, *(shifted(sent, shift) for shift in range(1, pairs))]
    qt, given, basis = run(
        orthonormal_kernel, [info], [start, *parts],
        [((width, order), BF16), ((share, width), F32), ((pivots, share, width), F32)],
        [
            tall, matrix, pltpu.VMEM((BLOCK // SUB, (SUB + width // 128) * SUB, 128), F32), pltpu.VMEM((share, width), F32),
            pltpu.SemaphoreType.DMA((1,))
        ],
        16,
        128 * square * order, "orthonormal", away=1
    )
    qt_other = lax.ppermute(qt, "cols", swap)
    give_a, keep_a, left_a = projected(True, qt, cross_own)
    qt_other, give_a, keep_a = lax.optimization_barrier((qt_other, give_a, keep_a))
    give_b, keep_b, left_b = projected(False, qt_other, cross_other)
    give_a, give_b = lax.ppermute(give_a, "cols", swap), lax.ppermute(give_b, "cols", swap)
    sent = run(
        halve_kernel, [info], [keep_b, keep_a, give_a, give_b], [((pivots, share, width), BF16)] * (pairs - 1), [], 8,
        square, "halve"
    )
    left_b, *sent = lax.optimization_barrier((left_b, *sent))
    recv = [shifted(each, shift) for shift, each in enumerate(sent, 1)]
    (coeff,) = run(
        own_kernel, [info], [left_b, left_a, keep_b, keep_a, give_a, give_b], [((pivots, share, width), F32)],
        [pltpu.VMEM((pivots, share, width), BF16), pltpu.SemaphoreType.DMA((2,))], 8, square * width, "own", apart=[orig_v]
    )
    (basis,) = run(
        place_kernel, [info], [lax.ppermute(given, "cols", swap)], [((pivots, share, width), F32)],
        [pltpu.SemaphoreType.DMA((1,))], 4, 1, "place", {2: 0}, [basis], 1
    )
    for each in recv:
        coeff = coeff - each.astype(F32)
    return (basis[:, None], coeff[:, None])


def solution(mesh):
    placed = (
        P("rows", "cols", None, None),
        P("rows", "cols", None, None),
        P("rows", "cols"),
        P(None, "cols", "rows", None),
        P(None, "cols", "rows", None),
        P(None, "cols"),
        P(None, "rows", None, None),
        P(None, "rows", None, None),
        P(),
    )
    return jax.shard_map(
        body,
        mesh=mesh,
        in_specs=placed,
        out_specs=(P(None, "rows", "cols", None), P(None, "rows", "cols", None)),
        check_vma=False,
    )
```

```python
import functools
import math

import jax
import jax.numpy as jnp
import numpy as np
from jax import lax
from jax.experimental import pallas as pl
from jax.experimental.pallas import tpu as pltpu
from jax.sharding import PartitionSpec as P

F32 = jnp.float32
BF16 = jnp.bfloat16
BLOCK = 32
SUB = 8
RING_MOST = 16
MIB = 1 << 20


def dot(a, b):
    return lax.dot_general(a, b, (((1,), (0,)), ((), ())), preferred_element_type=F32)


def dot00(a, b):
    return lax.dot_general(a, b, (((0,), (0,)), ((), ())), preferred_element_type=F32)


def dot11(a, b):
    return lax.dot_general(a, b, (((1,), (1,)), ((), ())), preferred_element_type=F32)


def split3(x):
    high = x.astype(BF16)
    rest = x - high.astype(F32)
    mid = rest.astype(BF16)
    low = (rest - mid.astype(F32)).astype(BF16)
    return high, mid, low


def eliminate(panel, first, store):
    rows, width = panel.shape
    lanes = 128
    tile = (SUB, lanes)
    lane = lax.broadcasted_iota(jnp.int32, tile, 1)
    sub = lax.broadcasted_iota(jnp.int32, tile, 0)
    high = rows // SUB
    halves = width // lanes
    part = [
        [panel[v * SUB : (v + 1) * SUB, h * lanes : (h + 1) * lanes] for h in range(halves)]
        for v in range(high)
    ]
    mine, start = first // lanes, first % lanes
    scales = []
    for top in range(high):
        at = start + top * SUB
        inside = (lane >= at) & (lane < at + SUB)
        column = [
            [jnp.broadcast_to(part[v][mine][:, at + m : at + m + 1], tile) for v in range(top, high)]
            for m in range(SUB)
        ]
        for n, value in enumerate([c[0] for c in column] + part[top]):
            store[top, n * SUB : (n + 1) * SUB, :] = value

        def spread(n, a):
            return jnp.broadcast_to(store[top, n * SUB + a : n * SUB + a + 1, :], tile)

        small = [[spread(b, a) for b in range(a + 1)] for a in range(SUB)]
        row = []
        for a in range(SUB):
            row.append([spread(SUB + h, a) for h in range(halves)])
            row[a][mine] = jnp.where(inside, jnp.where(lane == at + a, 1.0, 0.0), row[a][mine])
        pivots = small[0][0]
        factor = []
        for m in range(SUB):
            inverse = pl.reciprocal(small[m][m], approx=True)
            if m:
                pivots = jnp.where(sub == m, small[m][m], pivots)
            for a in range(m + 1, SUB):
                ratio = small[a][m] * inverse
                for b in range(m + 1, a + 1):
                    small[a][b] = small[a][b] - ratio * small[b][m]
                row[a] = [x - ratio * y for x, y in zip(row[a], row[m])]
            factor.append([c * inverse for c in column[m][1:]])
            for b in range(m + 1, SUB):
                column[b][1:] = [c - f * small[b][m] for c, f in zip(column[b][1:], factor[m])]
        for v in range(top + 1, high):
            for h in range(halves):
                value = jnp.where(inside, 0.0, part[v][h]) if h == mine else part[v][h]
                for m in range(SUB):
                    value = value - factor[m][v - top - 1] * row[m][h]
                part[v][h] = value
        for h in range(halves):
            value = row[0][h]
            for m in range(1, SUB):
                value = jnp.where(sub == m, row[m][h], value)
            part[top][h] = value
        scales.append(lax.rsqrt(pivots))
    done = []
    for v in range(high):
        cells = []
        for h in range(halves):
            value = part[v][h] * scales[v]
            if h == mine:
                value = jnp.where((lane > start + v * SUB + sub) & (lane < start + rows), 0.0, value)
            cells.append(value)
        done.append(jnp.concatenate(cells, 1))
    return jnp.concatenate(done, 0)


def invert_blocks(work, store, begin, end):
    width = work.shape[0]
    lane = lax.broadcasted_iota(jnp.int32, (1, width), 1)
    for first in range(begin, end, BLOCK):
        last = first + BLOCK
        panel = eliminate(work[first:last, :], first, store)
        work[first:last, :] = panel
        if last < width:
            base = last // 128 * 128
            high, mid, low = split3(panel)
            left = jnp.concatenate([high, high, mid, mid, high, low], 0)[:, base:]
            right = jnp.concatenate([high, mid, high, mid, low, high], 0)
            update = dot00(left, right)[last - base :, :]
            inside = (lane >= first) & (lane < last)
            work[last:, :] = jnp.where(inside, 0.0, work[last:, :]) - update


def orthonormal_kernel(info, start, *refs):
    parts, (qt, given, basis, yt, work, store, rows, sem) = refs[:-8], refs[-8:]
    width, order = yt.shape
    core = info[0]
    total = start[...]
    for part in parts:
        total = total - part[...].astype(F32)
    yt[...] = total
    high, mid, low = split3(yt[...])
    cross = dot11(high, mid) + dot11(high, low)
    work[...] = dot11(high, high) + (cross + cross.T + dot11(mid, mid))
    invert_blocks(work, store, 0, width)
    row = lax.broadcasted_iota(jnp.int32, (width, width), 0)
    col = lax.broadcasted_iota(jnp.int32, (width, width), 1)
    m_high, m_low, _ = split3(jnp.where(col <= row, work[...], 0.0))
    high, mid, _ = split3(yt[...])
    product = dot(m_high, high) + (dot(m_high, mid) + dot(m_low, high))
    yt[...] = product
    share = given.shape[0]

    def rows_at(index):
        return yt[:, pl.ds(pl.multiple_of(index * share, 128), share)].T * math.sqrt(order)

    rows[...] = rows_at(info[1])
    copy = pltpu.make_async_copy(rows, basis.at[core], sem.at[0])
    copy.start()
    given[...] = rows_at(info[1] + 1 - 2 * core)
    qt[...] = product.astype(BF16)
    copy.wait()


def place_kernel(info, given, basis, out, sem):
    copy = pltpu.make_async_copy(given, out.at[1 - info[0]], sem.at[0])
    copy.start()
    copy.wait()


def gather_kernel(places, blocks, info, panel_vt, sampler_t, *refs):
    new = len(places)
    u, v = refs[:new], refs[new : 2 * new]
    kept = refs[2 * new : -3]
    sampled, met, u_all = refs[-3:]
    pivots, priors, order, width = u_all.shape
    slab = order // blocks
    spans = [pl.ds(pl.multiple_of(info[2 + p] * slab, 128), slab) for p in places]
    drawn = jnp.concatenate([sampler_t[:, span] for span in spans], 1)
    for j in range(priors):
        left = jnp.concatenate([panel_vt[j, :, span] for span in spans], 1)
        for c in range(pivots):
            u_new = jnp.concatenate([block[c, j] for block in u], 0)
            v_new = jnp.concatenate([block[c, j] for block in v], 0)
            one, two = dot(drawn, u_new), dot(left, v_new)
            if kept:
                one, two = one + kept[0][c, j], two + kept[1][c, j]
            sampled[c, j] = one
            met[c, j] = two
            for n, p in enumerate(places):
                u_all[c, j, p * slab : (p + 1) * slab, :] = u_new[n * slab : (n + 1) * slab, :]


def sampled_kernel(places, blocks, info, sampled, sampler_t, *refs):
    late, (out, u_all) = refs[: len(refs) - 3], refs[-2:]
    slab = sampler_t.shape[1] // blocks
    for c in range(out.shape[0]):
        for j in range(out.shape[1]):
            total = sampled[c, j]
            for place in places:
                span = pl.ds(pl.multiple_of(info[2 + place] * slab, 128), slab)
                total += dot(sampler_t[:, span], late[c][j])
                u_all[c, j, place * slab : (place + 1) * slab, :] = late[c][j]
            out[c, j] = total.astype(BF16)


def update_kernel(own_column, places, blocks, info, panel_rank, pivot_rank, sampled, met, panel_u, panel_vt, *refs):
    late, (cross, out) = refs[:-2], refs[-2:]
    priors, width, _ = cross.shape
    slab = panel_vt.shape[2] // blocks
    column = info[0] if own_column else 1 - info[0]
    row = lax.broadcasted_iota(jnp.int32, (width, width), 0)
    col = lax.broadcasted_iota(jnp.int32, (width, width), 1)
    terms = []
    for j in range(priors):
        two = met[column, j]
        for place in places:
            span = pl.ds(pl.multiple_of(info[2 + place] * slab, 128), slab)
            two += dot(panel_vt[j, :, span], jnp.where(column == 0, late[0][j], late[1][j]))
        inside = (row < panel_rank[0, j]) & (col < pivot_rank[column, j])
        cross[j] = jnp.where(inside, two, 0.0).astype(BF16)
        terms.append(dot11(sampled[column, j], cross[j]).astype(BF16))
    half = out.shape[1] // 2
    for at in (0, half):
        total = jnp.zeros((width, half), F32)
        for j in range(priors):
            total += dot11(terms[j], panel_u[j, at : at + half, :])
        out[:, at : at + half] = total.astype(out.dtype)


def project_kernel(blocks, own_column, info, qt, panel_u, cross, u_all, give, keep, work):
    _, priors, order, width = u_all.shape
    slab = order // blocks
    pairs, share, _ = keep.shape
    core = info[0]
    column = core if own_column else 1 - core
    mids = []
    for j in range(priors):
        inner = dot(qt[...], panel_u[j]).astype(BF16)
        mids.append(dot(inner, cross[j]).astype(BF16))
    some = max(1, blocks // 2)
    for begin in range(0, blocks, some):
        total = jnp.zeros((some * slab, width), F32)
        for j in range(priors):
            total += dot11(u_all[column, j, begin * slab : (begin + some) * slab, :], mids[j])
        for n in range(some):
            place = pl.ds(pl.multiple_of(info[2 + begin + n] * slab, SUB), slab)
            work[place, :] = total[n * slab : (n + 1) * slab, :]
    for a in range(pairs):
        for out, which in ((give, 1 - core), (keep, core)):
            place = pl.ds(pl.multiple_of((2 * a + which) * share, SUB), share)
            out[a] = work[place, :].astype(out.dtype)


def halve_kernel(info, keep_b, keep_a, give_a, give_b, *sent):
    pairs = keep_a.shape[0]
    for shift in range(1, pairs):
        a = lax.rem(info[1] // 2 + shift, pairs)
        for column, keep, recv in ((1 - info[0], keep_b, give_a), (info[0], keep_a, give_b)):
            sent[shift - 1][column] = (keep[a] + recv[a].astype(F32)).astype(BF16)


def own_kernel(info, qt_b, qt_a, keep_b, keep_a, give_a, give_b, orig_u, orig_v, out, u_buf, v_buf, sems):
    share = out.shape[1]
    pair = info[1] // 2
    rows = pl.ds(pl.multiple_of(info[1] * share, 16), share)
    work = ((1 - info[0], qt_b, keep_b, give_a), (info[0], qt_a, keep_a, give_b))
    copies = []
    for n, (column, *_) in enumerate(work):
        copies.append(pltpu.make_async_copy(orig_u.at[column], u_buf.at[n], sems.at[2 * n]))
        copies.append(pltpu.make_async_copy(orig_v.at[column, rows], v_buf.at[n], sems.at[2 * n + 1]))
    for copy in copies:
        copy.start()
    for n, (column, qt, keep, recv) in enumerate(work):
        copies[2 * n].wait()
        copies[2 * n + 1].wait()
        left = dot(qt[...], u_buf[n]).astype(BF16)
        out[column] = dot11(v_buf[n], left) - (keep[pair] + recv[pair].astype(F32))


def turn_kernel(panel_v, sampler, panel_vt, sampler_t):
    sampler_t[...] = sampler[...].T
    for j in range(panel_v.shape[0]):
        panel_vt[j] = panel_v[j].T


def start_kernel(info, sampler_t, orig_u, orig_v, out):
    core = info[0]
    proj = dot(sampler_t[...], orig_v[core]).astype(BF16)
    out[...] = dot11(proj, orig_u[core])


def run(kernel, scalars, arrays, outs, scratch, limit, flops, name, aliases={}, apart=(), away=0):
    smem = pl.BlockSpec(memory_space=pltpu.SMEM)
    vmem = pl.BlockSpec(memory_space=pltpu.VMEM)
    shapes = [jax.ShapeDtypeStruct(*o) for o in outs]
    moved = sum(a.size * a.dtype.itemsize for a in list(arrays) + shapes)
    return pl.pallas_call(
        kernel,
        out_shape=shapes,
        in_specs=[smem] * len(scalars) + [vmem] * len(arrays) + [pl.BlockSpec(memory_space=pl.ANY)] * len(apart),
        out_specs=[vmem] * (len(shapes) - away) + [pl.BlockSpec(memory_space=pl.ANY)] * away,
        scratch_shapes=scratch,
        input_output_aliases=aliases,
        compiler_params=pltpu.CompilerParams(vmem_limit_bytes=limit * MIB),
        cost_estimate=pl.CostEstimate(flops=flops, bytes_accessed=moved, transcendentals=0),
        name=name,
    )(*scalars, *arrays, *apart)


def ring_order(count):
    if count % 2:
        return list(range(count))
    return list(range(0, count, 2)) + list(range(count - 1, 0, -2))


class Ring:
    def __init__(self, arrays, order, axis):
        count = len(order)
        self.count, self.axis, self.near = count, axis, (count - 1) // 2
        self.ahead = [(order[(p + 1) % count], order[p]) for p in range(count)]
        self.behind = [(order[p], order[(p + 1) % count]) for p in range(count)]
        self.found = [{0: a} for a in arrays]
        self.up, self.down = list(arrays), list(arrays)

    def step(self, number):
        for t in range(2):
            found = self.found[t]
            if number <= self.near:
                self.up[t] = found[number] = lax.ppermute(self.up[t], self.axis, self.ahead)
                self.down[t] = found[self.count - number] = lax.ppermute(self.down[t], self.axis, self.behind)
            else:
                found[number] = [
                    lax.ppermute(self.up[t][0], self.axis, self.ahead),
                    lax.ppermute(self.down[t][1], self.axis, self.behind),
                ]

    def tie(self, value, number, which=(0, 1)):
        lists = [(self.up, t, number) for t in which if number <= self.near or t == 0]
        lists += [(self.down, t, self.count - number) for t in which if number <= self.near or t == 1]
        value, *held = lax.optimization_barrier((value, *(way[t] for way, t, _ in lists)))
        for (way, t, place), block in zip(lists, held):
            way[t] = self.found[t][place] = block
        return value


def body(panel_u, panel_v, panel_rank, pivot_u, pivot_v, pivot_rank, orig_u, orig_v, sampler):
    order, width = panel_u.shape[2:]
    priors = panel_u.shape[1]
    pivots = pivot_u.shape[0]
    count = lax.axis_size("rows")
    cols = lax.axis_size("cols")
    pairs = cols // 2
    half, share = order // 2, order // cols
    me = lax.axis_index("cols")
    core, pair = me % 2, me // 2
    swap = [(i, i ^ 1) for i in range(cols)]

    ring = ring_order(count)
    place = np.argsort(np.array(ring))
    table = np.array([[ring[(place[r] + d) % count] for d in range(count)] for r in range(count)], np.int32)
    last = count // 2
    whole = count % 2 == 1 or last < 4 or count > RING_MOST
    if whole:
        table = np.zeros((count, 1), np.int32)
    sources = jnp.asarray(table)[lax.axis_index("rows")]
    info = jnp.concatenate([jnp.stack([core, me]).astype(jnp.int32), sources])

    panel_u, panel_v, orig_u, orig_v = panel_u[0], panel_v[0], orig_u[:, 0], orig_v[:, 0]
    square = 2 * width * width
    panel_vt, sampler_t = run(
        turn_kernel, [], [panel_v, sampler], [((priors, width, order), BF16), ((sampler.shape[1], order), BF16)], [], 12,
        10 * square * order, "turn"
    )
    (start,) = run(
        start_kernel, [info], [sampler_t, orig_u, orig_v], [((width, order), F32)], [], 12,
        2 * square * order, "start"
    )

    def shifted(x, shift):
        return lax.ppermute(x, "cols", [(i, (i + 2 * shift) % cols) for i in range(cols)])

    matrix = pltpu.VMEM((width, width), F32)
    tall = pltpu.VMEM((width, order), F32)

    def gathered(places, blocks, new_u, new_v, kept):
        new = len(places)
        shapes = [
            ((pivots, priors, width, width), F32), ((pivots, priors, width, width), F32),
            ((pivots, priors, order, width), BF16)
        ]
        first = 3 + 2 * new
        return run(
            functools.partial(gather_kernel, places, blocks), [info], [panel_vt, sampler_t, *new_u, *new_v, *kept],
            shapes, [], 28, 2 * pivots * priors * square * order * new // blocks, "gather",
            {first + n: n for n in range(len(kept))}
        )

    def updated(own_column, sampled, met):
        return run(
            functools.partial(update_kernel, own_column, places, blocks), [info, panel_rank, pivot_rank],
            [sampled, met, panel_u, panel_vt, *late_v],
            [((priors, width, width), BF16), ((width, order), F32 if own_column else BF16)], [], 20,
            2 * priors * square * (order + width), "update"
        )

    def projected(own_column, qt, cross):
        return run(
            functools.partial(project_kernel, blocks, own_column), [info], [qt, panel_u, cross, u_all],
            [((pairs, share, width), BF16), ((pairs, share, width), F32)], [pltpu.VMEM((order, width), F32)],
            20, 3 * priors * square * (2 * order + width), "project"
        )

    if whole:
        blocks, places = 1, []
        new_u, new_v = ([lax.all_gather(x, "rows", axis=2, tiled=True)] for x in (pivot_u, pivot_v))
        sampled, met, u_all = gathered([0], 1, new_u, new_v, [])
        late_u, late_v = [], []
    else:
        blocks = count
        now, kept = Ring([pivot_u, pivot_v], ring, "rows"), []
        for number in range(1, last + 1):
            now.step(number)
            if 1 < number < last:
                kept[0] = now.tie(kept[0], number, (0,))
                if number == 2:
                    start = now.tie(start, number, (1,))
            if number == last:
                places = [last]
                late_u, late_v = now.found[0][last], now.found[1][last]
            else:
                places = sorted({number, count - number} | ({0} if number == 1 else set()))
                new_u, new_v = ([now.found[t][p] for p in places] for t in range(2))
                kept = list(gathered(places, count, new_u, new_v, kept))
        sampled, met, u_all = kept
    sampled, u_all = run(
        functools.partial(sampled_kernel, places, blocks), [info], [sampled, sampler_t, *late_u, u_all],
        [((pivots, priors, width, width), BF16), ((pivots, priors, order, width), BF16)], [], 16, square * order,
        "sampled", {3 + len(late_u): 1}
    )
    cross_other, give = updated(False, sampled, met)
    recv = lax.ppermute(give, "cols", swap)
    cross_own, keep = updated(True, sampled, met)
    sent = (keep + recv.astype(F32)).astype(BF16)
    parts = [keep, recv, *(shifted(sent, shift) for shift in range(1, pairs))]
    qt, given, basis = run(
        orthonormal_kernel, [info], [start, *parts],
        [((width, order), BF16), ((share, width), F32), ((pivots, share, width), F32)],
        [
            tall, matrix, pltpu.VMEM((BLOCK // SUB, (SUB + width // 128) * SUB, 128), F32), pltpu.VMEM((share, width), F32),
            pltpu.SemaphoreType.DMA((1,))
        ],
        16,
        128 * square * order, "orthonormal", away=1
    )
    qt_other = lax.ppermute(qt, "cols", swap)
    give_a, keep_a = projected(True, qt, cross_own)
    qt_other, give_a, keep_a = lax.optimization_barrier((qt_other, give_a, keep_a))
    give_b, keep_b = projected(False, qt_other, cross_other)
    give_a, give_b = lax.ppermute(give_a, "cols", swap), lax.ppermute(give_b, "cols", swap)
    sent = run(
        halve_kernel, [info], [keep_b, keep_a, give_a, give_b], [((pivots, share, width), BF16)] * (pairs - 1), [], 8,
        square, "halve"
    )
    qt, *sent = lax.optimization_barrier((qt, *sent))
    recv = [shifted(each, shift) for shift, each in enumerate(sent, 1)]
    (coeff,) = run(
        own_kernel, [info], [qt_other, qt, keep_b, keep_a, give_a, give_b], [((pivots, share, width), F32)],
        [pltpu.VMEM((pivots, order, width), BF16), pltpu.VMEM((pivots, share, width), BF16), pltpu.SemaphoreType.DMA((4,))],
        12, square * width, "own", apart=[orig_u, orig_v]
    )
    (basis,) = run(
        place_kernel, [info], [lax.ppermute(given, "cols", swap)], [((pivots, share, width), F32)],
        [pltpu.SemaphoreType.DMA((1,))], 4, 1, "place", {2: 0}, [basis], 1
    )
    for each in recv:
        coeff = coeff - each.astype(F32)
    return (basis[:, None], coeff[:, None])


def solution(mesh):
    placed = (
        P("rows", "cols", None, None),
        P("rows", "cols", None, None),
        P("rows", "cols"),
        P(None, "cols", "rows", None),
        P(None, "cols", "rows", None),
        P(None, "cols"),
        P(None, "rows", None, None),
        P(None, "rows", None, None),
        P(),
    )
    return jax.shard_map(
        body,
        mesh=mesh,
        in_specs=placed,
        out_specs=(P(None, "rows", "cols", None), P(None, "rows", "cols", None)),
        check_vma=False,
    )
```

```python
import functools
import math

import jax
import jax.numpy as jnp
import numpy as np
from jax import lax
from jax.experimental import pallas as pl
from jax.experimental.pallas import tpu as pltpu
from jax.sharding import PartitionSpec as P

F32 = jnp.float32
BF16 = jnp.bfloat16
BLOCK = 32
SUB = 8
RING_MOST = 16
MIB = 1 << 20


def dot(a, b):
    return lax.dot_general(a, b, (((1,), (0,)), ((), ())), preferred_element_type=F32)


def dot00(a, b):
    return lax.dot_general(a, b, (((0,), (0,)), ((), ())), preferred_element_type=F32)


def dot11(a, b):
    return lax.dot_general(a, b, (((1,), (1,)), ((), ())), preferred_element_type=F32)


def split3(x):
    high = x.astype(BF16)
    rest = x - high.astype(F32)
    mid = rest.astype(BF16)
    low = (rest - mid.astype(F32)).astype(BF16)
    return high, mid, low


def eliminate(panel, first, store):
    rows, width = panel.shape
    lanes = 128
    tile = (SUB, lanes)
    lane = lax.broadcasted_iota(jnp.int32, tile, 1)
    sub = lax.broadcasted_iota(jnp.int32, tile, 0)
    high = rows // SUB
    halves = width // lanes
    part = [
        [panel[v * SUB : (v + 1) * SUB, h * lanes : (h + 1) * lanes] for h in range(halves)]
        for v in range(high)
    ]
    mine, start = first // lanes, first % lanes
    scales = []
    for top in range(high):
        at = start + top * SUB
        inside = (lane >= at) & (lane < at + SUB)
        column = [
            [jnp.broadcast_to(part[v][mine][:, at + m : at + m + 1], tile) for v in range(top, high)]
            for m in range(SUB)
        ]
        for n, value in enumerate([c[0] for c in column] + part[top]):
            store[top, n * SUB : (n + 1) * SUB, :] = value

        def spread(n, a):
            return jnp.broadcast_to(store[top, n * SUB + a : n * SUB + a + 1, :], tile)

        small = [[spread(b, a) for b in range(a + 1)] for a in range(SUB)]
        row = []
        for a in range(SUB):
            row.append([spread(SUB + h, a) for h in range(halves)])
            row[a][mine] = jnp.where(inside, jnp.where(lane == at + a, 1.0, 0.0), row[a][mine])
        pivots = small[0][0]
        factor = []
        for m in range(SUB):
            inverse = pl.reciprocal(small[m][m], approx=True)
            if m:
                pivots = jnp.where(sub == m, small[m][m], pivots)
            for a in range(m + 1, SUB):
                ratio = small[a][m] * inverse
                for b in range(m + 1, a + 1):
                    small[a][b] = small[a][b] - ratio * small[b][m]
                row[a] = [x - ratio * y for x, y in zip(row[a], row[m])]
            factor.append([c * inverse for c in column[m][1:]])
            for b in range(m + 1, SUB):
                column[b][1:] = [c - f * small[b][m] for c, f in zip(column[b][1:], factor[m])]
        for v in range(top + 1, high):
            for h in range(halves):
                value = jnp.where(inside, 0.0, part[v][h]) if h == mine else part[v][h]
                for m in range(SUB):
                    value = value - factor[m][v - top - 1] * row[m][h]
                part[v][h] = value
        for h in range(halves):
            value = row[0][h]
            for m in range(1, SUB):
                value = jnp.where(sub == m, row[m][h], value)
            part[top][h] = value
        scales.append(lax.rsqrt(pivots))
    done = []
    for v in range(high):
        cells = []
        for h in range(halves):
            value = part[v][h] * scales[v]
            if h == mine:
                value = jnp.where((lane > start + v * SUB + sub) & (lane < start + rows), 0.0, value)
            cells.append(value)
        done.append(jnp.concatenate(cells, 1))
    return jnp.concatenate(done, 0)


def invert_blocks(work, store, begin, end):
    width = work.shape[0]
    lane = lax.broadcasted_iota(jnp.int32, (1, width), 1)
    for first in range(begin, end, BLOCK):
        last = first + BLOCK
        panel = eliminate(work[first:last, :], first, store)
        work[first:last, :] = panel
        if last < width:
            base = last // 128 * 128
            high, mid, low = split3(panel)
            left = jnp.concatenate([high, high, mid, mid, high, low], 0)[:, base:]
            right = jnp.concatenate([high, mid, high, mid, low, high], 0)
            update = dot00(left, right)[last - base :, :]
            inside = (lane >= first) & (lane < last)
            work[last:, :] = jnp.where(inside, 0.0, work[last:, :]) - update


def orthonormal_kernel(info, start, *refs):
    parts, (qt, given, basis, yt, work, store, rows, sem) = refs[:-8], refs[-8:]
    width, order = yt.shape
    core = info[0]
    total = start[...]
    for part in parts:
        total = total - part[...].astype(F32)
    yt[...] = total
    high, mid, low = split3(yt[...])
    cross = dot11(high, mid) + dot11(high, low)
    work[...] = dot11(high, high) + (cross + cross.T + dot11(mid, mid))
    invert_blocks(work, store, 0, width)
    row = lax.broadcasted_iota(jnp.int32, (width, width), 0)
    col = lax.broadcasted_iota(jnp.int32, (width, width), 1)
    m_high, m_low, _ = split3(jnp.where(col <= row, work[...], 0.0))
    high, mid, _ = split3(yt[...])
    product = dot(m_high, high) + (dot(m_high, mid) + dot(m_low, high))
    yt[...] = product
    share = given.shape[0]

    def rows_at(index):
        return yt[:, pl.ds(pl.multiple_of(index * share, 128), share)].T * math.sqrt(order)

    rows[...] = rows_at(info[1])
    copy = pltpu.make_async_copy(rows, basis.at[core], sem.at[0])
    copy.start()
    given[...] = rows_at(info[1] + 1 - 2 * core)
    qt[...] = product.astype(BF16)
    copy.wait()


def place_kernel(info, given, basis, out, sem):
    copy = pltpu.make_async_copy(given, out.at[1 - info[0]], sem.at[0])
    copy.start()
    copy.wait()


def gather_kernel(places, blocks, info, panel_vt, sampler_t, *refs):
    new = len(places)
    u, v = refs[:new], refs[new : 2 * new]
    kept = refs[2 * new : -3]
    sampled, met, u_all = refs[-3:]
    pivots, priors, order, width = u_all.shape
    slab = order // blocks
    spans = [pl.ds(pl.multiple_of(info[2 + p] * slab, 128), slab) for p in places]
    drawn = jnp.concatenate([sampler_t[:, span] for span in spans], 1)
    for j in range(priors):
        left = jnp.concatenate([panel_vt[j, :, span] for span in spans], 1)
        for c in range(pivots):
            u_new = jnp.concatenate([block[c, j] for block in u], 0)
            v_new = jnp.concatenate([block[c, j] for block in v], 0)
            one, two = dot(drawn, u_new), dot(left, v_new)
            if kept:
                one, two = one + kept[0][c, j], two + kept[1][c, j]
            sampled[c, j] = one
            met[c, j] = two
            for n, p in enumerate(places):
                u_all[c, j, p * slab : (p + 1) * slab, :] = u_new[n * slab : (n + 1) * slab, :]


def sampled_kernel(places, blocks, info, sampled, sampler_t, *refs):
    late, (out, u_all) = refs[: len(refs) - 3], refs[-2:]
    slab = sampler_t.shape[1] // blocks
    for c in range(out.shape[0]):
        for j in range(out.shape[1]):
            total = sampled[c, j]
            for place in places:
                span = pl.ds(pl.multiple_of(info[2 + place] * slab, 128), slab)
                total += dot(sampler_t[:, span], late[c][j])
                u_all[c, j, place * slab : (place + 1) * slab, :] = late[c][j]
            out[c, j] = total.astype(BF16)


def update_kernel(own_column, places, blocks, info, panel_rank, pivot_rank, sampled, met, panel_u, panel_vt, *refs):
    late, (cross, out) = refs[:-2], refs[-2:]
    priors, width, _ = cross.shape
    slab = panel_vt.shape[2] // blocks
    column = info[0] if own_column else 1 - info[0]
    row = lax.broadcasted_iota(jnp.int32, (width, width), 0)
    col = lax.broadcasted_iota(jnp.int32, (width, width), 1)
    terms = []
    for j in range(priors):
        two = met[column, j]
        for place in places:
            span = pl.ds(pl.multiple_of(info[2 + place] * slab, 128), slab)
            two += dot(panel_vt[j, :, span], jnp.where(column == 0, late[0][j], late[1][j]))
        inside = (row < panel_rank[0, j]) & (col < pivot_rank[column, j])
        cross[j] = jnp.where(inside, two, 0.0).astype(BF16)
        terms.append(dot11(sampled[column, j], cross[j]).astype(BF16))
    half = out.shape[1] // 2
    for at in (0, half):
        total = jnp.zeros((width, half), F32)
        for j in range(priors):
            total += dot11(terms[j], panel_u[j, at : at + half, :])
        out[:, at : at + half] = total.astype(out.dtype)


def project_kernel(blocks, own_column, info, qt, panel_u, cross, u_all, give, keep, work):
    _, priors, order, width = u_all.shape
    slab = order // blocks
    pairs, share, _ = keep.shape
    core = info[0]
    column = core if own_column else 1 - core
    mids = []
    for j in range(priors):
        inner = dot(qt[...], panel_u[j]).astype(BF16)
        mids.append(dot(inner, cross[j]).astype(BF16))
    some = max(1, blocks // 2)
    for begin in range(0, blocks, some):
        total = jnp.zeros((some * slab, width), F32)
        for j in range(priors):
            total += dot11(u_all[column, j, begin * slab : (begin + some) * slab, :], mids[j])
        for n in range(some):
            place = pl.ds(pl.multiple_of(info[2 + begin + n] * slab, SUB), slab)
            work[place, :] = total[n * slab : (n + 1) * slab, :]
    for a in range(pairs):
        for out, which in ((give, 1 - core), (keep, core)):
            place = pl.ds(pl.multiple_of((2 * a + which) * share, SUB), share)
            out[a] = work[place, :].astype(out.dtype)


def halve_kernel(info, keep_b, keep_a, give_a, give_b, *sent):
    pairs = keep_a.shape[0]
    for shift in range(1, pairs):
        a = lax.rem(info[1] // 2 + shift, pairs)
        for column, keep, recv in ((1 - info[0], keep_b, give_a), (info[0], keep_a, give_b)):
            sent[shift - 1][column] = (keep[a] + recv[a].astype(F32)).astype(BF16)


def own_kernel(info, qt_b, qt_a, keep_b, keep_a, give_a, give_b, orig_u, orig_v, out, u_buf, v_buf, sems):
    share = out.shape[1]
    pair = info[1] // 2
    rows = pl.ds(pl.multiple_of(info[1] * share, 16), share)
    work = ((1 - info[0], qt_b, keep_b, give_a), (info[0], qt_a, keep_a, give_b))
    copies = []
    for n, (column, *_) in enumerate(work):
        copies.append(pltpu.make_async_copy(orig_u.at[column], u_buf.at[n], sems.at[2 * n]))
        copies.append(pltpu.make_async_copy(orig_v.at[column, rows], v_buf.at[n], sems.at[2 * n + 1]))
    for copy in copies:
        copy.start()
    for n, (column, qt, keep, recv) in enumerate(work):
        copies[2 * n].wait()
        copies[2 * n + 1].wait()
        left = dot(qt[...], u_buf[n]).astype(BF16)
        out[column] = dot11(v_buf[n], left) - (keep[pair] + recv[pair].astype(F32))


def turn_kernel(panel_v, sampler, panel_vt, sampler_t):
    sampler_t[...] = sampler[...].T
    for j in range(panel_v.shape[0]):
        panel_vt[j] = panel_v[j].T


def start_kernel(info, sampler_t, orig_u, orig_v, out):
    core = info[0]
    proj = dot(sampler_t[...], orig_v[core]).astype(BF16)
    out[...] = dot11(proj, orig_u[core])


def run(kernel, scalars, arrays, outs, scratch, limit, flops, name, aliases={}, apart=(), away=0):
    smem = pl.BlockSpec(memory_space=pltpu.SMEM)
    vmem = pl.BlockSpec(memory_space=pltpu.VMEM)
    shapes = [jax.ShapeDtypeStruct(*o) for o in outs]
    moved = sum(a.size * a.dtype.itemsize for a in list(arrays) + shapes)
    return pl.pallas_call(
        kernel,
        out_shape=shapes,
        in_specs=[smem] * len(scalars) + [vmem] * len(arrays) + [pl.BlockSpec(memory_space=pl.ANY)] * len(apart),
        out_specs=[vmem] * (len(shapes) - away) + [pl.BlockSpec(memory_space=pl.ANY)] * away,
        scratch_shapes=scratch,
        input_output_aliases=aliases,
        compiler_params=pltpu.CompilerParams(vmem_limit_bytes=limit * MIB),
        cost_estimate=pl.CostEstimate(flops=flops, bytes_accessed=moved, transcendentals=0),
        name=name,
    )(*scalars, *arrays, *apart)


def ring_order(count):
    if count % 2:
        return list(range(count))
    return list(range(0, count, 2)) + list(range(count - 1, 0, -2))


class Ring:
    def __init__(self, arrays, order, axis):
        count = len(order)
        self.count, self.axis, self.near = count, axis, (count - 1) // 2
        self.ahead = [(order[(p + 1) % count], order[p]) for p in range(count)]
        self.behind = [(order[p], order[(p + 1) % count]) for p in range(count)]
        self.found = [{0: a} for a in arrays]
        self.up, self.down = list(arrays), list(arrays)

    def step(self, number):
        for t in range(2):
            found = self.found[t]
            if number <= self.near:
                self.up[t] = found[number] = lax.ppermute(self.up[t], self.axis, self.ahead)
                self.down[t] = found[self.count - number] = lax.ppermute(self.down[t], self.axis, self.behind)
            else:
                found[number] = [
                    lax.ppermute(self.up[t][0], self.axis, self.ahead),
                    lax.ppermute(self.down[t][1], self.axis, self.behind),
                ]

    def tie(self, value, number, which=(0, 1)):
        lists = [(self.up, t, number) for t in which if number <= self.near or t == 0]
        lists += [(self.down, t, self.count - number) for t in which if number <= self.near or t == 1]
        value, *held = lax.optimization_barrier((value, *(way[t] for way, t, _ in lists)))
        for (way, t, place), block in zip(lists, held):
            way[t] = self.found[t][place] = block
        return value


def body(panel_u, panel_v, panel_rank, pivot_u, pivot_v, pivot_rank, orig_u, orig_v, sampler):
    order, width = panel_u.shape[2:]
    priors = panel_u.shape[1]
    pivots = pivot_u.shape[0]
    count = lax.axis_size("rows")
    cols = lax.axis_size("cols")
    pairs = cols // 2
    half, share = order // 2, order // cols
    me = lax.axis_index("cols")
    core, pair = me % 2, me // 2
    swap = [(i, i ^ 1) for i in range(cols)]

    ring = ring_order(count)
    place = np.argsort(np.array(ring))
    table = np.array([[ring[(place[r] + d) % count] for d in range(count)] for r in range(count)], np.int32)
    last = count // 2
    whole = count % 2 == 1 or last < 4 or count > RING_MOST
    if whole:
        table = np.zeros((count, 1), np.int32)
    sources = jnp.asarray(table)[lax.axis_index("rows")]
    info = jnp.concatenate([jnp.stack([core, me]).astype(jnp.int32), sources])

    panel_u, panel_v, orig_u, orig_v = panel_u[0], panel_v[0], orig_u[:, 0], orig_v[:, 0]
    square = 2 * width * width
    panel_vt, sampler_t = run(
        turn_kernel, [], [panel_v, sampler], [((priors, width, order), BF16), ((sampler.shape[1], order), BF16)], [], 12,
        10 * square * order, "turn"
    )
    (start,) = run(
        start_kernel, [info], [sampler_t, orig_u, orig_v], [((width, order), F32)], [], 12,
        2 * square * order, "start"
    )

    def shifted(x, shift):
        return lax.ppermute(x, "cols", [(i, (i + 2 * shift) % cols) for i in range(cols)])

    matrix = pltpu.VMEM((width, width), F32)
    tall = pltpu.VMEM((width, order), F32)

    def gathered(places, blocks, new_u, new_v, kept):
        new = len(places)
        shapes = [
            ((pivots, priors, width, width), F32), ((pivots, priors, width, width), F32),
            ((pivots, priors, order, width), BF16)
        ]
        first = 3 + 2 * new
        return run(
            functools.partial(gather_kernel, places, blocks), [info], [panel_vt, sampler_t, *new_u, *new_v, *kept],
            shapes, [], 28, 2 * pivots * priors * square * order * new // blocks, "gather",
            {first + n: n for n in range(len(kept))}
        )

    def updated(own_column, sampled, met):
        return run(
            functools.partial(update_kernel, own_column, places, blocks), [info, panel_rank, pivot_rank],
            [sampled, met, panel_u, panel_vt, *late_v],
            [((priors, width, width), BF16), ((width, order), F32 if own_column else BF16)], [], 20,
            2 * priors * square * (order + width), "update"
        )

    def projected(own_column, qt, cross):
        return run(
            functools.partial(project_kernel, blocks, own_column), [info], [qt, panel_u, cross, u_all],
            [((pairs, share, width), BF16), ((pairs, share, width), F32)], [pltpu.VMEM((order, width), F32)],
            20, 3 * priors * square * (2 * order + width), "project"
        )

    if whole:
        blocks, places = 1, []
        new_u, new_v = ([lax.all_gather(x, "rows", axis=2, tiled=True)] for x in (pivot_u, pivot_v))
        sampled, met, u_all = gathered([0], 1, new_u, new_v, [])
        late_u, late_v = [], []
    else:
        blocks = count
        now, kept = Ring([pivot_u, pivot_v], ring, "rows"), []
        for number in range(1, last + 1):
            now.step(number)
            if 1 < number < last:
                kept[0] = now.tie(kept[0], number, (0,))
                if number == 2:
                    start = now.tie(start, number, (1,))
            if number == last:
                places = [last]
                late_u, late_v = now.found[0][last], now.found[1][last]
            else:
                places = sorted({number, count - number} | ({0} if number == 1 else set()))
                new_u, new_v = ([now.found[t][p] for p in places] for t in range(2))
                kept = list(gathered(places, count, new_u, new_v, kept))
        sampled, met, u_all = kept
    sampled, u_all = run(
        functools.partial(sampled_kernel, places, blocks), [info], [sampled, sampler_t, *late_u, u_all],
        [((pivots, priors, width, width), BF16), ((pivots, priors, order, width), BF16)], [], 16, square * order,
        "sampled", {3 + len(late_u): 1}
    )
    cross_other, give = updated(False, sampled, met)
    recv = lax.ppermute(give, "cols", swap)
    cross_own, keep = updated(True, sampled, met)
    sent = (keep + recv.astype(F32)).astype(BF16)
    parts = [shifted(sent, shift) for shift in range(1, pairs)]
    begun = start - keep - recv.astype(F32)
    qt, given, basis = run(
        orthonormal_kernel, [info], [begun, *parts],
        [((width, order), BF16), ((share, width), F32), ((pivots, share, width), F32)],
        [
            tall, matrix, pltpu.VMEM((BLOCK // SUB, (SUB + width // 128) * SUB, 128), F32), pltpu.VMEM((share, width), F32),
            pltpu.SemaphoreType.DMA((1,))
        ],
        16,
        128 * square * order, "orthonormal", away=1
    )
    qt_other = lax.ppermute(qt, "cols", swap)
    give_a, keep_a = projected(True, qt, cross_own)
    qt_other, give_a, keep_a = lax.optimization_barrier((qt_other, give_a, keep_a))
    give_b, keep_b = projected(False, qt_other, cross_other)
    give_a, give_b = lax.ppermute(give_a, "cols", swap), lax.ppermute(give_b, "cols", swap)
    sent = run(
        halve_kernel, [info], [keep_b, keep_a, give_a, give_b], [((pivots, share, width), BF16)] * (pairs - 1), [], 8,
        square, "halve"
    )
    qt, *sent = lax.optimization_barrier((qt, *sent))
    recv = [shifted(each, shift) for shift, each in enumerate(sent, 1)]
    (coeff,) = run(
        own_kernel, [info], [qt_other, qt, keep_b, keep_a, give_a, give_b], [((pivots, share, width), F32)],
        [pltpu.VMEM((pivots, order, width), BF16), pltpu.VMEM((pivots, share, width), BF16), pltpu.SemaphoreType.DMA((4,))],
        12, square * width, "own", apart=[orig_u, orig_v]
    )
    (basis,) = run(
        place_kernel, [info], [lax.ppermute(given, "cols", swap)], [((pivots, share, width), F32)],
        [pltpu.SemaphoreType.DMA((1,))], 4, 1, "place", {2: 0}, [basis], 1
    )
    for each in recv:
        coeff = coeff - each.astype(F32)
    return (basis[:, None], coeff[:, None])


def solution(mesh):
    placed = (
        P("rows", "cols", None, None),
        P("rows", "cols", None, None),
        P("rows", "cols"),
        P(None, "cols", "rows", None),
        P(None, "cols", "rows", None),
        P(None, "cols"),
        P(None, "rows", None, None),
        P(None, "rows", None, None),
        P(),
    )
    return jax.shard_map(
        body,
        mesh=mesh,
        in_specs=placed,
        out_specs=(P(None, "rows", "cols", None), P(None, "rows", "cols", None)),
        check_vma=False,
    )
```
